32 devices in a mesh: blk: 16 (over z, x, core), spec: 2 (over y).
Axes of the slice: x: 2, y: 2, z: 4, core: 2. Of those that a mesh axis runs over, the one named last changes fastest.
Arguments:
- spectrum: float32 [32, 24, 16384], P('spec', None, 'blk'), may hold values from 0.05 to 2
- depths: float32 [16384], P('blk'), may hold values from 5 to 4000
- currents: float32 [2, 16384], P(None, 'blk'), may hold values from -4 to 4
- slopes: float32 [2, 16384], P(None, 'blk'), may hold values from -0.12 to 0.12
- wind_speed: float32 [2, 16384], P(None, 'blk'), may hold values from -40 to 40
- wet_mask: int32 [16384], P('blk'), may hold values 0 or 1
- face_owner: int32 [1024, 1], P('blk'), may hold values from 0 to 15, as said below
- face_block: int32 [1024], P('blk'), may hold values from 0 to 15
- freq_weights: bfloat16 [2, 32, 32], replicated, may hold values from 0.0049743652 to 0.079589844
- angle_weights: bfloat16 [2, 2, 24, 24], replicated, may hold values from 0.0049743652 to 0.099609375
- transfer_rate: float32 [32], replicated, may hold values from 0.05 to 0.3
Outputs:
- next_spectrum: float32 [32, 24, 16384], P('spec', None, 'blk')
The draws below stay inside these ranges and needn't reach their ends.
Inputs may be any that keep to these rules, and one draw needn't show every extreme that they name: `face_owner`: face i of one device is side i % 4 (west, east, south, north) of its block i // 4. Of the 64 rows of one device, 32 name another index and the rest name the device itself; no other index is named more than 3 times in those rows, and one is named exactly 3 times.
All inputs are finite; a program needn't handle non-finite values. No bound on the sum of `wet_mask` on one device may be relied on, other than what follows from the above.
Results may differ from the reference program's by a relative error of at most 0.0011.
The reference program's roundings to bfloat16 on the way count: a program that leaves them out, or rounds other values in their place, can miss the bound.
Values may be sent and summed in bfloat16 or wider, within the bound.
No kernel may reach another device: no remote copies, remote signals or barrier semaphores. Data moves between devices by JAX's collectives and lax.ppermute only.
A program may use at most 192 MiB of HBM per device.

```python
import math
import jax
import jax.numpy as jnp
from jax import lax

FREQ = 32
DIRS = 24
TILE = 8
BLK_DEV = 16
FACES_DEV = 64
PTS_DEV = 1024
FACES = 1024
POINTS = 16384
CAP = 3
N_BLK = 16


def draw_face_owner(key, part):
    remote_count = 2 * BLK_DEV

    def one_device(device):
        device_key = jax.random.fold_in(key, device)
        start = jax.random.randint(jax.random.fold_in(device_key, 11), (), 0, N_BLK - 1, dtype=jnp.int32)
        slot = jnp.arange(remote_count, dtype=jnp.int32)
        group = slot // CAP
        offset = 1 + (group + start) % (N_BLK - 1)
        remote = (device + offset) % N_BLK
        own_part = jnp.zeros((FACES_DEV - remote_count,), jnp.int32) + device
        owners = jnp.concatenate([remote, own_part])
        placing = jax.random.permutation(jax.random.fold_in(device_key, 23), FACES_DEV)
        return owners[placing]
    every = jax.vmap(one_device)(jnp.arange(N_BLK, dtype=jnp.int32))
    return every.reshape(FACES, 1).astype(jnp.int32)


def with_ends(values, rng, least, high):
    longest = values.shape.index(max(values.shape))
    spots = []
    for shift in (0, 1):
        where = [jax.random.randint(jax.random.fold_in(rng, axis), (), 0, length) for axis, length in enumerate(values.shape)]
        where[longest] = (where[longest] + shift) % values.shape[longest]
        spots.append(tuple(where))
    return values.at[spots[0]].set(least).at[spots[1]].set(high)


def level_of(key, dims, cuts, smallest, largest):
    loudness = 1.0
    for position, shards_of in cuts:
        heights = jax.random.uniform(jax.random.fold_in(jax.random.fold_in(key, 6), position), (shards_of,), jnp.float32, smallest / len(cuts), largest / len(cuts))
        loudness = loudness * jnp.repeat(jnp.exp(heights), dims[position] // shards_of).reshape((-1,) + (1,) * (len(dims) - 1 - position))
    return loudness


def normal_values(stream_key, extent, scale, bound, shards=(), held_as=jnp.bfloat16):
    level = level_of(stream_key, extent, shards, -0.22, 0.18) if shards else 1.0
    drawn = jax.random.normal(stream_key, extent, jnp.float32) * scale * level
    return jnp.minimum(jnp.maximum(drawn, -bound), bound).astype(held_as)


def setup_inputs(seed: int = 0) -> dict:
    streams_of = jax.random.split(jax.random.key(seed), 12)
    return {
        "spectrum": jnp.clip(jnp.exp(math.log(2.0) - 3.6888794 * jax.random.uniform(streams_of[0], (FREQ, DIRS, POINTS), jnp.float32) ** level_of(streams_of[0], (FREQ, DIRS, POINTS), ((0, 2), (2, 16)), -0.2, 0.2)), 0.05, 2.0),
        "depths": jnp.clip(jnp.exp(math.log(4000.0) - 6.684612 * jax.random.uniform(streams_of[1], (POINTS,), jnp.float32) ** level_of(streams_of[1], (POINTS,), ((0, 16),), -0.2, 0.2)), 5.0, 4000.0),
        "currents": normal_values(streams_of[2], (2, POINTS), 1.0, 4.0, ((1, 16),), jnp.float32),
        "slopes": normal_values(streams_of[3], (2, POINTS), 0.02, 0.12, ((1, 16),), jnp.float32),
        "wind_speed": normal_values(streams_of[4], (2, POINTS), 8.0, 40.0, ((1, 16),), jnp.float32),
        "wet_mask": with_ends((jax.random.randint(streams_of[5], (POINTS,), 0, 8) < 7).astype(jnp.int32), jax.random.fold_in(streams_of[5], 1), 0, 1),
        "face_owner": draw_face_owner(jax.random.fold_in(streams_of[11], 71), 0),
        "face_block": with_ends(jax.random.randint(streams_of[7], (FACES,), 0, BLK_DEV), jax.random.fold_in(streams_of[7], 1), 0, BLK_DEV - 1).astype(jnp.int32),
        "freq_weights": jnp.clip(jnp.exp(jax.random.uniform(streams_of[8], (2, FREQ, FREQ), jnp.float32, math.log(0.0049743652), math.log(0.079589844))), 0.0049743652, 0.079589844).astype(jnp.bfloat16),
        "angle_weights": jnp.clip(jnp.exp(jax.random.uniform(streams_of[9], (2, 2, DIRS, DIRS), jnp.float32, math.log(0.0049743652), math.log(0.099609375))), 0.0049743652, 0.099609375).astype(jnp.bfloat16),
        "transfer_rate": jnp.clip(jnp.exp(jax.random.uniform(streams_of[10], (FREQ,), jnp.float32, math.log(0.05), math.log(0.3))), 0.05, 0.3),
    }


GRAVITY = 9.81
TIME_STEP = 200.0
CELL_SIZE = 5500.0
LOWEST_FREQ = 0.0418
FREQ_GROWTH = 1.1
WIND_GROWTH = 0.0003
TURN_LIMIT = 0.9

def dispersion(radian_freq, water_depth):
    deep_kh = radian_freq * radian_freq / GRAVITY * water_depth
    wave_kh = deep_kh / jnp.sqrt(jnp.tanh(deep_kh))
    decay_two = jnp.exp(-2.0 * wave_kh)
    denom_term = 1.0 - decay_two * decay_two
    shoal_ratio = 4.0 * wave_kh * decay_two / denom_term
    phase_speed = radian_freq * water_depth / wave_kh
    group_speed = 0.5 * (1.0 + shoal_ratio) * phase_speed
    turn_factor = 2.0 * radian_freq * decay_two / denom_term
    return (phase_speed, group_speed, turn_factor)

def courants(radian_freq, angle_values, water_depth, current_xy, slope_xy, wet_float):
    freq_column = radian_freq[:, None, None, None, None]
    phase_speed, group_speed, turn_factor = dispersion(freq_column, water_depth[None, None])
    cosine = jnp.cos(angle_values)[None, :, None, None, None]
    sine = jnp.sin(angle_values)[None, :, None, None, None]
    grid_ratio = TIME_STEP / CELL_SIZE
    cour_x = (group_speed * cosine + current_xy[0][None, None]) * grid_ratio * wet_float[None, None]
    cour_y = (group_speed * sine + current_xy[1][None, None]) * grid_ratio * wet_float[None, None]
    angle_step = 2.0 * math.pi / angle_values.shape[0]
    turning = turn_factor * (sine * slope_xy[0][None, None] - cosine * slope_xy[1][None, None]) * (TIME_STEP / angle_step)
    cour_turn = jnp.clip(turning, -TURN_LIMIT, TURN_LIMIT)
    return (phase_speed, cour_x, cour_y, cour_turn)

def edge_fluxes(wave_field, cour_x, cour_y):
    west_side = jnp.maximum(-cour_x[..., :, 0], 0.0) * wave_field[..., :, 0]
    east_side = jnp.maximum(cour_x[..., :, -1], 0.0) * wave_field[..., :, -1]
    south_side = jnp.maximum(-cour_y[..., 0, :], 0.0) * wave_field[..., 0, :]
    north_side = jnp.maximum(cour_y[..., -1, :], 0.0) * wave_field[..., -1, :]
    return jnp.stack([west_side, east_side, south_side, north_side], axis=3)

def transported(wave_field, cour_x, cour_y, cour_turn, inflow):
    tile_side = wave_field.shape[-1]
    rightward = jnp.maximum(cour_x, 0.0) * wave_field
    leftward = jnp.maximum(-cour_x, 0.0) * wave_field
    upward = jnp.maximum(cour_y, 0.0) * wave_field
    downward = jnp.maximum(-cour_y, 0.0) * wave_field
    lead_pads = [(0, 0)] * 3
    from_x = jnp.pad(rightward[..., :, :-1], lead_pads + [(0, 0), (1, 0)]) + jnp.pad(leftward[..., :, 1:], lead_pads + [(0, 0), (0, 1)])
    from_y = jnp.pad(upward[..., :-1, :], lead_pads + [(1, 0), (0, 0)]) + jnp.pad(downward[..., 1:, :], lead_pads + [(0, 1), (0, 0)])
    from_turn = jnp.roll(jnp.maximum(cour_turn, 0.0) * wave_field, 1, axis=1) + jnp.roll(jnp.maximum(-cour_turn, 0.0) * wave_field, -1, axis=1)
    ghost_x = jnp.pad(inflow[:, :, :, 0, :, None], lead_pads + [(0, 0), (0, tile_side - 1)])
    ghost_x = ghost_x + jnp.pad(inflow[:, :, :, 1, :, None], lead_pads + [(0, 0), (tile_side - 1, 0)])
    ghost_y = jnp.pad(inflow[:, :, :, 2, None, :], lead_pads + [(0, tile_side - 1), (0, 0)])
    ghost_y = ghost_y + jnp.pad(inflow[:, :, :, 3, None, :], lead_pads + [(tile_side - 1, 0), (0, 0)])
    outflow = (jnp.abs(cour_x) + jnp.abs(cour_y) + jnp.abs(cour_turn)) * wave_field
    return wave_field - outflow + from_x + from_y + from_turn + ghost_x + ghost_y

def rounded(values):
    return lax.optimization_barrier(values.astype(jnp.bfloat16)).astype(jnp.float32)

def nonlinear(levels, freq_weights, angle_weights, transfer_rate):
    levels_wide = levels.astype(jnp.float32)
    freq_wide = freq_weights.astype(jnp.float32)
    angle_wide = angle_weights.astype(jnp.float32)
    shifted_plus = rounded(jnp.einsum('gf,fdq->gdq', freq_wide[0], levels_wide))
    shifted_minus = rounded(jnp.einsum('gf,fdq->gdq', freq_wide[1], levels_wide))
    rate_column = transfer_rate[:, None, None]
    delta_list = []
    for mirror in range(2):
        image_plus = jnp.einsum('ed,gdq->geq', angle_wide[mirror, 0], shifted_plus)
        image_minus = jnp.einsum('ed,gdq->geq', angle_wide[mirror, 1], shifted_minus)
        delta_list.append(rate_column * (levels_wide * levels_wide * (image_plus + image_minus) - 2.0 * levels_wide * image_plus * image_minus))
    low_first = rounded(delta_list[0])
    low_second = rounded(delta_list[1])
    back_plus = rounded(jnp.einsum('ed,geq->gdq', angle_wide[0, 0], low_first) + jnp.einsum('ed,geq->gdq', angle_wide[1, 0], low_second))
    back_minus = rounded(jnp.einsum('ed,geq->gdq', angle_wide[0, 1], low_first) + jnp.einsum('ed,geq->gdq', angle_wide[1, 1], low_second))
    return -2.0 * (delta_list[0] + delta_list[1]) + jnp.einsum('gf,gdq->fdq', freq_wide[0], back_plus) + jnp.einsum('gf,gdq->fdq', freq_wide[1], back_minus)

def reference(spectrum, depths, currents, slopes, wind_speed, wet_mask, face_owner, face_block, freq_weights, angle_weights, transfer_rate):
    block_total = POINTS // (TILE * TILE)
    shape_five = (FREQ, DIRS, block_total, TILE, TILE)
    wave_field = spectrum.reshape(shape_five)
    freq_index = jnp.arange(FREQ, dtype=jnp.int32).astype(jnp.float32)
    radian_freq = 2.0 * math.pi * LOWEST_FREQ * jnp.power(jnp.float32(FREQ_GROWTH), freq_index)
    angle_values = jnp.arange(DIRS, dtype=jnp.int32).astype(jnp.float32) * (2.0 * math.pi / DIRS)
    wet_float = wet_mask.astype(jnp.float32)
    phase_speed, cour_x, cour_y, cour_turn = courants(radian_freq, angle_values, depths.reshape(block_total, TILE, TILE), currents.reshape(2, block_total, TILE, TILE), slopes.reshape(2, block_total, TILE, TILE), wet_float.reshape(block_total, TILE, TILE))
    edges = edge_fluxes(wave_field, cour_x, cour_y).reshape(FREQ, DIRS, block_total * 4, TILE)
    face_sides = jnp.arange(FACES, dtype=jnp.int32) % 4
    neighbour = (face_owner[:, 0] * BLK_DEV + face_block) * 4 + jnp.bitwise_xor(face_sides, 1)
    inflow = jnp.take(edges, neighbour, axis=2).reshape(FREQ, DIRS, block_total, 4, TILE)
    moved = transported(wave_field, cour_x, cour_y, cour_turn, inflow).reshape(FREQ, DIRS, POINTS)
    levels = moved.astype(jnp.bfloat16)
    pieces = levels.reshape(FREQ, DIRS, N_BLK, PTS_DEV).transpose(2, 0, 1, 3)
    transfer = lax.map(lambda block_piece: nonlinear(block_piece, freq_weights, angle_weights, transfer_rate), pieces)
    transfer = transfer.transpose(1, 2, 0, 3).reshape(FREQ, DIRS, POINTS)
    along_wind = wind_speed[0][None, None, :] * jnp.cos(angle_values)[None, :, None] + wind_speed[1][None, None, :] * jnp.sin(angle_values)[None, :, None]
    phase_flat = phase_speed.reshape(FREQ, 1, POINTS)
    growth = TIME_STEP * WIND_GROWTH * radian_freq[:, None, None] * jnp.maximum(along_wind / phase_flat - 1.0, 0.0)
    return wet_float[None, None, :] * (moved + transfer + growth * moved)
```

```python
import functools
import math

import jax
import jax.numpy as jnp
from jax import lax
from jax.experimental import pallas as pl
from jax.experimental.pallas import tpu as pltpu
from jax.sharding import PartitionSpec as P

GRAVITY = 9.81
TIME_STEP = 200.0
CELL_SIZE = 5500.0
LOWEST_FREQ = 0.0418
FREQ_GROWTH = 1.1
WIND_GROWTH = 0.0003
TURN_LIMIT = 0.9

TILE = 8
CELLS = TILE * TILE
GROUP = 256
HALF = 128
EDGE = 128
LANES = 128
VMEM_BYTES = 48 * 1024 * 1024

F32 = jnp.float32
BF16 = jnp.bfloat16
I32 = jnp.int32


def iota(shape, dim):
    return lax.broadcasted_iota(I32, shape, dim)


def onehot(mask):
    return jnp.where(mask, 1.0, 0.0).astype(BF16)


def dot(a, b):
    return jnp.dot(a, b, preferred_element_type=F32)


def dot_nt(a, b):
    return lax.dot_general(a, b, (((1,), (1,)), ((), ())), preferred_element_type=F32)


def dispersion(radian_freq, water_depth):
    deep_kh = radian_freq * radian_freq / GRAVITY * water_depth
    wave_kh = deep_kh / jnp.sqrt(jnp.tanh(deep_kh))
    return wave_kh


def radian_rows(freq_local, width):
    index = iota((freq_local, width), 0) + lax.axis_index("spec") * freq_local
    return (2.0 * math.pi * LOWEST_FREQ) * jnp.exp(index.astype(F32) * math.log(FREQ_GROWTH))


def angle_table(angles, width):
    values = iota((angles, width), 0).astype(F32) * (2.0 * math.pi / angles)
    return jnp.cos(values), jnp.sin(values)


def place_of(point):
    block = point // CELLS
    row = (point // TILE) % TILE
    col = point % TILE
    inner = (row >= 1) & (row <= 6) & (col >= 1) & (col <= 6)
    rank = (row - 1) * 6 + jnp.clip(col - 1, 0, 6)
    early = inner & (rank < 32)
    before = jnp.clip(rank, 0, 32)
    return jnp.where(early, block * 32 + rank, HALF + block * 32 + point % CELLS - before)


def transport_kernel(
    spec_ref, depth_ref, current_ref, slope_ref, wet_ref,
    moved_ref, high_ref, low_ref, early_ref,
    flux_ref, group_ref, turn_x_ref, turn_y_ref,
):
    freq_local, angles, width = spec_ref.shape
    radian_freq = radian_rows(freq_local, width)
    depth = depth_ref[...]
    wave_kh = dispersion(radian_freq, depth)
    decay_two = jnp.exp(-2.0 * wave_kh)
    denom = 1.0 - decay_two * decay_two
    ratio = 4.0 * wave_kh * decay_two / denom
    phase = radian_freq * depth / wave_kh
    wet = wet_ref[...].astype(F32) * (TIME_STEP / CELL_SIZE)
    group_ref[...] = 0.5 * (1.0 + ratio) * phase * wet
    turn = 2.0 * radian_freq * decay_two / denom * (TIME_STEP / (2.0 * math.pi / angles))
    turn_x_ref[...] = turn * slope_ref[0:1, :]
    turn_y_ref[...] = turn * slope_ref[1:2, :]
    drift_x = current_ref[0:1, :] * wet
    drift_y = current_ref[1:2, :] * wet
    cosine, sine = angle_table(angles, LANES)
    lane = iota((angles, LANES), 1)
    col = lane % TILE
    row = (lane // TILE) % TILE
    west, east = col == 0, col == TILE - 1
    south, north = row == 0, row == TILE - 1
    for half in range(width // LANES):
        part = slice(half * LANES, (half + 1) * LANES)
        drift_xp = jnp.broadcast_to(drift_x[:, part], (angles, LANES))
        drift_yp = jnp.broadcast_to(drift_y[:, part], (angles, LANES))
        for f in range(freq_local):
            energy = spec_ref[f, :, part]
            speed = jnp.broadcast_to(group_ref[f : f + 1, part], (angles, LANES))
            turn_x = jnp.broadcast_to(turn_x_ref[f : f + 1, part], (angles, LANES))
            turn_y = jnp.broadcast_to(turn_y_ref[f : f + 1, part], (angles, LANES))
            flow_x = (speed * cosine + drift_xp) * energy
            flow_y = (speed * sine + drift_yp) * energy
            turning = jnp.clip(sine * turn_x - cosine * turn_y, -TURN_LIMIT, TURN_LIMIT)
            flow_t = turning * energy
            right = jnp.maximum(flow_x, 0.0)
            left = right - flow_x
            up = jnp.maximum(flow_y, 0.0)
            down = up - flow_y
            ahead = jnp.maximum(flow_t, 0.0)
            back = ahead - flow_t
            total = energy - (right + left) - (up + down) - (ahead + back)
            total = total + pltpu.roll(jnp.where(east, 0.0, right), 1, 1)
            total = total + pltpu.roll(jnp.where(west, 0.0, left), LANES - 1, 1)
            total = total + pltpu.roll(jnp.where(north, 0.0, up), TILE, 1)
            total = total + pltpu.roll(jnp.where(south, 0.0, down), LANES - TILE, 1)
            total = total + pltpu.roll(ahead, 1, 0) + pltpu.roll(back, angles - 1, 0)
            moved_ref[f, :, part] = total
            flux_ref[f, :, half * LANES : (half + 1) * LANES] = jnp.where(
                east, right, jnp.where(west, left, 0.0)
            )
            flux_ref[f, :, width + half * LANES : width + (half + 1) * LANES] = jnp.where(
                north, up, jnp.where(south, down, 0.0)
            )
    source = iota((2 * width, EDGE), 0)
    upright = source // width
    point = source % width
    block = point // CELLS
    prow = (point // TILE) % TILE
    pcol = point % TILE
    across = jnp.where(upright == 0, pcol, prow)
    along = jnp.where(upright == 0, prow, pcol)
    edge = upright * 64 + jnp.where(across == 0, 0, 32) + block * TILE + along
    on_edge = (across == 0) | (across == TILE - 1)
    pick = onehot(on_edge & (edge == iota((2 * width, EDGE), 1)))
    flux = flux_ref[...].reshape(freq_local * angles, 2 * width)
    high = flux.astype(BF16)
    low = (flux - high.astype(F32)).astype(BF16)
    high_ref[...] = dot(high, pick).astype(BF16)
    low_ref[...] = dot(low, pick).astype(BF16)
    inner = onehot(place_of(iota((width, HALF), 0)) == iota((width, HALF), 1))
    for j in range(angles // 8):
        levels = moved_ref[:, 8 * j : 8 * j + 8, :].reshape(freq_local * 8, width).astype(BF16)
        early_ref[j] = dot(levels, inner).astype(BF16)


def select_kernel(capacity, table_ref, high_ref, reply_ref):
    peers, faces = table_ref.shape
    rows = peers * capacity * TILE
    edges = high_ref.shape[1]
    mine = lax.axis_index("blk").astype(F32)
    table = table_ref[...]
    owner = (table // 256).astype(F32).astype(BF16)
    block = (table % 256).astype(F32).astype(BF16)
    spread = onehot(iota((rows, peers), 0) // (capacity * TILE) == iota((rows, peers), 1))
    owner_rows = dot(spread, owner)
    block_rows = dot(spread, block).astype(I32)
    row = iota((rows, faces), 0)
    face = iota((rows, faces), 1)
    asked = (owner_rows == mine) & ((row // (capacity * TILE)).astype(F32) != mine)
    earlier = onehot(iota((faces, faces), 0) < iota((faces, faces), 1))
    rank = dot(onehot(asked), earlier).astype(I32)
    chosen = asked & (rank == (row // TILE) % capacity)
    side = face % 4
    base = (
        (block_rows // 4) * EDGE + (side // 2) * 64 + (1 - side % 2) * 32 + (block_rows % 4) * TILE
    )
    target = jnp.sum(jnp.where(chosen, (base + row % TILE + 1).astype(F32), 0.0), axis=1, keepdims=True)
    pick = onehot(iota((rows, edges), 1).astype(F32) + 1.0 == target)
    reply = dot_nt(pick, high_ref[...]).astype(BF16)
    for p in range(peers):
        reply_ref[p] = reply[p * capacity * TILE : (p + 1) * capacity * TILE]


def weights_kernel(freq_ref, angle_ref, shift_ref, spread_ref, image_ref, back_ref):
    freqs = freq_ref.shape[1]
    angles = angle_ref.shape[2]
    wide = freqs * 8
    own = spread_ref.shape[0]
    start = lax.axis_index("spec") * (own // 8)
    rows = onehot((iota((wide, freqs), 0) // 8 + start) % freqs == iota((wide, freqs), 1))
    same = iota((wide, wide), 0) % 8 == iota((wide, wide), 1) % 8
    for s in range(2):
        weights = freq_ref[s]
        left = dot(rows, weights).astype(BF16)
        shift_ref[s * wide : (s + 1) * wide, :] = jnp.where(same, dot_nt(left, rows), 0.0).astype(BF16)
        turned = dot_nt(rows[:own], weights).astype(BF16)
        spread_ref[:, s * wide : (s + 1) * wide] = jnp.where(
            same[:own], dot_nt(turned, rows), 0.0
        ).astype(BF16)
    stacked = jnp.concatenate(
        [angle_ref[m, s].astype(F32) for m in range(2) for s in range(2)], axis=0
    ).astype(BF16)
    lines = angles * 4
    r = iota((4 * lines, 4 * angles), 0)
    c = iota((4 * lines, 4 * angles), 1)
    direction = (r // 32) % (angles // 8) * 8 + r % 8
    chosen = onehot((r // lines) * angles + direction == c)
    lines_rows = dot(chosen, stacked).astype(BF16)
    r = iota((2 * lines, angles), 0)
    column = onehot((r // 32) % (angles // 8) * 8 + r % 8 == iota((2 * lines, angles), 1))
    r = iota((4 * lines, 2 * lines), 0)
    c = iota((4 * lines, 2 * lines), 1)
    keep = ((r // lines) % 2 == c // lines) & ((r // 8) % 4 == (c // 8) % 4)
    image_ref[...] = jnp.where(keep, dot_nt(lines_rows, column), 0.0).astype(BF16)
    for s in range(2):
        r = iota((2 * lines, 4 * angles), 0)
        c = iota((2 * lines, 4 * angles), 1)
        direction = (r // 32) % (angles // 8) * 8 + r % 8
        chosen = onehot(((r // lines) * 2 + s) * angles + direction == c)
        lines_rows = dot(chosen, stacked).astype(BF16)
        r = iota((lines, 2 * lines), 0)
        c = iota((lines, 2 * lines), 1)
        keep = (r // 8) % 4 == (c // 8) % 4
        back_ref[s * lines : (s + 1) * lines, :] = jnp.where(
            keep, dot_nt(column[:lines], lines_rows), 0.0
        ).astype(BF16)


def local_kernel(capacity, owner_ref, block_ref, high_ref, low_ref, moved_in_ref, moved_ref, map_ref):
    freq_local, angles, width = moved_ref.shape
    faces = owner_ref.shape[1]
    edges = high_ref.shape[1]
    rows = map_ref.shape[0]
    mine = lax.axis_index("blk")
    owner = owner_ref[...]
    by_column = jnp.broadcast_to(owner, (faces, faces))
    below = iota((faces, faces), 0)
    right = iota((faces, faces), 1)
    by_row = jnp.sum(jnp.where(below == right, by_column, 0).astype(F32), axis=1, keepdims=True)
    equal = (by_row == by_column.astype(F32)) & (below < right)
    rank = jnp.sum(jnp.where(equal, 1.0, 0.0), axis=0, keepdims=True)
    table = jnp.concatenate(
        [
            block_ref[...].astype(F32),
            owner.astype(F32),
            rank,
            jnp.zeros((5, faces), F32),
        ],
        axis=0,
    ).astype(BF16)
    point = iota((faces, width), 1)
    block = point // CELLS + pl.program_id(0) * (width // CELLS)
    col = point % TILE
    row = (point // TILE) % TILE
    face = iota((faces, width), 0)
    at_x = dot(table, onehot((face == block * 4 + jnp.where(col == 0, 0, 1)))).astype(I32)
    at_y = dot(table, onehot((face == block * 4 + jnp.where(row == 0, 2, 3)))).astype(I32)
    point = iota((1, width), 1)
    col = point % TILE
    row = (point // TILE) % TILE

    def ids(found, across, along, upright):
        edge = (across == 0) | (across == TILE - 1)
        from_block, from_owner, slot = found[0:1], found[1:2], found[2:3]
        local = edge & (from_owner == mine)
        remote = edge & (from_owner != mine)
        base = upright * 64 + jnp.where(across == 0, 32, 0)
        source = (from_block // 4) * EDGE + base + (from_block % 4) * TILE + along
        reply = (from_owner * capacity + slot) * TILE + along
        return jnp.where(local, source, -1), jnp.where(remote, reply, -1)

    source_x, reply_x = ids(at_x, col, row, 0)
    source_y, reply_y = ids(at_y, row, col, 1)
    line = iota((edges, width), 0)
    pick = onehot((line == source_x) | (line == source_y))
    inflow = dot(high_ref[...], pick) + dot(low_ref[...], pick)
    moved_ref[...] = moved_in_ref[...] + inflow.reshape(freq_local, angles, width)
    line = iota((rows, width), 0)
    map_ref[...] = onehot((line == reply_x) | (line == reply_y))


def late_kernel(reply_ref, map_ref, moved_in_ref, moved_ref, late_ref, turned_ref):
    freq_local, angles, width = moved_ref.shape
    rows = map_ref.shape[0]

    @pl.when(pl.program_id(0) == 0)
    def _():
        reply = reply_ref[...].astype(F32).reshape(rows, freq_local * angles)
        turned_ref[...] = reply.T.astype(BF16)

    inflow = dot(turned_ref[...], map_ref[...])
    moved_ref[...] = moved_in_ref[...] + inflow.reshape(freq_local, angles, width)
    outer = onehot(place_of(iota((width, HALF), 0)) == iota((width, HALF), 1) + HALF)
    for j in range(angles // 8):
        levels = moved_ref[:, 8 * j : 8 * j + 8, :].reshape(freq_local * 8, width).astype(BF16)
        late_ref[j] = dot(levels, outer).astype(BF16)


def nonlinear_tile(level_refs, shift_ref, spread_ref, image_ref, back_ref, rate_ref, shifted_ref, gained_ref):
    parts, own, width = level_refs[0].shape
    wide = shift_ref.shape[1]
    freqs = wide // 8
    lines = parts * 32
    start = lax.axis_index("spec") * (own // 8)
    for j in range(parts):
        levels = jnp.concatenate([ref[j] for ref in level_refs], axis=0)
        shifted_ref[j] = dot(shift_ref[...], levels).astype(BF16)
    doubled = []
    for q in range(freqs // 4):
        source, place = divmod(q * 32, own)
        shifted = jnp.concatenate(
            [
                shifted_ref[j, s * wide + 32 * q : s * wide + 32 * q + 32, :]
                for s in range(2)
                for j in range(parts)
            ],
            axis=0,
        )
        images = dot(image_ref[...], shifted)
        level = jnp.concatenate(
            [level_refs[source][j, place : place + 32, :].astype(F32) for j in range(parts)], axis=0
        )
        rates = [rate_ref[(start + 4 * q + k) % freqs] for k in range(4)]
        scaled = jnp.concatenate(
            [
                level[32 * j + 8 * k : 32 * j + 8 * k + 8] * rates[k]
                for j in range(parts)
                for k in range(4)
            ],
            axis=0,
        )
        deltas = []
        for m in range(2):
            plus = images[2 * m * lines : (2 * m + 1) * lines]
            minus = images[(2 * m + 1) * lines : (2 * m + 2) * lines]
            deltas.append(scaled * (level * (plus + minus) - 2.0 * plus * minus))
        low = jnp.concatenate(deltas, axis=0).astype(BF16)
        back = dot(back_ref[...], low).astype(BF16)
        for s in range(2):
            for j in range(parts):
                gained_ref[j, s * wide + 32 * q : s * wide + 32 * q + 32, :] = back[
                    (s * parts + j) * 32 : (s * parts + j) * 32 + 32
                ]
        if source == 0:
            doubled.append(deltas[0] + deltas[1])
    result = []
    for j in range(parts):
        lost = jnp.concatenate([d[32 * j : 32 * j + 32] for d in doubled], axis=0)
        result.append(dot(spread_ref[...], gained_ref[j]) - 2.0 * lost)
    return result


def early_kernel(sources, *refs):
    levels = refs[:sources]
    shift_ref, spread_ref, image_ref, back_ref, rate_ref, out_ref, shifted_ref, gained_ref = refs[sources:]
    result = nonlinear_tile(
        levels, shift_ref, spread_ref, image_ref, back_ref, rate_ref, shifted_ref, gained_ref
    )
    for j, values in enumerate(result):
        out_ref[j] = values


def final_kernel(sources, *refs):
    levels = refs[:sources]
    shift_ref, spread_ref, image_ref, back_ref, rate_ref = refs[sources : sources + 5]
    early_ref, moved_ref, depth_ref, wind_ref, wet_ref, out_ref = refs[sources + 5 : sources + 11]
    shifted_ref, gained_ref, gain_ref = refs[sources + 11 :]
    late = nonlinear_tile(
        levels, shift_ref, spread_ref, image_ref, back_ref, rate_ref, shifted_ref, gained_ref
    )
    freq_local, angles, width = moved_ref.shape
    own = freq_local * 8
    radian_freq = radian_rows(freq_local, width)
    wave_kh = dispersion(radian_freq, depth_ref[...])
    gain_ref[...] = wave_kh / (radian_freq * depth_ref[...])
    scale = radian_freq[:, 0:LANES] * (TIME_STEP * WIND_GROWTH)
    cosine, sine = angle_table(angles, LANES)
    restore = onehot(iota((GROUP, GROUP), 0) == place_of(iota((GROUP, GROUP), 1)))
    for g in range(width // GROUP):
        lanes = slice(g * HALF, (g + 1) * HALF)
        mixed = jnp.concatenate(
            [
                jnp.concatenate([early_ref[j, :, lanes], late[j][:, lanes]], axis=1)
                for j in range(angles // 8)
            ],
            axis=0,
        )
        high = mixed.astype(BF16)
        low = (mixed - high.astype(F32)).astype(BF16)
        transfer = dot(high, restore) + dot(low, restore)
        for half in range(GROUP // LANES):
            part = slice(g * GROUP + half * LANES, g * GROUP + (half + 1) * LANES)
            here = slice(half * LANES, (half + 1) * LANES)
            wet = jnp.broadcast_to(wet_ref[:, part].astype(F32), (angles, LANES))
            along = wind_ref[0:1, part] * cosine + wind_ref[1:2, part] * sine
            for f in range(freq_local):
                slow = jnp.broadcast_to(gain_ref[f : f + 1, part], (angles, LANES))
                rise = jnp.broadcast_to(scale[f : f + 1, :], (angles, LANES))
                growth = rise * jnp.maximum(along * slow - 1.0, 0.0)
                moved = moved_ref[f, :, part]
                gained = jnp.concatenate(
                    [
                        transfer[j * own + 8 * f : j * own + 8 * f + 8, here]
                        for j in range(angles // 8)
                    ],
                    axis=0,
                )
                out_ref[f, :, part] = wet * (moved + gained + growth * moved)


def whole(shape):
    return pl.BlockSpec(shape, lambda *_: (0,) * len(shape))


def lanes_of(lead, width):
    return pl.BlockSpec((*lead, width), lambda i: (0,) * len(lead) + (i,))


def params():
    return pltpu.CompilerParams(vmem_limit_bytes=VMEM_BYTES)


def cost(flops, moved):
    return pl.CostEstimate(flops=int(flops), bytes_accessed=int(moved), transcendentals=0)


def shards(
    spectrum, depths, currents, slopes, wind_speed, wet_mask,
    face_owner, face_block, freq_weights, angle_weights, transfer_rate,
):
    freq_local, angles, points = spectrum.shape
    group_count = lax.axis_size("spec")
    peers = lax.axis_size("blk")
    faces = face_block.shape[0]
    freqs = freq_local * group_count
    groups = points // GROUP
    own = freq_local * 8
    parts = angles // 8
    rows_fd = freq_local * angles
    wide = freqs * 8
    lines = 4 * angles
    edges = groups * EDGE
    capacity = max(2, (faces // 2 + peers - 2) // (peers - 1))
    reply_rows = peers * capacity * TILE
    size = freq_local * angles * points

    owner_row = face_owner.reshape(1, faces)
    block_row = face_block.reshape(1, faces)
    depth_row = depths.reshape(1, points)
    wet_row = wet_mask.reshape(1, points)

    table = lax.all_gather(owner_row * 256 + block_row, "blk", axis=0, tiled=True)

    moved_first, high, low, early = pl.pallas_call(
        transport_kernel,
        grid=(groups,),
        in_specs=[
            lanes_of((freq_local, angles), GROUP),
            lanes_of((1,), GROUP),
            lanes_of((2,), GROUP),
            lanes_of((2,), GROUP),
            lanes_of((1,), GROUP),
        ],
        out_specs=[
            lanes_of((freq_local, angles), GROUP),
            lanes_of((rows_fd,), EDGE),
            lanes_of((rows_fd,), EDGE),
            lanes_of((parts, own), HALF),
        ],
        out_shape=[
            jax.ShapeDtypeStruct((freq_local, angles, points), F32),
            jax.ShapeDtypeStruct((rows_fd, edges), BF16),
            jax.ShapeDtypeStruct((rows_fd, edges), BF16),
            jax.ShapeDtypeStruct((parts, own, groups * HALF), BF16),
        ],
        scratch_shapes=[
            pltpu.VMEM((freq_local, angles, 2 * GROUP), F32),
            pltpu.VMEM((freq_local, GROUP), F32),
            pltpu.VMEM((freq_local, GROUP), F32),
            pltpu.VMEM((freq_local, GROUP), F32),
        ],
        compiler_params=params(),
        cost_estimate=cost(100 * size, 12 * size),
        name="transport",
    )(spectrum, depth_row, currents, slopes, wet_row)

    def exchanged(array):
        return [
            lax.ppermute(
                array, "spec", [(s, (s - step) % group_count) for s in range(group_count)]
            )
            for step in range(1, group_count)
        ]

    early_levels = [early] + exchanged(early)

    reply = pl.pallas_call(
        functools.partial(select_kernel, capacity),
        out_shape=jax.ShapeDtypeStruct((peers, capacity * TILE, rows_fd), BF16),
        compiler_params=params(),
        cost_estimate=cost(2 * reply_rows * edges * rows_fd, 4 * rows_fd * edges),
        name="select",
    )(table, high)
    replies = lax.all_to_all(reply, "blk", split_axis=0, concat_axis=0, tiled=True)

    weights = pl.pallas_call(
        weights_kernel,
        out_shape=[
            jax.ShapeDtypeStruct((2 * wide, wide), BF16),
            jax.ShapeDtypeStruct((own, 2 * wide), BF16),
            jax.ShapeDtypeStruct((4 * lines, 2 * lines), BF16),
            jax.ShapeDtypeStruct((2 * lines, 2 * lines), BF16),
        ],
        compiler_params=params(),
        cost_estimate=cost(1e9, 1e6),
        name="weights",
    )(freq_weights, angle_weights)

    moved_local, reply_map = pl.pallas_call(
        functools.partial(local_kernel, capacity),
        grid=(groups,),
        in_specs=[
            whole((1, faces)),
            whole((1, faces)),
            whole((rows_fd, edges)),
            whole((rows_fd, edges)),
            lanes_of((freq_local, angles), GROUP),
        ],
        out_specs=[
            lanes_of((freq_local, angles), GROUP),
            lanes_of((reply_rows,), GROUP),
        ],
        out_shape=[
            jax.ShapeDtypeStruct((freq_local, angles, points), F32),
            jax.ShapeDtypeStruct((reply_rows, points), BF16),
        ],
        compiler_params=params(),
        cost_estimate=cost(4 * rows_fd * edges * points, 10 * size),
        name="local_inflow",
    )(owner_row, block_row, high, low, moved_first)

    moved, late = pl.pallas_call(
        late_kernel,
        grid=(groups,),
        in_specs=[
            whole((peers, capacity * TILE, rows_fd)),
            lanes_of((reply_rows,), GROUP),
            lanes_of((freq_local, angles), GROUP),
        ],
        out_specs=[
            lanes_of((freq_local, angles), GROUP),
            lanes_of((parts, own), HALF),
        ],
        out_shape=[
            jax.ShapeDtypeStruct((freq_local, angles, points), F32),
            jax.ShapeDtypeStruct((parts, own, groups * HALF), BF16),
        ],
        scratch_shapes=[pltpu.VMEM((rows_fd, reply_rows), BF16)],
        compiler_params=params(),
        cost_estimate=cost(2 * rows_fd * reply_rows * points, 10 * size),
        name="late_inflow",
    )(replies, reply_map, moved_local)

    late_levels = [late] + exchanged(late)
    tile = 2 * HALF if groups % 2 == 0 else HALF
    tiles = groups * HALF // tile
    weight_specs = [
        whole((2 * wide, wide)),
        whole((own, 2 * wide)),
        whole((4 * lines, 2 * lines)),
        whole((2 * lines, 2 * lines)),
        pl.BlockSpec(memory_space=pltpu.SMEM),
    ]
    tile_scratch = [
        pltpu.VMEM((parts, 2 * wide, tile), BF16),
        pltpu.VMEM((parts, 2 * wide, tile), BF16),
    ]
    gained_early = pl.pallas_call(
        functools.partial(early_kernel, group_count),
        grid=(tiles,),
        in_specs=[lanes_of((parts, own), tile)] * group_count + weight_specs,
        out_specs=lanes_of((parts, own), tile),
        out_shape=jax.ShapeDtypeStruct((parts, own, groups * HALF), F32),
        scratch_shapes=tile_scratch,
        compiler_params=params(),
        cost_estimate=cost(3e9, 3 * size),
        name="early_transfer",
    )(*early_levels, *weights, transfer_rate)

    return pl.pallas_call(
        functools.partial(final_kernel, group_count),
        grid=(tiles,),
        in_specs=[lanes_of((parts, own), tile)] * group_count
        + weight_specs
        + [
            lanes_of((parts, own), tile),
            lanes_of((freq_local, angles), 2 * tile),
            lanes_of((1,), 2 * tile),
            lanes_of((2,), 2 * tile),
            lanes_of((1,), 2 * tile),
        ],
        out_specs=lanes_of((freq_local, angles), 2 * tile),
        out_shape=jax.ShapeDtypeStruct((freq_local, angles, points), F32),
        scratch_shapes=tile_scratch + [pltpu.VMEM((freq_local, 2 * tile), F32)],
        compiler_params=params(),
        cost_estimate=cost(3e9, 12 * size),
        name="late_transfer",
    )(*late_levels, *weights, transfer_rate, gained_early, moved, depth_row, wind_speed, wet_row)


def solution(mesh):
    in_specs = (
        P("spec", None, "blk"),
        P("blk"),
        P(None, "blk"),
        P(None, "blk"),
        P(None, "blk"),
        P("blk"),
        P("blk", None),
        P("blk"),
        P(),
        P(),
        P(),
    )
    out_specs = P("spec", None, "blk")
    return jax.shard_map(shards, mesh=mesh, in_specs=in_specs, out_specs=out_specs, check_vma=False)
```

```python
import functools
import math

import jax
import jax.numpy as jnp
from jax import lax
from jax.experimental import pallas as pl
from jax.experimental.pallas import tpu as pltpu
from jax.sharding import PartitionSpec as P

GRAVITY = 9.81
TIME_STEP = 200.0
CELL_SIZE = 5500.0
LOWEST_FREQ = 0.0418
FREQ_GROWTH = 1.1
WIND_GROWTH = 0.0003
TURN_LIMIT = 0.9

TILE = 8
CELLS = TILE * TILE
GROUP = 256
HALF = 128
EDGE = 128
LANES = 128
VMEM_BYTES = 60 * 1024 * 1024

F32 = jnp.float32
BF16 = jnp.bfloat16
I32 = jnp.int32


def iota(shape, dim):
    return lax.broadcasted_iota(I32, shape, dim)


def onehot(mask):
    return jnp.where(mask, 1.0, 0.0).astype(BF16)


def dot(a, b):
    return jnp.dot(a, b, preferred_element_type=F32)


def dot_nt(a, b):
    return lax.dot_general(a, b, (((1,), (1,)), ((), ())), preferred_element_type=F32)


def dispersion(radian_freq, water_depth):
    deep_kh = radian_freq * radian_freq / GRAVITY * water_depth
    wave_kh = deep_kh / jnp.sqrt(jnp.tanh(deep_kh))
    return wave_kh


def radian_rows(freq_local, width):
    index = iota((freq_local, width), 0) + lax.axis_index("spec") * freq_local
    return (2.0 * math.pi * LOWEST_FREQ) * jnp.exp(index.astype(F32) * math.log(FREQ_GROWTH))


def angle_table(angles, width):
    values = iota((angles, width), 0).astype(F32) * (2.0 * math.pi / angles)
    return jnp.cos(values), jnp.sin(values)


def place_of(point):
    block = point // CELLS
    row = (point // TILE) % TILE
    col = point % TILE
    inner = (row >= 1) & (row <= 6) & (col >= 1) & (col <= 6)
    rank = (row - 1) * 6 + jnp.clip(col - 1, 0, 6)
    early = inner & (rank < 32)
    before = jnp.clip(rank, 0, 32)
    return jnp.where(early, block * 32 + rank, HALF + block * 32 + point % CELLS - before)


def edges_kernel(
    spec_ref, depth_ref, current_ref, wet_ref, high_ref, low_ref, flux_ref, group_ref
):
    freq_local, angles, width = spec_ref.shape
    group_speeds(freq_local, depth_ref, wet_ref, group_ref)
    wet = wet_ref[...].astype(F32) * (TIME_STEP / CELL_SIZE)
    drift_x = current_ref[0:1, :] * wet
    drift_y = current_ref[1:2, :] * wet
    cosine, sine = angle_table(angles, LANES)
    lane = iota((angles, LANES), 1)
    col = lane % TILE
    row = (lane // TILE) % TILE
    away_x = jnp.where(col == TILE - 1, 1.0, jnp.where(col == 0, -1.0, 0.0))
    away_y = jnp.where(row == TILE - 1, 1.0, jnp.where(row == 0, -1.0, 0.0))
    lean_x, lean_y = cosine * away_x, sine * away_y
    for half in range(width // LANES):
        part = slice(half * LANES, (half + 1) * LANES)
        drift_xp = jnp.broadcast_to(drift_x[:, part], (angles, LANES)) * away_x
        drift_yp = jnp.broadcast_to(drift_y[:, part], (angles, LANES)) * away_y
        for f in range(freq_local):
            energy = spec_ref[f, :, part]
            speed = jnp.broadcast_to(group_ref[f : f + 1, part], (angles, LANES))
            flux_ref[f, :, part] = jnp.maximum(speed * lean_x + drift_xp, 0.0) * energy
            flux_ref[f, :, width + half * LANES : width + (half + 1) * LANES] = (
                jnp.maximum(speed * lean_y + drift_yp, 0.0) * energy
            )
    source = iota((2 * width, EDGE), 0)
    upright = source // width
    point = source % width
    block = point // CELLS
    prow = (point // TILE) % TILE
    pcol = point % TILE
    across = jnp.where(upright == 0, pcol, prow)
    along = jnp.where(upright == 0, prow, pcol)
    edge = upright * 64 + jnp.where(across == 0, 0, 32) + block * TILE + along
    on_edge = (across == 0) | (across == TILE - 1)
    pick = onehot(on_edge & (edge == iota((2 * width, EDGE), 1)))
    flux = flux_ref[...].reshape(freq_local * angles, 2 * width)
    high = flux.astype(BF16)
    low = (flux - high.astype(F32)).astype(BF16)
    high_ref[...] = dot(high, pick).astype(BF16)
    low_ref[...] = dot(low, pick).astype(BF16)


def group_speeds(freq_local, depth_ref, wet_ref, group_ref):
    width = depth_ref.shape[1]
    radian_freq = radian_rows(freq_local, width)
    depth = depth_ref[...]
    wave_kh = dispersion(radian_freq, depth)
    decay_two = jnp.exp(-2.0 * wave_kh)
    denom = 1.0 - decay_two * decay_two
    ratio = 4.0 * wave_kh * decay_two / denom
    phase = radian_freq * depth / wave_kh
    wet = wet_ref[...].astype(F32) * (TIME_STEP / CELL_SIZE)
    group_ref[...] = 0.5 * (1.0 + ratio) * phase * wet
    return 2.0 * radian_freq * decay_two / denom


def request_kernel(capacity, owner_ref, block_ref, request_ref):
    peers = request_ref.shape[0]
    faces = owner_ref.shape[1]
    mine = lax.axis_index("blk")
    peer = iota((peers, faces), 0)
    asked = (owner_ref[...] == peer) & (peer != mine)
    earlier = onehot(iota((faces, faces), 0) < iota((faces, faces), 1))
    rank = dot(onehot(asked), earlier).astype(I32)
    side = iota((1, faces), 1) % 4
    block = block_ref[...]
    base = (block // 4) * EDGE + (side // 2) * 64 + (1 - side % 2) * 32 + (block % 4) * TILE + 1
    base = base.astype(F32)
    lane = iota((peers, LANES), 1)
    result = jnp.zeros((peers, LANES), F32)
    for k in range(capacity):
        found = jnp.sum(jnp.where(asked & (rank == k), base, 0.0), axis=1, keepdims=True)
        result = jnp.where(lane == k, found, result)
    result = result.astype(I32)
    for p in range(peers):
        request_ref[p] = result[p : p + 1]


def select_kernel(capacity, request_ref, high_ref, reply_ref):
    peers = request_ref.shape[0]
    rows = peers * capacity * TILE
    edges = high_ref.shape[1]
    asked = jnp.concatenate([request_ref[p] for p in range(peers)], axis=0)
    coarse = (asked // 16).astype(F32).astype(BF16)
    fine = (asked % 16).astype(F32).astype(BF16)
    spread = onehot(iota((rows, peers), 0) // (capacity * TILE) == iota((rows, peers), 1))
    asked = 16.0 * dot(spread, coarse) + dot(spread, fine)
    row = iota((rows, LANES), 0)
    slot = (row // TILE) % capacity
    chosen = (slot == iota((rows, LANES), 1)) & (asked > 0.0)
    target = jnp.sum(
        jnp.where(chosen, asked + (row % TILE).astype(F32), 0.0), axis=1, keepdims=True
    )
    pick = onehot(iota((rows, edges), 1).astype(F32) + 1.0 == target)
    reply = dot_nt(pick, high_ref[...]).astype(BF16)
    for p in range(peers):
        reply_ref[p] = reply[p * capacity * TILE : (p + 1) * capacity * TILE]


def transport_kernel(
    capacity, first_group,
    owner_ref, block_ref, high_edge_ref, low_edge_ref,
    spec_ref, depth_ref, current_ref, slope_ref, wet_ref,
    moved_ref, early_ref, map_ref,
    group_ref, turn_x_ref, turn_y_ref,
):
    freq_local, angles, width = spec_ref.shape
    turn = group_speeds(freq_local, depth_ref, wet_ref, group_ref)
    turn = turn * (TIME_STEP / (2.0 * math.pi / angles))
    turn_x_ref[...] = turn * slope_ref[0:1, :]
    turn_y_ref[...] = turn * slope_ref[1:2, :]
    wet = wet_ref[...].astype(F32) * (TIME_STEP / CELL_SIZE)
    drift_x = current_ref[0:1, :] * wet
    drift_y = current_ref[1:2, :] * wet
    cosine, sine = angle_table(angles, LANES)
    lane = iota((angles, LANES), 1)
    col = lane % TILE
    row = (lane // TILE) % TILE
    west, east = col == 0, col == TILE - 1
    south, north = row == 0, row == TILE - 1
    pick = inflow_maps(capacity, first_group, owner_ref, block_ref, high_edge_ref.shape[1], width, map_ref)
    inflow = dot(high_edge_ref[...], pick) + dot(low_edge_ref[...], pick)
    moved_ref[...] = inflow.reshape(freq_local, angles, width)
    for half in range(width // LANES):
        part = slice(half * LANES, (half + 1) * LANES)
        drift_xp = jnp.broadcast_to(drift_x[:, part], (angles, LANES))
        drift_yp = jnp.broadcast_to(drift_y[:, part], (angles, LANES))
        for f in range(freq_local):
            energy = spec_ref[f, :, part]
            speed = jnp.broadcast_to(group_ref[f : f + 1, part], (angles, LANES))
            turn_x = jnp.broadcast_to(turn_x_ref[f : f + 1, part], (angles, LANES))
            turn_y = jnp.broadcast_to(turn_y_ref[f : f + 1, part], (angles, LANES))
            flow_x = (speed * cosine + drift_xp) * energy
            flow_y = (speed * sine + drift_yp) * energy
            turning = jnp.clip(sine * turn_x - cosine * turn_y, -TURN_LIMIT, TURN_LIMIT)
            flow_t = turning * energy
            right = jnp.maximum(flow_x, 0.0)
            left = right - flow_x
            up = jnp.maximum(flow_y, 0.0)
            down = up - flow_y
            ahead = jnp.maximum(flow_t, 0.0)
            back = ahead - flow_t
            total = energy - (right + left) - (up + down) - (ahead + back)
            total = total + pltpu.roll(jnp.where(east, 0.0, right), 1, 1)
            total = total + pltpu.roll(jnp.where(west, 0.0, left), LANES - 1, 1)
            total = total + pltpu.roll(jnp.where(north, 0.0, up), TILE, 1)
            total = total + pltpu.roll(jnp.where(south, 0.0, down), LANES - TILE, 1)
            total = total + pltpu.roll(ahead, 1, 0) + pltpu.roll(back, angles - 1, 0)
            moved_ref[f, :, part] = moved_ref[f, :, part] + total
    inner = onehot(place_of(iota((width, HALF), 0)) == iota((width, HALF), 1))
    for j in range(angles // 8):
        levels = moved_ref[:, 8 * j : 8 * j + 8, :].reshape(freq_local * 8, width).astype(BF16)
        early_ref[j] = dot(levels, inner).astype(BF16)


def inflow_maps(capacity, first_group, owner_ref, block_ref, edges, width, map_ref):
    faces = owner_ref.shape[1]
    rows = map_ref.shape[0]
    mine = lax.axis_index("blk")
    owner = owner_ref[...]
    by_column = jnp.broadcast_to(owner, (faces, faces))
    below = iota((faces, faces), 0)
    right = iota((faces, faces), 1)
    by_row = jnp.sum(jnp.where(below == right, by_column, 0).astype(F32), axis=1, keepdims=True)
    equal = (by_row == by_column.astype(F32)) & (below < right)
    rank = jnp.sum(jnp.where(equal, 1.0, 0.0), axis=0, keepdims=True)
    table = jnp.concatenate(
        [block_ref[...].astype(F32), owner.astype(F32), rank, jnp.zeros((5, faces), F32)], axis=0
    ).astype(BF16)
    point = iota((faces, width), 1)
    block = point // CELLS + (first_group + pl.program_id(0)) * (width // CELLS)
    col = point % TILE
    row = (point // TILE) % TILE
    face = iota((faces, width), 0)
    at_x = dot(table, onehot((face == block * 4 + jnp.where(col == 0, 0, 1)))).astype(I32)
    at_y = dot(table, onehot((face == block * 4 + jnp.where(row == 0, 2, 3)))).astype(I32)
    point = iota((1, width), 1)
    col = point % TILE
    row = (point // TILE) % TILE

    def ids(found, across, along, upright):
        edge = (across == 0) | (across == TILE - 1)
        from_block, from_owner, slot = found[0:1], found[1:2], found[2:3]
        local = edge & (from_owner == mine)
        remote = edge & (from_owner != mine)
        base = upright * 64 + jnp.where(across == 0, 32, 0)
        source = (from_block // 4) * EDGE + base + (from_block % 4) * TILE + along
        reply = (from_owner * capacity + slot) * TILE + along
        return jnp.where(local, source, -1), jnp.where(remote, reply, -1)

    source_x, reply_x = ids(at_x, col, row, 0)
    source_y, reply_y = ids(at_y, row, col, 1)
    line = iota((rows, width), 0)
    map_ref[...] = onehot((line == reply_x) | (line == reply_y))
    line = iota((edges, width), 0)
    return onehot((line == source_x) | (line == source_y))


def weights_kernel(freq_ref, angle_ref, shift_ref, spread_ref, image_ref, back_ref):
    freqs = freq_ref.shape[1]
    angles = angle_ref.shape[2]
    wide = freqs * 8
    own = spread_ref.shape[0]
    start = lax.axis_index("spec") * (own // 8)
    rows = onehot((iota((wide, freqs), 0) // 8 + start) % freqs == iota((wide, freqs), 1))
    same = iota((wide, wide), 0) % 8 == iota((wide, wide), 1) % 8
    for s in range(2):
        weights = freq_ref[s]
        left = dot(rows, weights).astype(BF16)
        shift_ref[s * wide : (s + 1) * wide, :] = jnp.where(same, dot_nt(left, rows), 0.0).astype(BF16)
        turned = dot_nt(rows[:own], weights).astype(BF16)
        spread_ref[:, s * wide : (s + 1) * wide] = jnp.where(
            same[:own], dot_nt(turned, rows), 0.0
        ).astype(BF16)
    stacked = jnp.concatenate(
        [angle_ref[m, s].astype(F32) for m in range(2) for s in range(2)], axis=0
    ).astype(BF16)
    lines = angles * 4
    r = iota((4 * lines, 4 * angles), 0)
    c = iota((4 * lines, 4 * angles), 1)
    direction = (r // 32) % (angles // 8) * 8 + r % 8
    chosen = onehot((r // lines) * angles + direction == c)
    lines_rows = dot(chosen, stacked).astype(BF16)
    r = iota((2 * lines, angles), 0)
    column = onehot((r // 32) % (angles // 8) * 8 + r % 8 == iota((2 * lines, angles), 1))
    r = iota((4 * lines, 2 * lines), 0)
    c = iota((4 * lines, 2 * lines), 1)
    keep = ((r // lines) % 2 == c // lines) & ((r // 8) % 4 == (c // 8) % 4)
    image_ref[...] = jnp.where(keep, dot_nt(lines_rows, column), 0.0).astype(BF16)
    for s in range(2):
        r = iota((2 * lines, 4 * angles), 0)
        c = iota((2 * lines, 4 * angles), 1)
        direction = (r // 32) % (angles // 8) * 8 + r % 8
        chosen = onehot(((r // lines) * 2 + s) * angles + direction == c)
        lines_rows = dot(chosen, stacked).astype(BF16)
        r = iota((lines, 2 * lines), 0)
        c = iota((lines, 2 * lines), 1)
        keep = (r // 8) % 4 == (c // 8) % 4
        back_ref[s * lines : (s + 1) * lines, :] = jnp.where(
            keep, dot_nt(column[:lines], lines_rows), 0.0
        ).astype(BF16)


def late_kernel(reply_ref, map_ref, moved_in_ref, moved_ref, late_ref, turned_ref):
    freq_local, angles, width = moved_ref.shape
    rows = map_ref.shape[0]

    @pl.when(pl.program_id(0) == 0)
    def _():
        reply = reply_ref[...].astype(F32).reshape(rows, freq_local * angles)
        turned_ref[...] = reply.T.astype(BF16)

    inflow = dot(turned_ref[...], map_ref[...])
    moved_ref[...] = moved_in_ref[...] + inflow.reshape(freq_local, angles, width)
    outer = onehot(place_of(iota((width, HALF), 0)) == iota((width, HALF), 1) + HALF)
    for j in range(angles // 8):
        levels = moved_ref[:, 8 * j : 8 * j + 8, :].reshape(freq_local * 8, width).astype(BF16)
        late_ref[j] = dot(levels, outer).astype(BF16)


def nonlinear_tile(level_refs, shift_ref, spread_ref, image_ref, back_ref, rate_ref, shifted_ref, gained_ref):
    parts, own, width = level_refs[0].shape
    wide = shift_ref.shape[1]
    freqs = wide // 8
    lines = parts * 32
    start = lax.axis_index("spec") * (own // 8)
    for j in range(parts):
        levels = jnp.concatenate([ref[j] for ref in level_refs], axis=0)
        shifted_ref[j] = dot(shift_ref[...], levels).astype(BF16)
    def image_of(q):
        shifted = jnp.concatenate(
            [
                shifted_ref[j, s * wide + 32 * q : s * wide + 32 * q + 32, :]
                for s in range(2)
                for j in range(parts)
            ],
            axis=0,
        )
        return dot(image_ref[...], shifted)

    doubled = []
    coming = image_of(0)
    for q in range(freqs // 4):
        source, place = divmod(q * 32, own)
        images = coming
        if q + 1 < freqs // 4:
            coming = image_of(q + 1)
        level = jnp.concatenate(
            [level_refs[source][j, place : place + 32, :].astype(F32) for j in range(parts)], axis=0
        )
        rates = [rate_ref[(start + 4 * q + k) % freqs] for k in range(4)]
        scaled = jnp.concatenate(
            [
                level[32 * j + 8 * k : 32 * j + 8 * k + 8] * rates[k]
                for j in range(parts)
                for k in range(4)
            ],
            axis=0,
        )
        deltas = []
        for m in range(2):
            plus = images[2 * m * lines : (2 * m + 1) * lines]
            minus = images[(2 * m + 1) * lines : (2 * m + 2) * lines]
            deltas.append(scaled * (level * (plus + minus) - 2.0 * plus * minus))
        low = jnp.concatenate(deltas, axis=0).astype(BF16)
        back = dot(back_ref[...], low).astype(BF16)
        for s in range(2):
            for j in range(parts):
                gained_ref[j, s * wide + 32 * q : s * wide + 32 * q + 32, :] = back[
                    (s * parts + j) * 32 : (s * parts + j) * 32 + 32
                ]
        if source == 0:
            doubled.append(deltas[0] + deltas[1])
    result = []
    for j in range(parts):
        lost = jnp.concatenate([d[32 * j : 32 * j + 32] for d in doubled], axis=0)
        result.append(dot(spread_ref[...], gained_ref[j]) - 2.0 * lost)
    return result


def early_kernel(sources, *refs):
    levels = refs[:sources]
    shift_ref, spread_ref, image_ref, back_ref, rate_ref, out_ref, shifted_ref, gained_ref = refs[sources:]
    result = nonlinear_tile(
        levels, shift_ref, spread_ref, image_ref, back_ref, rate_ref, shifted_ref, gained_ref
    )
    for j, values in enumerate(result):
        out_ref[j] = values


def final_kernel(sources, *refs):
    levels = refs[:sources]
    shift_ref, spread_ref, image_ref, back_ref, rate_ref = refs[sources : sources + 5]
    early_ref, moved_ref, depth_ref, wind_ref, wet_ref = refs[sources + 5 : sources + 10]
    out_ref, shifted_ref, gained_ref, gain_ref = refs[-4:]
    late = nonlinear_tile(
        levels, shift_ref, spread_ref, image_ref, back_ref, rate_ref, shifted_ref, gained_ref
    )
    freq_local, angles, width = moved_ref.shape
    own = freq_local * 8
    radian_freq = radian_rows(freq_local, width)
    wave_kh = dispersion(radian_freq, depth_ref[...])
    gain_ref[...] = wave_kh / (radian_freq * depth_ref[...])
    scale = radian_freq[:, 0:LANES] * (TIME_STEP * WIND_GROWTH)
    cosine, sine = angle_table(angles, LANES)
    restore = onehot(iota((GROUP, GROUP), 0) == place_of(iota((GROUP, GROUP), 1)))
    for g in range(width // GROUP):
        lanes = slice(g * HALF, (g + 1) * HALF)
        mixed = jnp.concatenate(
            [
                jnp.concatenate([early_ref[j, :, lanes], late[j][:, lanes]], axis=1)
                for j in range(angles // 8)
            ],
            axis=0,
        )
        high = mixed.astype(BF16)
        low = (mixed - high.astype(F32)).astype(BF16)
        transfer = dot(high, restore) + dot(low, restore)
        for half in range(GROUP // LANES):
            part = slice(g * GROUP + half * LANES, g * GROUP + (half + 1) * LANES)
            here = slice(half * LANES, (half + 1) * LANES)
            wet = jnp.broadcast_to(wet_ref[:, part].astype(F32), (angles, LANES))
            along = wind_ref[0:1, part] * cosine + wind_ref[1:2, part] * sine
            for f in range(freq_local):
                slow = jnp.broadcast_to(gain_ref[f : f + 1, part], (angles, LANES))
                rise = jnp.broadcast_to(scale[f : f + 1, :], (angles, LANES))
                growth = rise * jnp.maximum(along * slow - 1.0, 0.0)
                moved = moved_ref[f, :, part]
                gained = jnp.concatenate(
                    [
                        transfer[j * own + 8 * f : j * own + 8 * f + 8, here]
                        for j in range(angles // 8)
                    ],
                    axis=0,
                )
                out_ref[f, :, part] = wet * (moved + gained + growth * moved)


def whole(shape):
    return pl.BlockSpec(shape, lambda *_: (0,) * len(shape))


def lanes_of(lead, width, first=0):
    return pl.BlockSpec((*lead, width), lambda i: (0,) * len(lead) + (i + first,))


def params():
    return pltpu.CompilerParams(vmem_limit_bytes=VMEM_BYTES)


def cost(flops, moved):
    return pl.CostEstimate(flops=int(flops), bytes_accessed=int(moved), transcendentals=0)


def shards(
    spectrum, depths, currents, slopes, wind_speed, wet_mask,
    face_owner, face_block, freq_weights, angle_weights, transfer_rate,
):
    freq_local, angles, points = spectrum.shape
    group_count = lax.axis_size("spec")
    peers = lax.axis_size("blk")
    faces = face_block.shape[0]
    freqs = freq_local * group_count
    groups = points // GROUP
    own = freq_local * 8
    parts = angles // 8
    rows_fd = freq_local * angles
    wide = freqs * 8
    lines = 4 * angles
    edges = groups * EDGE
    capacity = max(2, (faces // 2 + peers - 2) // (peers - 1))
    reply_rows = peers * capacity * TILE
    size = freq_local * angles * points

    owner_row = face_owner.reshape(1, faces)
    block_row = face_block.reshape(1, faces)
    depth_row = depths.reshape(1, points)
    wet_row = wet_mask.reshape(1, points)

    requests = pl.pallas_call(
        functools.partial(request_kernel, capacity),
        out_shape=jax.ShapeDtypeStruct((peers, 1, LANES), I32),
        compiler_params=params(),
        cost_estimate=cost(1e6, 1e5),
        name="requests",
    )(owner_row, block_row)
    asked = lax.all_to_all(requests, "blk", split_axis=0, concat_axis=0, tiled=True)

    high, low = pl.pallas_call(
        edges_kernel,
        grid=(groups,),
        in_specs=[
            lanes_of((freq_local, angles), GROUP),
            lanes_of((1,), GROUP),
            lanes_of((2,), GROUP),
            lanes_of((1,), GROUP),
        ],
        out_specs=[lanes_of((rows_fd,), EDGE)] * 2,
        out_shape=[jax.ShapeDtypeStruct((rows_fd, edges), BF16)] * 2,
        scratch_shapes=[
            pltpu.VMEM((freq_local, angles, 2 * GROUP), F32),
            pltpu.VMEM((freq_local, GROUP), F32),
        ],
        compiler_params=params(),
        cost_estimate=cost(50 * size, 8 * size),
        name="edges",
    )(spectrum, depth_row, currents, wet_row)

    reply = pl.pallas_call(
        functools.partial(select_kernel, capacity),
        out_shape=jax.ShapeDtypeStruct((peers, capacity * TILE, rows_fd), BF16),
        compiler_params=params(),
        cost_estimate=cost(2 * reply_rows * edges * rows_fd, 4 * rows_fd * edges),
        name="select",
    )(asked, high)
    replies = lax.all_to_all(reply, "blk", split_axis=0, concat_axis=0, tiled=True)

    weights = pl.pallas_call(
        weights_kernel,
        out_shape=[
            jax.ShapeDtypeStruct((2 * wide, wide), BF16),
            jax.ShapeDtypeStruct((own, 2 * wide), BF16),
            jax.ShapeDtypeStruct((4 * lines, 2 * lines), BF16),
            jax.ShapeDtypeStruct((2 * lines, 2 * lines), BF16),
        ],
        compiler_params=params(),
        cost_estimate=cost(1e9, 1e6),
        name="weights",
    )(freq_weights, angle_weights)

    def exchanged(array):
        return [
            lax.ppermute(
                array, "spec", [(s, (s - step) % group_count) for s in range(group_count)]
            )
            for step in range(1, group_count)
        ]

    halves = 2
    half_groups = groups // halves
    half_points = points // halves
    tile = half_groups * HALF
    wave = (freq_local, angles)

    moved_own, early, reply_maps = [], [], []
    for h in range(halves):
        first = h * half_groups
        out = pl.pallas_call(
            functools.partial(transport_kernel, capacity, first),
            grid=(half_groups,),
            in_specs=[
                whole((1, faces)),
                whole((1, faces)),
                whole((rows_fd, edges)),
                whole((rows_fd, edges)),
                lanes_of(wave, GROUP, first),
                lanes_of((1,), GROUP, first),
                lanes_of((2,), GROUP, first),
                lanes_of((2,), GROUP, first),
                lanes_of((1,), GROUP, first),
            ],
            out_specs=[
                lanes_of(wave, GROUP),
                lanes_of((parts, own), HALF),
                lanes_of((reply_rows,), GROUP),
            ],
            out_shape=[
                jax.ShapeDtypeStruct((*wave, half_points), F32),
                jax.ShapeDtypeStruct((parts, own, tile), BF16),
                jax.ShapeDtypeStruct((reply_rows, half_points), BF16),
            ],
            scratch_shapes=[pltpu.VMEM((freq_local, GROUP), F32)] * 3,
            compiler_params=params(),
            cost_estimate=cost(100 * size, 12 * size),
            name=f"transport_{h}",
        )(owner_row, block_row, high, low, spectrum, depth_row, currents, slopes, wet_row)
        moved_own.append(out[0])
        early.append([out[1]] + exchanged(out[1]))
        reply_maps.append(out[2])

    moved, late = [], []
    for h in range(halves):
        out = pl.pallas_call(
            late_kernel,
            grid=(half_groups,),
            in_specs=[
                whole((peers, capacity * TILE, rows_fd)),
                lanes_of((reply_rows,), GROUP),
                lanes_of(wave, GROUP),
            ],
            out_specs=[lanes_of(wave, GROUP), lanes_of((parts, own), HALF)],
            out_shape=[
                jax.ShapeDtypeStruct((*wave, half_points), F32),
                jax.ShapeDtypeStruct((parts, own, tile), BF16),
            ],
            scratch_shapes=[pltpu.VMEM((rows_fd, reply_rows), BF16)],
            compiler_params=params(),
            cost_estimate=cost(rows_fd * reply_rows * points, 5 * size),
            name=f"late_inflow_{h}",
        )(replies, reply_maps[h], moved_own[h])
        moved.append(out[0])
        late.append([out[1]] + exchanged(out[1]))

    weight_specs = [
        whole((2 * wide, wide)),
        whole((own, 2 * wide)),
        whole((4 * lines, 2 * lines)),
        whole((2 * lines, 2 * lines)),
        pl.BlockSpec(memory_space=pltpu.SMEM),
    ]
    tile_scratch = [pltpu.VMEM((parts, 2 * wide, tile), BF16)] * 2
    level_specs = [whole((parts, own, tile))] * group_count
    gained = [
        pl.pallas_call(
            functools.partial(early_kernel, group_count),
            in_specs=level_specs + weight_specs,
            out_specs=whole((parts, own, tile)),
            out_shape=jax.ShapeDtypeStruct((parts, own, tile), F32),
            scratch_shapes=tile_scratch,
            compiler_params=params(),
            cost_estimate=cost(1.5e9, 2 * size),
            name=f"early_transfer_{h}",
        )(*early[h], *weights, transfer_rate)
        for h in range(halves)
    ]
    result = []
    for h in range(halves):
        operands = [
            *late[h], *weights, transfer_rate, gained[h], moved[h], depth_row, wind_speed, wet_row, *result,
        ]
        result = [
            pl.pallas_call(
                functools.partial(final_kernel, group_count),
                grid=(1,),
                in_specs=level_specs
                + weight_specs
                + [
                    whole((parts, own, tile)),
                    whole((*wave, half_points)),
                    lanes_of((1,), half_points, h),
                    lanes_of((2,), half_points, h),
                    lanes_of((1,), half_points, h),
                ]
                + [pl.BlockSpec(memory_space=pl.ANY)] * len(result),
                out_specs=lanes_of(wave, half_points, h),
                out_shape=jax.ShapeDtypeStruct((*wave, points), F32),
                scratch_shapes=tile_scratch + [pltpu.VMEM((freq_local, half_points), F32)],
                input_output_aliases={len(operands) - 1: 0} if result else {},
                compiler_params=params(),
                cost_estimate=cost(1.5e9, 6 * size),
                name=f"late_transfer_{h}",
            )(*operands)
        ]
    return result[0]


def solution(mesh):
    in_specs = (
        P("spec", None, "blk"),
        P("blk"),
        P(None, "blk"),
        P(None, "blk"),
        P(None, "blk"),
        P("blk"),
        P("blk", None),
        P("blk"),
        P(),
        P(),
        P(),
    )
    out_specs = P("spec", None, "blk")
    return jax.shard_map(shards, mesh=mesh, in_specs=in_specs, out_specs=out_specs, check_vma=False)
```

```python
import functools
import math

import jax
import jax.numpy as jnp
from jax import lax
from jax.experimental import pallas as pl
from jax.experimental.pallas import tpu as pltpu
from jax.sharding import PartitionSpec as P

GRAVITY = 9.81
TIME_STEP = 200.0
CELL_SIZE = 5500.0
LOWEST_FREQ = 0.0418
FREQ_GROWTH = 1.1
WIND_GROWTH = 0.0003
TURN_LIMIT = 0.9

TILE = 8
CELLS = TILE * TILE
GROUP = 256
HALF = 128
EDGE = 128
LANES = 128
VMEM_BYTES = 24 * 1024 * 1024

F32 = jnp.float32
BF16 = jnp.bfloat16
I32 = jnp.int32


def iota(shape, dim):
    return lax.broadcasted_iota(I32, shape, dim)


def onehot(mask):
    return jnp.where(mask, 1.0, 0.0).astype(BF16)


def dot(a, b):
    return jnp.dot(a, b, preferred_element_type=F32)


def dot_nt(a, b):
    return lax.dot_general(a, b, (((1,), (1,)), ((), ())), preferred_element_type=F32)


def dispersion(radian_freq, water_depth):
    deep_kh = radian_freq * radian_freq / GRAVITY * water_depth
    wave_kh = deep_kh / jnp.sqrt(jnp.tanh(deep_kh))
    return wave_kh


def radian_rows(freq_local, width):
    index = iota((freq_local, width), 0) + lax.axis_index("spec") * freq_local
    return (2.0 * math.pi * LOWEST_FREQ) * jnp.exp(index.astype(F32) * math.log(FREQ_GROWTH))


def angle_table(angles, width):
    values = iota((angles, width), 0).astype(F32) * (2.0 * math.pi / angles)
    return jnp.cos(values), jnp.sin(values)


def place_of(point):
    block = point // CELLS
    row = (point // TILE) % TILE
    col = point % TILE
    inner = (row >= 1) & (row <= 6) & (col >= 1) & (col <= 6)
    rank = (row - 1) * 6 + jnp.clip(col - 1, 0, 6)
    early = inner & (rank < 32)
    before = jnp.clip(rank, 0, 32)
    return jnp.where(early, block * 32 + rank, HALF + block * 32 + point % CELLS - before)


def edge_columns(width):
    source = iota((2 * width, EDGE), 0)
    upright = source // width
    point = source % width
    block = point // CELLS
    row = (point // TILE) % TILE
    col = point % TILE
    across = jnp.where(upright == 0, col, row)
    along = jnp.where(upright == 0, row, col)
    edge = upright * 64 + jnp.where(across == 0, 0, 32) + block * TILE + along
    on_edge = (across == 0) | (across == TILE - 1)
    return onehot(on_edge & (edge == iota((2 * width, EDGE), 1)))


def fetch(sources, targets, sems, first=0):
    copies = [
        pltpu.make_async_copy(source, target, sems.at[first + k])
        for k, (source, target) in enumerate(zip(sources, targets))
    ]
    for copy in copies:
        copy.start()
    return copies


def request_kernel(capacity, owner_hbm, block_hbm, request_ref, owner_ref, block_ref, sems):
    copies = fetch([owner_hbm, block_hbm], [owner_ref, block_ref], sems)
    peers = request_ref.shape[0]
    faces = owner_ref.shape[1]
    mine = lax.axis_index("blk")
    for copy in copies:
        copy.wait()
    peer = iota((peers, faces), 0)
    asked = (owner_ref[...] == peer) & (peer != mine)
    earlier = onehot(iota((faces, faces), 0) < iota((faces, faces), 1))
    rank = dot(onehot(asked), earlier).astype(I32)
    side = iota((1, faces), 1) % 4
    block = block_ref[...]
    base = (block // 4) * EDGE + (side // 2) * 64 + (1 - side % 2) * 32 + (block % 4) * TILE + 1
    base = base.astype(F32)
    lane = iota((peers, LANES), 1)
    result = jnp.zeros((peers, LANES), F32)
    for k in range(capacity):
        found = jnp.sum(jnp.where(asked & (rank == k), base, 0.0), axis=1, keepdims=True)
        result = jnp.where(lane == k, found, result)
    result = result.astype(I32)
    for p in range(peers):
        request_ref[p] = result[p : p + 1]


def select_kernel(capacity, request_ref, high_ref, reply_ref):
    peers = request_ref.shape[0]
    rows = peers * capacity * TILE
    edges = high_ref.shape[1]
    asked = jnp.concatenate([request_ref[p] for p in range(peers)], axis=0)
    coarse = (asked // 16).astype(F32).astype(BF16)
    fine = (asked % 16).astype(F32).astype(BF16)
    spread = onehot(iota((rows, peers), 0) // (capacity * TILE) == iota((rows, peers), 1))
    asked = 16.0 * dot(spread, coarse) + dot(spread, fine)
    row = iota((rows, LANES), 0)
    slot = (row // TILE) % capacity
    chosen = (slot == iota((rows, LANES), 1)) & (asked > 0.0)
    target = jnp.sum(
        jnp.where(chosen, asked + (row % TILE).astype(F32), 0.0), axis=1, keepdims=True
    )
    pick = onehot(iota((rows, edges), 1).astype(F32) + 1.0 == target)
    reply = dot_nt(pick, high_ref[...]).astype(BF16)
    for p in range(peers):
        reply_ref[p] = reply[p * capacity * TILE : (p + 1) * capacity * TILE]


def transport_kernel(
    spec_hbm, depth_hbm, current_hbm, slope_hbm, wet_hbm,
    moved_ref, high_ref, low_ref, early_ref,
    spec_ref, depth_ref, current_ref, slope_ref, wet_ref,
    flux_ref, group_ref, turn_x_ref, turn_y_ref, drift_ref, sems,
):
    freq_local, angles, points = moved_ref.shape
    groups = points // GROUP
    small = fetch(
        [depth_hbm, wet_hbm, current_hbm, slope_hbm], [depth_ref, wet_ref, current_ref, slope_ref], sems
    )
    waves = fetch(
        [spec_hbm.at[:, :, g * GROUP : (g + 1) * GROUP] for g in range(groups)],
        [spec_ref.at[g] for g in range(groups)],
        sems,
        len(small),
    )
    cosine, sine = angle_table(angles, LANES)
    lane = iota((angles, LANES), 1)
    col = lane % TILE
    row = (lane // TILE) % TILE
    west, east = col == 0, col == TILE - 1
    south, north = row == 0, row == TILE - 1
    radian_freq = radian_rows(freq_local, points)
    for copy in small:
        copy.wait()
    depth = depth_ref[...]
    wave_kh = dispersion(radian_freq, depth)
    decay_two = jnp.exp(-2.0 * wave_kh)
    denom = 1.0 - decay_two * decay_two
    ratio = 4.0 * wave_kh * decay_two / denom
    phase = radian_freq * depth / wave_kh
    wet = wet_ref[...].astype(F32) * (TIME_STEP / CELL_SIZE)
    group_ref[...] = 0.5 * (1.0 + ratio) * phase * wet
    turn = 2.0 * radian_freq * decay_two / denom * (TIME_STEP / (2.0 * math.pi / angles))
    turn_x_ref[...] = turn * slope_ref[0:1, :]
    turn_y_ref[...] = turn * slope_ref[1:2, :]
    drift_ref[0:1, :] = current_ref[0:1, :] * wet
    drift_ref[1:2, :] = current_ref[1:2, :] * wet
    columns = edge_columns(GROUP)
    inner = onehot(place_of(iota((GROUP, HALF), 0)) == iota((GROUP, HALF), 1))

    def one_group(g, carry):
        pltpu.make_async_copy(
            spec_hbm.at[:, :, pl.ds(pl.multiple_of(g * GROUP, GROUP), GROUP)],
            spec_ref.at[g],
            sems.at[len(small) + g],
        ).wait()
        for half in range(GROUP // LANES):
            part = pl.ds(pl.multiple_of(g * GROUP + half * LANES, LANES), LANES)
            here = slice(half * LANES, (half + 1) * LANES)
            there = slice(GROUP + half * LANES, GROUP + (half + 1) * LANES)
            drift_x = jnp.broadcast_to(drift_ref[0:1, part], (angles, LANES))
            drift_y = jnp.broadcast_to(drift_ref[1:2, part], (angles, LANES))
            for f in range(freq_local):
                energy = spec_ref[g, f, :, here]
                speed = jnp.broadcast_to(group_ref[f : f + 1, part], (angles, LANES))
                turn_x = jnp.broadcast_to(turn_x_ref[f : f + 1, part], (angles, LANES))
                turn_y = jnp.broadcast_to(turn_y_ref[f : f + 1, part], (angles, LANES))
                flow_x = (speed * cosine + drift_x) * energy
                flow_y = (speed * sine + drift_y) * energy
                turning = jnp.clip(sine * turn_x - cosine * turn_y, -TURN_LIMIT, TURN_LIMIT)
                flow_t = turning * energy
                right = jnp.maximum(flow_x, 0.0)
                left = right - flow_x
                up = jnp.maximum(flow_y, 0.0)
                down = up - flow_y
                ahead = jnp.maximum(flow_t, 0.0)
                back = ahead - flow_t
                total = energy - (right + left) - (up + down) - (ahead + back)
                total = total + pltpu.roll(jnp.where(east, 0.0, right), 1, 1)
                total = total + pltpu.roll(jnp.where(west, 0.0, left), LANES - 1, 1)
                total = total + pltpu.roll(jnp.where(north, 0.0, up), TILE, 1)
                total = total + pltpu.roll(jnp.where(south, 0.0, down), LANES - TILE, 1)
                total = total + pltpu.roll(ahead, 1, 0) + pltpu.roll(back, angles - 1, 0)
                moved_ref[f, :, part] = total
                flux_ref[f, :, here] = jnp.where(east, right, left)
                flux_ref[f, :, there] = jnp.where(north, up, down)
        flux = flux_ref[...].reshape(freq_local * angles, 2 * GROUP)
        high = flux.astype(BF16)
        low = (flux - high.astype(F32)).astype(BF16)
        place = pl.ds(pl.multiple_of(g * EDGE, EDGE), EDGE)
        high_ref[:, place] = dot(high, columns).astype(BF16)
        low_ref[:, place] = dot(low, columns).astype(BF16)
        part = pl.ds(pl.multiple_of(g * GROUP, GROUP), GROUP)
        for j in range(angles // 8):
            levels = moved_ref[:, 8 * j : 8 * j + 8, part].reshape(freq_local * 8, GROUP).astype(BF16)
            early_ref[j, :, place] = dot(levels, inner).astype(BF16)
        return carry

    lax.fori_loop(0, groups, one_group, 0)


def local_kernel(
    capacity, owner_hbm, block_hbm, high_ref, low_ref, moved_in_ref, moved_ref, map_ref, owner_ref, block_ref, sems
):
    copies = fetch([owner_hbm, block_hbm], [owner_ref, block_ref], sems)
    for copy in copies:
        copy.wait()
    freq_local, angles, points = moved_ref.shape
    ranks = face_ranks(owner_ref, block_ref)
    for g in range(points // GROUP):
        part = slice(g * GROUP, (g + 1) * GROUP)
        pick, reply_map = inflow_maps(
            capacity, g, ranks, high_ref.shape[1], map_ref.shape[0]
        )
        map_ref[:, part] = reply_map
        inflow = dot(high_ref[...], pick) + dot(low_ref[...], pick)
        moved_ref[:, :, part] = moved_in_ref[:, :, part] + inflow.reshape(freq_local, angles, GROUP)


def face_ranks(owner_ref, block_ref):
    faces = owner_ref.shape[1]
    owner = owner_ref[...]
    by_column = jnp.broadcast_to(owner, (faces, faces))
    below = iota((faces, faces), 0)
    right = iota((faces, faces), 1)
    by_row = jnp.sum(jnp.where(below == right, by_column, 0).astype(F32), axis=1, keepdims=True)
    equal = (by_row == by_column.astype(F32)) & (below < right)
    rank = jnp.sum(jnp.where(equal, 1.0, 0.0), axis=0, keepdims=True)
    return jnp.concatenate(
        [block_ref[...].astype(F32), owner.astype(F32), rank, jnp.zeros((5, faces), F32)], axis=0
    ).astype(BF16)


def inflow_maps(capacity, group, table, edges, rows):
    faces = table.shape[1]
    width = GROUP
    mine = lax.axis_index("blk")
    point = iota((faces, width), 1)
    block = point // CELLS + group * (width // CELLS)
    col = point % TILE
    row = (point // TILE) % TILE
    face = iota((faces, width), 0)
    at_x = dot(table, onehot((face == block * 4 + jnp.where(col == 0, 0, 1)))).astype(I32)
    at_y = dot(table, onehot((face == block * 4 + jnp.where(row == 0, 2, 3)))).astype(I32)
    point = iota((1, width), 1)
    col = point % TILE
    row = (point // TILE) % TILE

    def ids(found, across, along, upright):
        edge = (across == 0) | (across == TILE - 1)
        from_block, from_owner, slot = found[0:1], found[1:2], found[2:3]
        local = edge & (from_owner == mine)
        remote = edge & (from_owner != mine)
        base = upright * 64 + jnp.where(across == 0, 32, 0)
        source = (from_block // 4) * EDGE + base + (from_block % 4) * TILE + along
        reply = (from_owner * capacity + slot) * TILE + along
        return jnp.where(local, source, -1), jnp.where(remote, reply, -1)

    source_x, reply_x = ids(at_x, col, row, 0)
    source_y, reply_y = ids(at_y, row, col, 1)
    line = iota((rows, width), 0)
    reply_map = onehot((line == reply_x) | (line == reply_y))
    line = iota((edges, width), 0)
    return onehot((line == source_x) | (line == source_y)), reply_map


def weights_kernel(freq_ref, angle_ref, shift_ref, spread_ref, image_ref, back_ref):
    freqs = freq_ref.shape[1]
    angles = angle_ref.shape[2]
    wide = freqs * 8
    own = spread_ref.shape[0]
    start = lax.axis_index("spec") * (own // 8)
    rows = onehot((iota((wide, freqs), 0) // 8 + start) % freqs == iota((wide, freqs), 1))
    same = iota((wide, wide), 0) % 8 == iota((wide, wide), 1) % 8
    for s in range(2):
        weights = freq_ref[s]
        left = dot(rows, weights).astype(BF16)
        shift_ref[s * wide : (s + 1) * wide, :] = jnp.where(same, dot_nt(left, rows), 0.0).astype(BF16)
        turned = dot_nt(rows[:own], weights).astype(BF16)
        spread_ref[:, s * wide : (s + 1) * wide] = jnp.where(
            same[:own], dot_nt(turned, rows), 0.0
        ).astype(BF16)
    stacked = jnp.concatenate(
        [angle_ref[m, s].astype(F32) for m in range(2) for s in range(2)], axis=0
    ).astype(BF16)
    lines = angles * 4
    r = iota((4 * lines, 4 * angles), 0)
    c = iota((4 * lines, 4 * angles), 1)
    direction = (r // 32) % (angles // 8) * 8 + r % 8
    chosen = onehot((r // lines) * angles + direction == c)
    lines_rows = dot(chosen, stacked).astype(BF16)
    r = iota((2 * lines, angles), 0)
    column = onehot((r // 32) % (angles // 8) * 8 + r % 8 == iota((2 * lines, angles), 1))
    r = iota((4 * lines, 2 * lines), 0)
    c = iota((4 * lines, 2 * lines), 1)
    keep = ((r // lines) % 2 == c // lines) & ((r // 8) % 4 == (c // 8) % 4)
    image_ref[...] = jnp.where(keep, dot_nt(lines_rows, column), 0.0).astype(BF16)
    for s in range(2):
        r = iota((2 * lines, 4 * angles), 0)
        c = iota((2 * lines, 4 * angles), 1)
        direction = (r // 32) % (angles // 8) * 8 + r % 8
        chosen = onehot(((r // lines) * 2 + s) * angles + direction == c)
        lines_rows = dot(chosen, stacked).astype(BF16)
        r = iota((lines, 2 * lines), 0)
        c = iota((lines, 2 * lines), 1)
        keep = (r // 8) % 4 == (c // 8) % 4
        back_ref[s * lines : (s + 1) * lines, :] = jnp.where(
            keep, dot_nt(column[:lines], lines_rows), 0.0
        ).astype(BF16)


def late_kernel(reply_ref, map_ref, moved_in_ref, moved_ref, late_ref):
    freq_local, angles, points = moved_ref.shape
    rows = map_ref.shape[0]
    reply = reply_ref[...].astype(F32).reshape(rows, freq_local * angles)
    turned = reply.T.astype(BF16)
    outer = onehot(place_of(iota((GROUP, HALF), 0)) == iota((GROUP, HALF), 1) + HALF)
    for g in range(points // GROUP):
        part = slice(g * GROUP, (g + 1) * GROUP)
        inflow = dot(turned, map_ref[:, part])
        moved_ref[:, :, part] = moved_in_ref[:, :, part] + inflow.reshape(freq_local, angles, GROUP)
        for j in range(angles // 8):
            levels = moved_ref[:, 8 * j : 8 * j + 8, part].reshape(freq_local * 8, GROUP)
            late_ref[j, :, g * HALF : (g + 1) * HALF] = dot(levels.astype(BF16), outer).astype(BF16)


def nonlinear_tile(level_refs, shift_ref, spread_ref, image_ref, back_ref, rate_ref, shifted_ref, gained_ref):
    parts, own, width = level_refs[0].shape
    wide = shift_ref.shape[1]
    freqs = wide // 8
    lines = parts * 32
    start = lax.axis_index("spec") * (own // 8)
    for j in range(parts):
        levels = jnp.concatenate([ref[j] for ref in level_refs], axis=0)
        shifted_ref[j] = dot(shift_ref[...], levels).astype(BF16)
    def image_of(q):
        shifted = jnp.concatenate(
            [
                shifted_ref[j, s * wide + 32 * q : s * wide + 32 * q + 32, :]
                for s in range(2)
                for j in range(parts)
            ],
            axis=0,
        )
        return dot(image_ref[...], shifted)

    doubled = []
    coming = image_of(0)
    for q in range(freqs // 4):
        source, place = divmod(q * 32, own)
        images = coming
        if q + 1 < freqs // 4:
            coming = image_of(q + 1)
        level = jnp.concatenate(
            [level_refs[source][j, place : place + 32, :].astype(F32) for j in range(parts)], axis=0
        )
        rates = [rate_ref[(start + 4 * q + k) % freqs] for k in range(4)]
        scaled = jnp.concatenate(
            [
                level[32 * j + 8 * k : 32 * j + 8 * k + 8] * rates[k]
                for j in range(parts)
                for k in range(4)
            ],
            axis=0,
        )
        deltas = []
        for m in range(2):
            plus = images[2 * m * lines : (2 * m + 1) * lines]
            minus = images[(2 * m + 1) * lines : (2 * m + 2) * lines]
            deltas.append(scaled * (level * (plus + minus) - 2.0 * plus * minus))
        low = jnp.concatenate(deltas, axis=0).astype(BF16)
        back = dot(back_ref[...], low).astype(BF16)
        for s in range(2):
            for j in range(parts):
                gained_ref[j, s * wide + 32 * q : s * wide + 32 * q + 32, :] = back[
                    (s * parts + j) * 32 : (s * parts + j) * 32 + 32
                ]
        if source == 0:
            doubled.append(deltas[0] + deltas[1])
    result = []
    for j in range(parts):
        lost = jnp.concatenate([d[32 * j : 32 * j + 32] for d in doubled], axis=0)
        result.append(dot(spread_ref[...], gained_ref[j]) - 2.0 * lost)
    return result


def early_kernel(sources, *refs):
    levels = refs[:sources]
    shift_ref, spread_ref, image_ref, back_ref, rate_ref, out_ref, shifted_ref, gained_ref = refs[sources:]
    result = nonlinear_tile(
        levels, shift_ref, spread_ref, image_ref, back_ref, rate_ref, shifted_ref, gained_ref
    )
    for j, values in enumerate(result):
        out_ref[j] = values


def final_kernel(sources, *refs):
    levels = refs[:sources]
    shift_ref, spread_ref, image_ref, back_ref, rate_ref = refs[sources : sources + 5]
    early_ref, moved_ref, depth_hbm, wind_hbm, wet_hbm, out_hbm = refs[sources + 5 : sources + 11]
    shifted_ref, gained_ref, late_ref, gain_ref, depth_ref, wind_ref, wet_ref, out_ref, sems = refs[
        sources + 11 :
    ]
    small = fetch([depth_hbm, wind_hbm, wet_hbm], [depth_ref, wind_ref, wet_ref], sems)
    late = nonlinear_tile(
        levels, shift_ref, spread_ref, image_ref, back_ref, rate_ref, shifted_ref, gained_ref
    )
    for j, values in enumerate(late):
        late_ref[j] = values
    freq_local, angles, points = moved_ref.shape
    groups = points // GROUP
    own = freq_local * 8
    for copy in small:
        copy.wait()
    radian_freq = radian_rows(freq_local, points)
    wave_kh = dispersion(radian_freq, depth_ref[...])
    gain_ref[...] = wave_kh / (radian_freq * depth_ref[...])
    scale = radian_freq[:, 0:LANES] * (TIME_STEP * WIND_GROWTH)
    cosine, sine = angle_table(angles, LANES)
    restore = onehot(iota((GROUP, GROUP), 0) == place_of(iota((GROUP, GROUP), 1)))

    def result_copy(g):
        part = pl.ds(pl.multiple_of(g * GROUP, GROUP), GROUP)
        return pltpu.make_async_copy(
            out_ref.at[:, :, part], out_hbm.at[:, :, part], sems.at[len(small) + g]
        )

    def one_group(g, carry):
        lanes = pl.ds(pl.multiple_of(g * HALF, HALF), HALF)
        mixed = jnp.concatenate(
            [
                jnp.concatenate([early_ref[j, :, lanes], late_ref[j, :, lanes]], axis=1)
                for j in range(angles // 8)
            ],
            axis=0,
        )
        high = mixed.astype(BF16)
        low = (mixed - high.astype(F32)).astype(BF16)
        transfer = dot(high, restore) + dot(low, restore)
        for half in range(GROUP // LANES):
            part = pl.ds(pl.multiple_of(g * GROUP + half * LANES, LANES), LANES)
            here = slice(half * LANES, (half + 1) * LANES)
            wet = jnp.broadcast_to(wet_ref[:, part].astype(F32), (angles, LANES))
            along = wind_ref[0:1, part] * cosine + wind_ref[1:2, part] * sine
            for f in range(freq_local):
                slow = jnp.broadcast_to(gain_ref[f : f + 1, part], (angles, LANES))
                rise = jnp.broadcast_to(scale[f : f + 1, :], (angles, LANES))
                growth = rise * jnp.maximum(along * slow - 1.0, 0.0)
                moved = moved_ref[f, :, part]
                gained = jnp.concatenate(
                    [
                        transfer[j * own + 8 * f : j * own + 8 * f + 8, here]
                        for j in range(angles // 8)
                    ],
                    axis=0,
                )
                out_ref[f, :, part] = wet * (moved + gained + growth * moved)
        result_copy(g).start()
        return carry

    lax.fori_loop(0, groups, one_group, 0)
    for g in range(groups):
        result_copy(g).wait()


HBM = pl.BlockSpec(memory_space=pltpu.HBM)
VMEM = pl.BlockSpec(memory_space=pltpu.VMEM)


def params():
    return pltpu.CompilerParams(vmem_limit_bytes=VMEM_BYTES)


def cost(flops, moved):
    return pl.CostEstimate(flops=int(flops), bytes_accessed=int(moved), transcendentals=0)


def shards(
    spectrum, depths, currents, slopes, wind_speed, wet_mask,
    face_owner, face_block, freq_weights, angle_weights, transfer_rate,
):
    freq_local, angles, points = spectrum.shape
    group_count = lax.axis_size("spec")
    peers = lax.axis_size("blk")
    faces = face_block.shape[0]
    freqs = freq_local * group_count
    groups = points // GROUP
    own = freq_local * 8
    parts = angles // 8
    rows_fd = freq_local * angles
    wide = freqs * 8
    lines = 4 * angles
    edges = groups * EDGE
    capacity = max(2, (faces // 2 + peers - 2) // (peers - 1))
    reply_rows = peers * capacity * TILE
    size = freq_local * angles * points

    owner_row = face_owner.reshape(1, faces)
    block_row = face_block.reshape(1, faces)
    depth_row = depths.reshape(1, points)
    wet_row = wet_mask.reshape(1, points)

    face_scratch = [
        pltpu.VMEM((1, faces), I32),
        pltpu.VMEM((1, faces), I32),
        pltpu.SemaphoreType.DMA((2,)),
    ]
    requests = pl.pallas_call(
        functools.partial(request_kernel, capacity),
        in_specs=[HBM, HBM],
        out_shape=jax.ShapeDtypeStruct((peers, 1, LANES), I32),
        scratch_shapes=face_scratch,
        compiler_params=params(),
        cost_estimate=cost(1e6, 1e5),
        name="requests",
    )(owner_row, block_row)
    asked = lax.all_to_all(requests, "blk", split_axis=0, concat_axis=0, tiled=True)

    moved_first, high, low, early = pl.pallas_call(
        transport_kernel,
        in_specs=[HBM] * 5,
        out_shape=[
            jax.ShapeDtypeStruct((freq_local, angles, points), F32),
            jax.ShapeDtypeStruct((rows_fd, edges), BF16),
            jax.ShapeDtypeStruct((rows_fd, edges), BF16),
            jax.ShapeDtypeStruct((parts, own, groups * HALF), BF16),
        ],
        scratch_shapes=[
            pltpu.VMEM((groups, freq_local, angles, GROUP), F32),
            pltpu.VMEM((1, points), F32),
            pltpu.VMEM((2, points), F32),
            pltpu.VMEM((2, points), F32),
            pltpu.VMEM((1, points), I32),
            pltpu.VMEM((freq_local, angles, 2 * GROUP), F32),
            pltpu.VMEM((freq_local, points), F32),
            pltpu.VMEM((freq_local, points), F32),
            pltpu.VMEM((freq_local, points), F32),
            pltpu.VMEM((2, points), F32),
            pltpu.SemaphoreType.DMA((4 + groups,)),
        ],
        compiler_params=params(),
        cost_estimate=cost(100 * size, 12 * size),
        name="transport",
    )(spectrum, depth_row, currents, slopes, wet_row)

    def exchanged(array):
        return [
            lax.ppermute(
                array, "spec", [(s, (s - step) % group_count) for s in range(group_count)]
            )
            for step in range(1, group_count)
        ]

    early_levels = [early] + exchanged(early)

    reply = pl.pallas_call(
        functools.partial(select_kernel, capacity),
        out_shape=jax.ShapeDtypeStruct((peers, capacity * TILE, rows_fd), BF16),
        compiler_params=params(),
        cost_estimate=cost(2 * reply_rows * edges * rows_fd, 4 * rows_fd * edges),
        name="select",
    )(asked, high)
    replies = lax.all_to_all(reply, "blk", split_axis=0, concat_axis=0, tiled=True)

    weights = pl.pallas_call(
        weights_kernel,
        out_shape=[
            jax.ShapeDtypeStruct((2 * wide, wide), BF16),
            jax.ShapeDtypeStruct((own, 2 * wide), BF16),
            jax.ShapeDtypeStruct((4 * lines, 2 * lines), BF16),
            jax.ShapeDtypeStruct((2 * lines, 2 * lines), BF16),
        ],
        compiler_params=params(),
        cost_estimate=cost(1e9, 1e6),
        name="weights",
    )(freq_weights, angle_weights)

    moved_local, reply_map = pl.pallas_call(
        functools.partial(local_kernel, capacity),
        in_specs=[HBM, HBM, VMEM, VMEM, VMEM],
        out_shape=[
            jax.ShapeDtypeStruct((freq_local, angles, points), F32),
            jax.ShapeDtypeStruct((reply_rows, points), BF16),
        ],
        scratch_shapes=face_scratch,
        input_output_aliases={4: 0},
        compiler_params=params(),
        cost_estimate=cost(4 * rows_fd * edges * points, 10 * size),
        name="local_inflow",
    )(owner_row, block_row, high, low, moved_first)

    moved, late = pl.pallas_call(
        late_kernel,
        out_shape=[
            jax.ShapeDtypeStruct((freq_local, angles, points), F32),
            jax.ShapeDtypeStruct((parts, own, groups * HALF), BF16),
        ],
        input_output_aliases={2: 0},
        compiler_params=params(),
        cost_estimate=cost(2 * rows_fd * reply_rows * points, 10 * size),
        name="late_inflow",
    )(replies, reply_map, moved_local)

    late_levels = [late] + exchanged(late)
    width = groups * HALF
    weight_specs = [VMEM] * 4 + [pl.BlockSpec(memory_space=pltpu.SMEM)]
    tile_scratch = [pltpu.VMEM((parts, 2 * wide, width), BF16)] * 2
    gained_early = pl.pallas_call(
        functools.partial(early_kernel, group_count),
        in_specs=[VMEM] * group_count + weight_specs,
        out_shape=jax.ShapeDtypeStruct((parts, own, width), F32),
        scratch_shapes=tile_scratch,
        compiler_params=params(),
        cost_estimate=cost(3e9, 3 * size),
        name="early_transfer",
    )(*early_levels, *weights, transfer_rate)

    return pl.pallas_call(
        functools.partial(final_kernel, group_count),
        in_specs=[VMEM] * group_count + weight_specs + [VMEM, VMEM, HBM, HBM, HBM],
        out_specs=HBM,
        out_shape=jax.ShapeDtypeStruct((freq_local, angles, points), F32),
        scratch_shapes=tile_scratch
        + [
            pltpu.VMEM((parts, own, width), F32),
            pltpu.VMEM((freq_local, points), F32),
            pltpu.VMEM((1, points), F32),
            pltpu.VMEM((2, points), F32),
            pltpu.VMEM((1, points), I32),
            pltpu.VMEM((freq_local, angles, points), F32),
            pltpu.SemaphoreType.DMA((3 + groups,)),
        ],
        compiler_params=params(),
        cost_estimate=cost(3e9, 12 * size),
        name="late_transfer",
    )(*late_levels, *weights, transfer_rate, gained_early, moved, depth_row, wind_speed, wet_row)


def solution(mesh):
    in_specs = (
        P("spec", None, "blk"),
        P("blk"),
        P(None, "blk"),
        P(None, "blk"),
        P(None, "blk"),
        P("blk"),
        P("blk", None),
        P("blk"),
        P(),
        P(),
        P(),
    )
    out_specs = P("spec", None, "blk")
    return jax.shard_map(shards, mesh=mesh, in_specs=in_specs, out_specs=out_specs, check_vma=False)
```

```python
import functools
import math

import jax
import jax.numpy as jnp
from jax import lax
from jax.experimental import pallas as pl
from jax.experimental.pallas import tpu as pltpu
from jax.sharding import PartitionSpec as P

GRAVITY = 9.81
TIME_STEP = 200.0
CELL_SIZE = 5500.0
LOWEST_FREQ = 0.0418
FREQ_GROWTH = 1.1
WIND_GROWTH = 0.0003
TURN_LIMIT = 0.9

TILE = 8
CELLS = TILE * TILE
GROUP = 256
HALF = 128
EDGE = 128
LANES = 128
VMEM_BYTES = 24 * 1024 * 1024

F32 = jnp.float32
BF16 = jnp.bfloat16
I32 = jnp.int32


def iota(shape, dim):
    return lax.broadcasted_iota(I32, shape, dim)


def onehot(mask):
    return jnp.where(mask, 1.0, 0.0).astype(BF16)


def dot(a, b):
    return jnp.dot(a, b, preferred_element_type=F32)


def dot_nt(a, b):
    return lax.dot_general(a, b, (((1,), (1,)), ((), ())), preferred_element_type=F32)


def dispersion(radian_freq, water_depth):
    deep_kh = radian_freq * radian_freq / GRAVITY * water_depth
    wave_kh = deep_kh / jnp.sqrt(jnp.tanh(deep_kh))
    return wave_kh


def radian_rows(freq_local, width):
    index = iota((freq_local, width), 0) + lax.axis_index("spec") * freq_local
    return (2.0 * math.pi * LOWEST_FREQ) * jnp.exp(index.astype(F32) * math.log(FREQ_GROWTH))


def angle_table(angles, width):
    values = iota((angles, width), 0).astype(F32) * (2.0 * math.pi / angles)
    return jnp.cos(values), jnp.sin(values)


def place_of(point):
    block = point // CELLS
    row = (point // TILE) % TILE
    col = point % TILE
    inner = (row >= 1) & (row <= 6) & (col >= 1) & (col <= 6)
    rank = (row - 1) * 6 + jnp.clip(col - 1, 0, 6)
    early = inner & (rank < 32)
    before = jnp.clip(rank, 0, 32)
    return jnp.where(early, block * 32 + rank, HALF + block * 32 + point % CELLS - before)


def edge_columns(width):
    source = iota((2 * width, EDGE), 0)
    upright = source // width
    point = source % width
    block = point // CELLS
    row = (point // TILE) % TILE
    col = point % TILE
    across = jnp.where(upright == 0, col, row)
    along = jnp.where(upright == 0, row, col)
    edge = upright * 64 + jnp.where(across == 0, 0, 32) + block * TILE + along
    on_edge = (across == 0) | (across == TILE - 1)
    return onehot(on_edge & (edge == iota((2 * width, EDGE), 1)))


def fetch(sources, targets, sems, first=0):
    copies = [
        pltpu.make_async_copy(source, target, sems.at[first + k])
        for k, (source, target) in enumerate(zip(sources, targets))
    ]
    for copy in copies:
        copy.start()
    return copies


def select_kernel(capacity, table_ref, high_ref, reply_ref):
    peers = table_ref.shape[0]
    faces = table_ref.shape[2] // 2
    rows = peers * capacity * TILE
    edges = high_ref.shape[1]
    mine = lax.axis_index("blk").astype(F32)
    table = jnp.concatenate([table_ref[p] for p in range(peers)], axis=0)
    spread = onehot(iota((rows, peers), 0) // (capacity * TILE) == iota((rows, peers), 1))
    table_rows = dot(spread, table.astype(F32).astype(BF16))
    owner_rows = table_rows[:, :faces]
    block_rows = table_rows[:, faces:].astype(I32)
    row = iota((rows, faces), 0)
    face = iota((rows, faces), 1)
    asked = (owner_rows == mine) & ((row // (capacity * TILE)).astype(F32) != mine)
    earlier = onehot(iota((faces, faces), 0) < iota((faces, faces), 1))
    rank = dot(onehot(asked), earlier).astype(I32)
    chosen = asked & (rank == (row // TILE) % capacity)
    side = face % 4
    base = (block_rows // 4) * EDGE + (side // 2) * 64 + (1 - side % 2) * 32 + (block_rows % 4) * TILE
    target = jnp.sum(
        jnp.where(chosen, (base + row % TILE + 1).astype(F32), 0.0), axis=1, keepdims=True
    )
    pick = onehot(iota((rows, edges), 1).astype(F32) + 1.0 == target)
    reply = dot_nt(pick, high_ref[...]).astype(BF16)
    for p in range(peers):
        reply_ref[p] = reply[p * capacity * TILE : (p + 1) * capacity * TILE]


def transport_kernel(
    spec_hbm, depth_hbm, current_hbm, slope_hbm, wet_hbm,
    moved_ref, high_ref, low_ref, early_ref,
    spec_ref, depth_ref, current_ref, slope_ref, wet_ref,
    flux_ref, group_ref, turn_x_ref, turn_y_ref, drift_ref, sems,
):
    freq_local, angles, points = moved_ref.shape
    groups = points // GROUP
    small = fetch(
        [depth_hbm, wet_hbm, current_hbm, slope_hbm], [depth_ref, wet_ref, current_ref, slope_ref], sems
    )
    waves = fetch(
        [spec_hbm.at[:, :, g * GROUP : (g + 1) * GROUP] for g in range(groups)],
        [spec_ref.at[g] for g in range(groups)],
        sems,
        len(small),
    )
    cosine, sine = angle_table(angles, LANES)
    lane = iota((angles, LANES), 1)
    col = lane % TILE
    row = (lane // TILE) % TILE
    west, east = col == 0, col == TILE - 1
    south, north = row == 0, row == TILE - 1
    radian_freq = radian_rows(freq_local, points)
    for copy in small:
        copy.wait()
    depth = depth_ref[...]
    wave_kh = dispersion(radian_freq, depth)
    decay_two = jnp.exp(-2.0 * wave_kh)
    denom = 1.0 - decay_two * decay_two
    ratio = 4.0 * wave_kh * decay_two / denom
    phase = radian_freq * depth / wave_kh
    wet = wet_ref[...].astype(F32) * (TIME_STEP / CELL_SIZE)
    group_ref[...] = 0.5 * (1.0 + ratio) * phase * wet
    turn = 2.0 * radian_freq * decay_two / denom * (TIME_STEP / (2.0 * math.pi / angles))
    turn_x_ref[...] = turn * slope_ref[0:1, :]
    turn_y_ref[...] = turn * slope_ref[1:2, :]
    drift_ref[0:1, :] = current_ref[0:1, :] * wet
    drift_ref[1:2, :] = current_ref[1:2, :] * wet
    columns = edge_columns(GROUP)
    inner = onehot(place_of(iota((GROUP, HALF), 0)) == iota((GROUP, HALF), 1))

    def one_group(g, carry):
        pltpu.make_async_copy(
            spec_hbm.at[:, :, pl.ds(pl.multiple_of(g * GROUP, GROUP), GROUP)],
            spec_ref.at[g],
            sems.at[len(small) + g],
        ).wait()
        for half in range(GROUP // LANES):
            part = pl.ds(pl.multiple_of(g * GROUP + half * LANES, LANES), LANES)
            here = slice(half * LANES, (half + 1) * LANES)
            there = slice(GROUP + half * LANES, GROUP + (half + 1) * LANES)
            drift_x = jnp.broadcast_to(drift_ref[0:1, part], (angles, LANES))
            drift_y = jnp.broadcast_to(drift_ref[1:2, part], (angles, LANES))
            for f in range(freq_local):
                energy = spec_ref[g, f, :, here]
                speed = jnp.broadcast_to(group_ref[f : f + 1, part], (angles, LANES))
                turn_x = jnp.broadcast_to(turn_x_ref[f : f + 1, part], (angles, LANES))
                turn_y = jnp.broadcast_to(turn_y_ref[f : f + 1, part], (angles, LANES))
                flow_x = (speed * cosine + drift_x) * energy
                flow_y = (speed * sine + drift_y) * energy
                turning = jnp.clip(sine * turn_x - cosine * turn_y, -TURN_LIMIT, TURN_LIMIT)
                flow_t = turning * energy
                right = jnp.maximum(flow_x, 0.0)
                left = right - flow_x
                up = jnp.maximum(flow_y, 0.0)
                down = up - flow_y
                ahead = jnp.maximum(flow_t, 0.0)
                back = ahead - flow_t
                total = energy - (right + left) - (up + down) - (ahead + back)
                total = total + pltpu.roll(jnp.where(east, 0.0, right), 1, 1)
                total = total + pltpu.roll(jnp.where(west, 0.0, left), LANES - 1, 1)
                total = total + pltpu.roll(jnp.where(north, 0.0, up), TILE, 1)
                total = total + pltpu.roll(jnp.where(south, 0.0, down), LANES - TILE, 1)
                total = total + pltpu.roll(ahead, 1, 0) + pltpu.roll(back, angles - 1, 0)
                moved_ref[f, :, part] = total
                flux_ref[f, :, here] = jnp.where(east, right, left)
                flux_ref[f, :, there] = jnp.where(north, up, down)
        flux = flux_ref[...].reshape(freq_local * angles, 2 * GROUP)
        high = flux.astype(BF16)
        low = (flux - high.astype(F32)).astype(BF16)
        place = pl.ds(pl.multiple_of(g * EDGE, EDGE), EDGE)
        high_ref[:, place] = dot(high, columns).astype(BF16)
        low_ref[:, place] = dot(low, columns).astype(BF16)
        part = pl.ds(pl.multiple_of(g * GROUP, GROUP), GROUP)
        for j in range(angles // 8):
            levels = moved_ref[:, 8 * j : 8 * j + 8, part].reshape(freq_local * 8, GROUP).astype(BF16)
            early_ref[j, :, place] = dot(levels, inner).astype(BF16)
        return carry

    lax.fori_loop(0, groups, one_group, 0)


def local_kernel(
    capacity, owner_hbm, block_hbm, high_ref, low_ref, moved_in_ref, *refs
):
    *moved_refs, map_ref, owner_ref, block_ref, sems = refs
    copies = fetch([owner_hbm, block_hbm], [owner_ref, block_ref], sems)
    for copy in copies:
        copy.wait()
    freq_local, angles, points = moved_in_ref.shape
    each = moved_refs[0].shape[2] // GROUP
    ranks = face_ranks(owner_ref, block_ref)
    for g in range(points // GROUP):
        part = slice(g * GROUP, (g + 1) * GROUP)
        pick, reply_map = inflow_maps(
            capacity, g, ranks, high_ref.shape[1], map_ref.shape[0]
        )
        map_ref[:, part] = reply_map
        inflow = dot(high_ref[...], pick) + dot(low_ref[...], pick)
        here = slice(g % each * GROUP, (g % each + 1) * GROUP)
        moved_refs[g // each][:, :, here] = moved_in_ref[:, :, part] + inflow.reshape(
            freq_local, angles, GROUP
        )


def face_ranks(owner_ref, block_ref):
    faces = owner_ref.shape[1]
    owner = owner_ref[...]
    by_column = jnp.broadcast_to(owner, (faces, faces))
    below = iota((faces, faces), 0)
    right = iota((faces, faces), 1)
    by_row = jnp.sum(jnp.where(below == right, by_column, 0).astype(F32), axis=1, keepdims=True)
    equal = (by_row == by_column.astype(F32)) & (below < right)
    rank = jnp.sum(jnp.where(equal, 1.0, 0.0), axis=0, keepdims=True)
    return jnp.concatenate(
        [block_ref[...].astype(F32), owner.astype(F32), rank, jnp.zeros((5, faces), F32)], axis=0
    ).astype(BF16)


def inflow_maps(capacity, group, table, edges, rows):
    faces = table.shape[1]
    width = GROUP
    mine = lax.axis_index("blk")
    point = iota((faces, width), 1)
    block = point // CELLS + group * (width // CELLS)
    col = point % TILE
    row = (point // TILE) % TILE
    face = iota((faces, width), 0)
    at_x = dot(table, onehot((face == block * 4 + jnp.where(col == 0, 0, 1)))).astype(I32)
    at_y = dot(table, onehot((face == block * 4 + jnp.where(row == 0, 2, 3)))).astype(I32)
    point = iota((1, width), 1)
    col = point % TILE
    row = (point // TILE) % TILE

    def ids(found, across, along, upright):
        edge = (across == 0) | (across == TILE - 1)
        from_block, from_owner, slot = found[0:1], found[1:2], found[2:3]
        local = edge & (from_owner == mine)
        remote = edge & (from_owner != mine)
        base = upright * 64 + jnp.where(across == 0, 32, 0)
        source = (from_block // 4) * EDGE + base + (from_block % 4) * TILE + along
        reply = (from_owner * capacity + slot) * TILE + along
        return jnp.where(local, source, -1), jnp.where(remote, reply, -1)

    source_x, reply_x = ids(at_x, col, row, 0)
    source_y, reply_y = ids(at_y, row, col, 1)
    line = iota((rows, width), 0)
    reply_map = onehot((line == reply_x) | (line == reply_y))
    line = iota((edges, width), 0)
    return onehot((line == source_x) | (line == source_y)), reply_map


def weights_kernel(freq_ref, angle_ref, shift_ref, spread_ref, image_ref, back_ref):
    freqs = freq_ref.shape[1]
    angles = angle_ref.shape[2]
    wide = freqs * 8
    own = spread_ref.shape[0]
    start = lax.axis_index("spec") * (own // 8)
    rows = onehot((iota((wide, freqs), 0) // 8 + start) % freqs == iota((wide, freqs), 1))
    same = iota((wide, wide), 0) % 8 == iota((wide, wide), 1) % 8
    for s in range(2):
        weights = freq_ref[s]
        left = dot(rows, weights).astype(BF16)
        shift_ref[s * wide : (s + 1) * wide, :] = jnp.where(same, dot_nt(left, rows), 0.0).astype(BF16)
        turned = dot_nt(rows[:own], weights).astype(BF16)
        spread_ref[:, s * wide : (s + 1) * wide] = jnp.where(
            same[:own], dot_nt(turned, rows), 0.0
        ).astype(BF16)
    stacked = jnp.concatenate(
        [angle_ref[m, s].astype(F32) for m in range(2) for s in range(2)], axis=0
    ).astype(BF16)
    lines = angles * 4
    r = iota((4 * lines, 4 * angles), 0)
    c = iota((4 * lines, 4 * angles), 1)
    direction = (r // 32) % (angles // 8) * 8 + r % 8
    chosen = onehot((r // lines) * angles + direction == c)
    lines_rows = dot(chosen, stacked).astype(BF16)
    r = iota((2 * lines, angles), 0)
    column = onehot((r // 32) % (angles // 8) * 8 + r % 8 == iota((2 * lines, angles), 1))
    r = iota((4 * lines, 2 * lines), 0)
    c = iota((4 * lines, 2 * lines), 1)
    keep = ((r // lines) % 2 == c // lines) & ((r // 8) % 4 == (c // 8) % 4)
    image_ref[...] = jnp.where(keep, dot_nt(lines_rows, column), 0.0).astype(BF16)
    for s in range(2):
        r = iota((2 * lines, 4 * angles), 0)
        c = iota((2 * lines, 4 * angles), 1)
        direction = (r // 32) % (angles // 8) * 8 + r % 8
        chosen = onehot(((r // lines) * 2 + s) * angles + direction == c)
        lines_rows = dot(chosen, stacked).astype(BF16)
        r = iota((lines, 2 * lines), 0)
        c = iota((lines, 2 * lines), 1)
        keep = (r // 8) % 4 == (c // 8) % 4
        back_ref[s * lines : (s + 1) * lines, :] = jnp.where(
            keep, dot_nt(column[:lines], lines_rows), 0.0
        ).astype(BF16)


def turned_late_kernel(first, reply_ref, map_ref, moved_in_ref, moved_ref, late_ref, turned_ref):
    freq_local, angles, points = moved_ref.shape
    reply = reply_ref[...].astype(F32).reshape(map_ref.shape[0], freq_local * angles)
    turned_ref[...] = reply.T.astype(BF16)
    late_kernel(first, turned_ref, map_ref, moved_in_ref, moved_ref, late_ref)


def late_kernel(first, turned_ref, map_ref, moved_in_ref, moved_ref, late_ref):
    freq_local, angles, points = moved_ref.shape
    outer = onehot(place_of(iota((GROUP, HALF), 0)) == iota((GROUP, HALF), 1) + HALF)
    for k in range(points // GROUP):
        here = slice(k * GROUP, (k + 1) * GROUP)
        inflow = dot(turned_ref[...], map_ref[:, (first + k) * GROUP : (first + k + 1) * GROUP])
        moved_ref[:, :, here] = moved_in_ref[:, :, here] + inflow.reshape(freq_local, angles, GROUP)
        for j in range(angles // 8):
            levels = moved_ref[:, 8 * j : 8 * j + 8, here].reshape(freq_local * 8, GROUP)
            late_ref[j, :, k * HALF : (k + 1) * HALF] = dot(levels.astype(BF16), outer).astype(BF16)


def nonlinear_tile(level_refs, shift_ref, spread_ref, image_ref, back_ref, rate_ref, shifted_ref, gained_ref):
    parts, own, width = level_refs[0].shape
    wide = shift_ref.shape[1]
    freqs = wide // 8
    lines = parts * 32
    start = lax.axis_index("spec") * (own // 8)
    for j in range(parts):
        levels = jnp.concatenate([ref[j] for ref in level_refs], axis=0)
        shifted_ref[j] = dot(shift_ref[...], levels).astype(BF16)
    def image_of(q):
        shifted = jnp.concatenate(
            [
                shifted_ref[j, s * wide + 32 * q : s * wide + 32 * q + 32, :]
                for s in range(2)
                for j in range(parts)
            ],
            axis=0,
        )
        return dot(image_ref[...], shifted)

    doubled = []
    coming = image_of(0)
    for q in range(freqs // 4):
        source, place = divmod(q * 32, own)
        images = coming
        if q + 1 < freqs // 4:
            coming = image_of(q + 1)
        level = jnp.concatenate(
            [level_refs[source][j, place : place + 32, :].astype(F32) for j in range(parts)], axis=0
        )
        rates = [rate_ref[(start + 4 * q + k) % freqs] for k in range(4)]
        scaled = jnp.concatenate(
            [
                level[32 * j + 8 * k : 32 * j + 8 * k + 8] * rates[k]
                for j in range(parts)
                for k in range(4)
            ],
            axis=0,
        )
        deltas = []
        for m in range(2):
            plus = images[2 * m * lines : (2 * m + 1) * lines]
            minus = images[(2 * m + 1) * lines : (2 * m + 2) * lines]
            deltas.append(scaled * (level * (plus + minus) - 2.0 * plus * minus))
        low = jnp.concatenate(deltas, axis=0).astype(BF16)
        back = dot(back_ref[...], low).astype(BF16)
        for s in range(2):
            for j in range(parts):
                gained_ref[j, s * wide + 32 * q : s * wide + 32 * q + 32, :] = back[
                    (s * parts + j) * 32 : (s * parts + j) * 32 + 32
                ]
        if source == 0:
            doubled.append(deltas[0] + deltas[1])
    result = []
    for j in range(parts):
        lost = jnp.concatenate([d[32 * j : 32 * j + 32] for d in doubled], axis=0)
        result.append(dot(spread_ref[...], gained_ref[j]) - 2.0 * lost)
    return result


def early_kernel(sources, *refs):
    levels = refs[:sources]
    shift_ref, spread_ref, image_ref, back_ref, rate_ref, out_ref, shifted_ref, gained_ref = refs[sources:]
    result = nonlinear_tile(
        levels, shift_ref, spread_ref, image_ref, back_ref, rate_ref, shifted_ref, gained_ref
    )
    for j, values in enumerate(result):
        out_ref[j] = values


def final_kernel(sources, first, *refs):
    levels = refs[:sources]
    shift_ref, spread_ref, image_ref, back_ref, rate_ref = refs[sources : sources + 5]
    early_ref, moved_ref, depth_hbm, wind_hbm, wet_hbm = refs[sources + 5 : sources + 10]
    out_hbm, shifted_ref, gained_ref, late_ref, gain_ref, depth_ref, wind_ref, wet_ref, out_ref, sems = (
        refs[-10:]
    )
    small = fetch([depth_hbm, wind_hbm, wet_hbm], [depth_ref, wind_ref, wet_ref], sems)
    late = nonlinear_tile(
        levels, shift_ref, spread_ref, image_ref, back_ref, rate_ref, shifted_ref, gained_ref
    )
    for j, values in enumerate(late):
        late_ref[j] = values
    freq_local, angles, _ = moved_ref.shape
    points = depth_ref.shape[1]
    groups = late_ref.shape[2] // HALF
    own = freq_local * 8
    for copy in small:
        copy.wait()
    radian_freq = radian_rows(freq_local, points)
    wave_kh = dispersion(radian_freq, depth_ref[...])
    gain_ref[...] = wave_kh / (radian_freq * depth_ref[...])
    scale = radian_freq[:, 0:LANES] * (TIME_STEP * WIND_GROWTH)
    cosine, sine = angle_table(angles, LANES)
    restore = onehot(iota((GROUP, GROUP), 0) == place_of(iota((GROUP, GROUP), 1)))

    def result_copy(k):
        part = pl.ds(pl.multiple_of((first + k) * GROUP, GROUP), GROUP)
        here = pl.ds(pl.multiple_of(k * GROUP, GROUP), GROUP)
        return pltpu.make_async_copy(
            out_ref.at[:, :, here], out_hbm.at[:, :, part], sems.at[len(small) + k]
        )

    def one_group(k, carry):
        early_lanes = pl.ds(pl.multiple_of((first + k) * HALF, HALF), HALF)
        late_lanes = pl.ds(pl.multiple_of(k * HALF, HALF), HALF)
        mixed = jnp.concatenate(
            [
                jnp.concatenate([early_ref[j, :, early_lanes], late_ref[j, :, late_lanes]], axis=1)
                for j in range(angles // 8)
            ],
            axis=0,
        )
        high = mixed.astype(BF16)
        low = (mixed - high.astype(F32)).astype(BF16)
        transfer = dot(high, restore) + dot(low, restore)
        for half in range(GROUP // LANES):
            part = pl.ds(pl.multiple_of((first + k) * GROUP + half * LANES, LANES), LANES)
            place = pl.ds(pl.multiple_of(k * GROUP + half * LANES, LANES), LANES)
            here = slice(half * LANES, (half + 1) * LANES)
            wet = jnp.broadcast_to(wet_ref[:, part].astype(F32), (angles, LANES))
            along = wind_ref[0:1, part] * cosine + wind_ref[1:2, part] * sine
            for f in range(freq_local):
                slow = jnp.broadcast_to(gain_ref[f : f + 1, part], (angles, LANES))
                rise = jnp.broadcast_to(scale[f : f + 1, :], (angles, LANES))
                growth = rise * jnp.maximum(along * slow - 1.0, 0.0)
                moved = moved_ref[f, :, place]
                gained = jnp.concatenate(
                    [
                        transfer[j * own + 8 * f : j * own + 8 * f + 8, here]
                        for j in range(angles // 8)
                    ],
                    axis=0,
                )
                out_ref[f, :, place] = wet * (moved + gained + growth * moved)
        result_copy(k).start()
        return carry

    lax.fori_loop(0, groups, one_group, 0)
    for k in range(groups):
        result_copy(k).wait()


HBM = pl.BlockSpec(memory_space=pltpu.HBM)
VMEM = pl.BlockSpec(memory_space=pltpu.VMEM)


def params():
    return pltpu.CompilerParams(vmem_limit_bytes=VMEM_BYTES)


def cost(flops, moved):
    return pl.CostEstimate(flops=int(flops), bytes_accessed=int(moved), transcendentals=0)


def shards(
    spectrum, depths, currents, slopes, wind_speed, wet_mask,
    face_owner, face_block, freq_weights, angle_weights, transfer_rate,
):
    freq_local, angles, points = spectrum.shape
    group_count = lax.axis_size("spec")
    peers = lax.axis_size("blk")
    faces = face_block.shape[0]
    freqs = freq_local * group_count
    groups = points // GROUP
    own = freq_local * 8
    parts = angles // 8
    rows_fd = freq_local * angles
    wide = freqs * 8
    lines = 4 * angles
    edges = groups * EDGE
    capacity = max(2, (faces // 2 + peers - 2) // (peers - 1))
    reply_rows = peers * capacity * TILE
    size = freq_local * angles * points

    owner_row = face_owner.reshape(1, faces)
    block_row = face_block.reshape(1, faces)
    depth_row = depths.reshape(1, points)
    wet_row = wet_mask.reshape(1, points)

    table = lax.all_gather(
        jnp.concatenate([owner_row, block_row], axis=1), "blk", axis=0, tiled=True
    ).reshape(peers, 1, 2 * faces)

    moved_first, high, low, early = pl.pallas_call(
        transport_kernel,
        in_specs=[HBM] * 5,
        out_shape=[
            jax.ShapeDtypeStruct((freq_local, angles, points), F32),
            jax.ShapeDtypeStruct((rows_fd, edges), BF16),
            jax.ShapeDtypeStruct((rows_fd, edges), BF16),
            jax.ShapeDtypeStruct((parts, own, groups * HALF), BF16),
        ],
        scratch_shapes=[
            pltpu.VMEM((groups, freq_local, angles, GROUP), F32),
            pltpu.VMEM((1, points), F32),
            pltpu.VMEM((2, points), F32),
            pltpu.VMEM((2, points), F32),
            pltpu.VMEM((1, points), I32),
            pltpu.VMEM((freq_local, angles, 2 * GROUP), F32),
            pltpu.VMEM((freq_local, points), F32),
            pltpu.VMEM((freq_local, points), F32),
            pltpu.VMEM((freq_local, points), F32),
            pltpu.VMEM((2, points), F32),
            pltpu.SemaphoreType.DMA((4 + groups,)),
        ],
        compiler_params=params(),
        cost_estimate=cost(100 * size, 12 * size),
        name="transport",
    )(spectrum, depth_row, currents, slopes, wet_row)

    def exchanged(array):
        return [
            lax.ppermute(
                array, "spec", [(s, (s - step) % group_count) for s in range(group_count)]
            )
            for step in range(1, group_count)
        ]

    early_levels = [early] + exchanged(early)

    reply = pl.pallas_call(
        functools.partial(select_kernel, capacity),
        out_shape=jax.ShapeDtypeStruct((peers, capacity * TILE, rows_fd), BF16),
        compiler_params=params(),
        cost_estimate=cost(2 * reply_rows * edges * rows_fd, 4 * rows_fd * edges),
        name="select",
    )(table, high)
    replies = lax.all_to_all(reply, "blk", split_axis=0, concat_axis=0, tiled=True)

    weights = pl.pallas_call(
        weights_kernel,
        out_shape=[
            jax.ShapeDtypeStruct((2 * wide, wide), BF16),
            jax.ShapeDtypeStruct((own, 2 * wide), BF16),
            jax.ShapeDtypeStruct((4 * lines, 2 * lines), BF16),
            jax.ShapeDtypeStruct((2 * lines, 2 * lines), BF16),
        ],
        compiler_params=params(),
        cost_estimate=cost(1e9, 1e6),
        name="weights",
    )(freq_weights, angle_weights)

    halves = 2
    half_groups = groups // halves
    tile = half_groups * HALF
    half_wave = jax.ShapeDtypeStruct((freq_local, angles, points // halves), F32)
    *moved_local, reply_map = pl.pallas_call(
        functools.partial(local_kernel, capacity),
        in_specs=[HBM, HBM, VMEM, VMEM, VMEM],
        out_shape=[half_wave] * halves + [jax.ShapeDtypeStruct((reply_rows, points), BF16)],
        scratch_shapes=[
            pltpu.VMEM((1, faces), I32),
            pltpu.VMEM((1, faces), I32),
            pltpu.SemaphoreType.DMA((2,)),
        ],
        compiler_params=params(),
        cost_estimate=cost(4 * rows_fd * edges * points, 10 * size),
        name="local_inflow",
    )(owner_row, block_row, high, low, moved_first)

    moved, turned, late_levels = [], None, []
    for h in range(halves):
        out = pl.pallas_call(
            functools.partial(late_kernel if h else turned_late_kernel, h * half_groups),
            out_shape=[half_wave, jax.ShapeDtypeStruct((parts, own, tile), BF16)]
            + [jax.ShapeDtypeStruct((rows_fd, reply_rows), BF16)] * (h == 0),
            input_output_aliases={2: 0},
            compiler_params=params(),
            cost_estimate=cost(rows_fd * reply_rows * points, 5 * size),
            name=f"late_inflow_{h}",
        )(turned if h else replies, reply_map, moved_local[h])
        moved.append(out[0])
        turned = turned if h else out[2]
        late_levels.append([out[1]] + exchanged(out[1]))

    width = groups * HALF
    weight_specs = [VMEM] * 4 + [pl.BlockSpec(memory_space=pltpu.SMEM)]
    tile_scratch = [pltpu.VMEM((parts, 2 * wide, width), BF16)] * 2
    gained_early = pl.pallas_call(
        functools.partial(early_kernel, group_count),
        in_specs=[VMEM] * group_count + weight_specs,
        out_shape=jax.ShapeDtypeStruct((parts, own, width), F32),
        scratch_shapes=tile_scratch,
        compiler_params=params(),
        cost_estimate=cost(3e9, 3 * size),
        name="early_transfer",
    )(*early_levels, *weights, transfer_rate)

    result = []
    for h in range(halves):
        operands = [
            *late_levels[h], *weights, transfer_rate, gained_early, moved[h],
            depth_row, wind_speed, wet_row, *result,
        ]
        result = [
            pl.pallas_call(
                functools.partial(final_kernel, group_count, h * half_groups),
                in_specs=[VMEM] * group_count
                + weight_specs
                + [VMEM, VMEM, HBM, HBM, HBM]
                + [HBM] * len(result),
                out_specs=HBM,
                out_shape=jax.ShapeDtypeStruct((freq_local, angles, points), F32),
                scratch_shapes=[pltpu.VMEM((parts, 2 * wide, tile), BF16)] * 2
                + [
                    pltpu.VMEM((parts, own, tile), F32),
                    pltpu.VMEM((freq_local, points), F32),
                    pltpu.VMEM((1, points), F32),
                    pltpu.VMEM((2, points), F32),
                    pltpu.VMEM((1, points), I32),
                    pltpu.VMEM((freq_local, angles, half_groups * GROUP), F32),
                    pltpu.SemaphoreType.DMA((3 + half_groups,)),
                ],
                input_output_aliases={len(operands) - 1: 0} if result else {},
                compiler_params=params(),
                cost_estimate=cost(2e9, 6 * size),
                name=f"late_transfer_{h}",
            )(*operands)
        ]
    return result[0]


def solution(mesh):
    in_specs = (
        P("spec", None, "blk"),
        P("blk"),
        P(None, "blk"),
        P(None, "blk"),
        P(None, "blk"),
        P("blk"),
        P("blk", None),
        P("blk"),
        P(),
        P(),
        P(),
    )
    out_specs = P("spec", None, "blk")
    return jax.shard_map(shards, mesh=mesh, in_specs=in_specs, out_specs=out_specs, check_vma=False)
```

```python
import functools
import math

import jax
import jax.numpy as jnp
from jax import lax
from jax.experimental import pallas as pl
from jax.experimental.pallas import tpu as pltpu
from jax.sharding import PartitionSpec as P

GRAVITY = 9.81
TIME_STEP = 200.0
CELL_SIZE = 5500.0
LOWEST_FREQ = 0.0418
FREQ_GROWTH = 1.1
WIND_GROWTH = 0.0003
TURN_LIMIT = 0.9

TILE = 8
CELLS = TILE * TILE
GROUP = 256
HALF = 128
EDGE = 128
LANES = 128
VMEM_BYTES = 24 * 1024 * 1024

F32 = jnp.float32
BF16 = jnp.bfloat16
I32 = jnp.int32


def iota(shape, dim):
    return lax.broadcasted_iota(I32, shape, dim)


def onehot(mask):
    return jnp.where(mask, 1.0, 0.0).astype(BF16)


def dot(a, b):
    return jnp.dot(a, b, preferred_element_type=F32)


def dot_nt(a, b):
    return lax.dot_general(a, b, (((1,), (1,)), ((), ())), preferred_element_type=F32)


def dispersion(radian_freq, water_depth):
    deep_kh = radian_freq * radian_freq / GRAVITY * water_depth
    wave_kh = deep_kh / jnp.sqrt(jnp.tanh(deep_kh))
    return wave_kh


def radian_rows(freq_local, width):
    index = iota((freq_local, width), 0) + lax.axis_index("spec") * freq_local
    return (2.0 * math.pi * LOWEST_FREQ) * jnp.exp(index.astype(F32) * math.log(FREQ_GROWTH))


def angle_table(angles, width):
    values = iota((angles, width), 0).astype(F32) * (2.0 * math.pi / angles)
    return jnp.cos(values), jnp.sin(values)


def place_of(point):
    block = point // CELLS
    row = (point // TILE) % TILE
    col = point % TILE
    inner = (row >= 1) & (row <= 6) & (col >= 1) & (col <= 6)
    rank = (row - 1) * 6 + jnp.clip(col - 1, 0, 6)
    early = inner & (rank < 32)
    before = jnp.clip(rank, 0, 32)
    return jnp.where(early, block * 32 + rank, HALF + block * 32 + point % CELLS - before)


def edge_columns(width):
    source = iota((2 * width, EDGE), 0)
    upright = source // width
    point = source % width
    block = point // CELLS
    row = (point // TILE) % TILE
    col = point % TILE
    across = jnp.where(upright == 0, col, row)
    along = jnp.where(upright == 0, row, col)
    edge = upright * 64 + jnp.where(across == 0, 0, 32) + block * TILE + along
    on_edge = (across == 0) | (across == TILE - 1)
    return onehot(on_edge & (edge == iota((2 * width, EDGE), 1)))


def fetch(sources, targets, sems, first=0):
    copies = [
        pltpu.make_async_copy(source, target, sems.at[first + k])
        for k, (source, target) in enumerate(zip(sources, targets))
    ]
    for copy in copies:
        copy.start()
    return copies


def request_kernel(capacity, owner_hbm, block_hbm, request_ref, owner_ref, block_ref, sems):
    copies = fetch([owner_hbm, block_hbm], [owner_ref, block_ref], sems)
    peers = request_ref.shape[0]
    faces = owner_ref.shape[1]
    mine = lax.axis_index("blk")
    for copy in copies:
        copy.wait()
    peer = iota((peers, faces), 0)
    asked = (owner_ref[...] == peer) & (peer != mine)
    earlier = onehot(iota((faces, faces), 0) < iota((faces, faces), 1))
    rank = dot(onehot(asked), earlier).astype(I32)
    side = iota((1, faces), 1) % 4
    block = block_ref[...]
    base = (block // 4) * EDGE + (side // 2) * 64 + (1 - side % 2) * 32 + (block % 4) * TILE + 1
    base = base.astype(F32)
    lane = iota((peers, LANES), 1)
    result = jnp.zeros((peers, LANES), F32)
    for k in range(capacity):
        found = jnp.sum(jnp.where(asked & (rank == k), base, 0.0), axis=1, keepdims=True)
        result = jnp.where(lane == k, found, result)
    result = result.astype(I32)
    for p in range(peers):
        request_ref[p] = result[p : p + 1]


def select_kernel(capacity, request_ref, high_ref, reply_ref):
    peers = request_ref.shape[0]
    rows = peers * capacity * TILE
    edges = high_ref.shape[1]
    asked = jnp.concatenate([request_ref[p] for p in range(peers)], axis=0)
    coarse = (asked // 16).astype(F32).astype(BF16)
    fine = (asked % 16).astype(F32).astype(BF16)
    spread = onehot(iota((rows, peers), 0) // (capacity * TILE) == iota((rows, peers), 1))
    asked = 16.0 * dot(spread, coarse) + dot(spread, fine)
    row = iota((rows, LANES), 0)
    slot = (row // TILE) % capacity
    chosen = (slot == iota((rows, LANES), 1)) & (asked > 0.0)
    target = jnp.sum(
        jnp.where(chosen, asked + (row % TILE).astype(F32), 0.0), axis=1, keepdims=True
    )
    pick = onehot(iota((rows, edges), 1).astype(F32) + 1.0 == target)
    reply = dot_nt(pick, high_ref[...]).astype(BF16)
    for p in range(peers):
        reply_ref[p] = reply[p * capacity * TILE : (p + 1) * capacity * TILE]


def transport_kernel(
    spec_hbm, depth_hbm, current_hbm, slope_hbm, wet_hbm,
    moved_ref, high_ref, low_ref, early_ref,
    spec_ref, depth_ref, current_ref, slope_ref, wet_ref,
    flux_ref, group_ref, turn_x_ref, turn_y_ref, drift_ref, sems,
):
    freq_local, angles, points = moved_ref.shape
    groups = points // GROUP
    small = fetch(
        [depth_hbm, wet_hbm, current_hbm, slope_hbm], [depth_ref, wet_ref, current_ref, slope_ref], sems
    )
    waves = fetch(
        [spec_hbm.at[:, :, g * GROUP : (g + 1) * GROUP] for g in range(groups)],
        [spec_ref.at[g] for g in range(groups)],
        sems,
        len(small),
    )
    cosine, sine = angle_table(angles, LANES)
    lane = iota((angles, LANES), 1)
    col = lane % TILE
    row = (lane // TILE) % TILE
    west, east = col == 0, col == TILE - 1
    south, north = row == 0, row == TILE - 1
    radian_freq = radian_rows(freq_local, points)
    for copy in small:
        copy.wait()
    depth = depth_ref[...]
    wave_kh = dispersion(radian_freq, depth)
    decay_two = jnp.exp(-2.0 * wave_kh)
    denom = 1.0 - decay_two * decay_two
    ratio = 4.0 * wave_kh * decay_two / denom
    phase = radian_freq * depth / wave_kh
    wet = wet_ref[...].astype(F32) * (TIME_STEP / CELL_SIZE)
    group_ref[...] = 0.5 * (1.0 + ratio) * phase * wet
    turn = 2.0 * radian_freq * decay_two / denom * (TIME_STEP / (2.0 * math.pi / angles))
    turn_x_ref[...] = turn * slope_ref[0:1, :]
    turn_y_ref[...] = turn * slope_ref[1:2, :]
    drift_ref[0:1, :] = current_ref[0:1, :] * wet
    drift_ref[1:2, :] = current_ref[1:2, :] * wet
    columns = edge_columns(GROUP)
    inner = onehot(place_of(iota((GROUP, HALF), 0)) == iota((GROUP, HALF), 1))

    def one_group(g, carry):
        pltpu.make_async_copy(
            spec_hbm.at[:, :, pl.ds(pl.multiple_of(g * GROUP, GROUP), GROUP)],
            spec_ref.at[g],
            sems.at[len(small) + g],
        ).wait()
        for half in range(GROUP // LANES):
            part = pl.ds(pl.multiple_of(g * GROUP + half * LANES, LANES), LANES)
            here = slice(half * LANES, (half + 1) * LANES)
            there = slice(GROUP + half * LANES, GROUP + (half + 1) * LANES)
            drift_x = jnp.broadcast_to(drift_ref[0:1, part], (angles, LANES))
            drift_y = jnp.broadcast_to(drift_ref[1:2, part], (angles, LANES))
            for f in range(freq_local):
                energy = spec_ref[g, f, :, here]
                speed = jnp.broadcast_to(group_ref[f : f + 1, part], (angles, LANES))
                turn_x = jnp.broadcast_to(turn_x_ref[f : f + 1, part], (angles, LANES))
                turn_y = jnp.broadcast_to(turn_y_ref[f : f + 1, part], (angles, LANES))
                flow_x = (speed * cosine + drift_x) * energy
                flow_y = (speed * sine + drift_y) * energy
                turning = jnp.clip(sine * turn_x - cosine * turn_y, -TURN_LIMIT, TURN_LIMIT)
                flow_t = turning * energy
                right = jnp.maximum(flow_x, 0.0)
                left = right - flow_x
                up = jnp.maximum(flow_y, 0.0)
                down = up - flow_y
                ahead = jnp.maximum(flow_t, 0.0)
                back = ahead - flow_t
                total = energy - (right + left) - (up + down) - (ahead + back)
                total = total + pltpu.roll(jnp.where(east, 0.0, right), 1, 1)
                total = total + pltpu.roll(jnp.where(west, 0.0, left), LANES - 1, 1)
                total = total + pltpu.roll(jnp.where(north, 0.0, up), TILE, 1)
                total = total + pltpu.roll(jnp.where(south, 0.0, down), LANES - TILE, 1)
                total = total + pltpu.roll(ahead, 1, 0) + pltpu.roll(back, angles - 1, 0)
                moved_ref[f, :, part] = total
                flux_ref[f, :, here] = jnp.where(east, right, left)
                flux_ref[f, :, there] = jnp.where(north, up, down)
        flux = flux_ref[...].reshape(freq_local * angles, 2 * GROUP)
        high = flux.astype(BF16)
        low = (flux - high.astype(F32)).astype(BF16)
        place = pl.ds(pl.multiple_of(g * EDGE, EDGE), EDGE)
        high_ref[:, place] = dot(high, columns).astype(BF16)
        low_ref[:, place] = dot(low, columns).astype(BF16)
        part = pl.ds(pl.multiple_of(g * GROUP, GROUP), GROUP)
        for j in range(angles // 8):
            levels = moved_ref[:, 8 * j : 8 * j + 8, part].reshape(freq_local * 8, GROUP).astype(BF16)
            early_ref[j, :, place] = dot(levels, inner).astype(BF16)
        return carry

    lax.fori_loop(0, groups, one_group, 0)


def local_kernel(
    capacity, owner_hbm, block_hbm, high_ref, low_ref, moved_in_ref, *refs
):
    *moved_refs, map_ref, owner_ref, block_ref, sems = refs
    copies = fetch([owner_hbm, block_hbm], [owner_ref, block_ref], sems)
    for copy in copies:
        copy.wait()
    freq_local, angles, points = moved_in_ref.shape
    each = moved_refs[0].shape[2] // GROUP
    ranks = face_ranks(owner_ref, block_ref)
    for g in range(points // GROUP):
        part = slice(g * GROUP, (g + 1) * GROUP)
        pick, reply_map = inflow_maps(
            capacity, g, ranks, high_ref.shape[1], map_ref.shape[0]
        )
        map_ref[:, part] = reply_map
        inflow = dot(high_ref[...], pick) + dot(low_ref[...], pick)
        here = slice(g % each * GROUP, (g % each + 1) * GROUP)
        moved_refs[g // each][:, :, here] = moved_in_ref[:, :, part] + inflow.reshape(
            freq_local, angles, GROUP
        )


def face_ranks(owner_ref, block_ref):
    faces = owner_ref.shape[1]
    owner = owner_ref[...]
    by_column = jnp.broadcast_to(owner, (faces, faces))
    below = iota((faces, faces), 0)
    right = iota((faces, faces), 1)
    by_row = jnp.sum(jnp.where(below == right, by_column, 0).astype(F32), axis=1, keepdims=True)
    equal = (by_row == by_column.astype(F32)) & (below < right)
    rank = jnp.sum(jnp.where(equal, 1.0, 0.0), axis=0, keepdims=True)
    return jnp.concatenate(
        [block_ref[...].astype(F32), owner.astype(F32), rank, jnp.zeros((5, faces), F32)], axis=0
    ).astype(BF16)


def inflow_maps(capacity, group, table, edges, rows):
    faces = table.shape[1]
    width = GROUP
    mine = lax.axis_index("blk")
    point = iota((faces, width), 1)
    block = point // CELLS + group * (width // CELLS)
    col = point % TILE
    row = (point // TILE) % TILE
    face = iota((faces, width), 0)
    at_x = dot(table, onehot((face == block * 4 + jnp.where(col == 0, 0, 1)))).astype(I32)
    at_y = dot(table, onehot((face == block * 4 + jnp.where(row == 0, 2, 3)))).astype(I32)
    point = iota((1, width), 1)
    col = point % TILE
    row = (point // TILE) % TILE

    def ids(found, across, along, upright):
        edge = (across == 0) | (across == TILE - 1)
        from_block, from_owner, slot = found[0:1], found[1:2], found[2:3]
        local = edge & (from_owner == mine)
        remote = edge & (from_owner != mine)
        base = upright * 64 + jnp.where(across == 0, 32, 0)
        source = (from_block // 4) * EDGE + base + (from_block % 4) * TILE + along
        reply = (from_owner * capacity + slot) * TILE + along
        return jnp.where(local, source, -1), jnp.where(remote, reply, -1)

    source_x, reply_x = ids(at_x, col, row, 0)
    source_y, reply_y = ids(at_y, row, col, 1)
    line = iota((rows, width), 0)
    reply_map = onehot((line == reply_x) | (line == reply_y))
    line = iota((edges, width), 0)
    return onehot((line == source_x) | (line == source_y)), reply_map


def weights_kernel(freq_ref, angle_ref, shift_ref, spread_ref, image_ref, back_ref):
    freqs = freq_ref.shape[1]
    angles = angle_ref.shape[2]
    wide = freqs * 8
    own = spread_ref.shape[0]
    start = lax.axis_index("spec") * (own // 8)
    rows = onehot((iota((wide, freqs), 0) // 8 + start) % freqs == iota((wide, freqs), 1))
    same = iota((wide, wide), 0) % 8 == iota((wide, wide), 1) % 8
    for s in range(2):
        weights = freq_ref[s]
        left = dot(rows, weights).astype(BF16)
        shift_ref[s * wide : (s + 1) * wide, :] = jnp.where(same, dot_nt(left, rows), 0.0).astype(BF16)
        turned = dot_nt(rows[:own], weights).astype(BF16)
        spread_ref[:, s * wide : (s + 1) * wide] = jnp.where(
            same[:own], dot_nt(turned, rows), 0.0
        ).astype(BF16)
    stacked = jnp.concatenate(
        [angle_ref[m, s].astype(F32) for m in range(2) for s in range(2)], axis=0
    ).astype(BF16)
    lines = angles * 4
    r = iota((4 * lines, 4 * angles), 0)
    c = iota((4 * lines, 4 * angles), 1)
    direction = (r // 32) % (angles // 8) * 8 + r % 8
    chosen = onehot((r // lines) * angles + direction == c)
    lines_rows = dot(chosen, stacked).astype(BF16)
    r = iota((2 * lines, angles), 0)
    column = onehot((r // 32) % (angles // 8) * 8 + r % 8 == iota((2 * lines, angles), 1))
    r = iota((4 * lines, 2 * lines), 0)
    c = iota((4 * lines, 2 * lines), 1)
    keep = ((r // lines) % 2 == c // lines) & ((r // 8) % 4 == (c // 8) % 4)
    image_ref[...] = jnp.where(keep, dot_nt(lines_rows, column), 0.0).astype(BF16)
    for s in range(2):
        r = iota((2 * lines, 4 * angles), 0)
        c = iota((2 * lines, 4 * angles), 1)
        direction = (r // 32) % (angles // 8) * 8 + r % 8
        chosen = onehot(((r // lines) * 2 + s) * angles + direction == c)
        lines_rows = dot(chosen, stacked).astype(BF16)
        r = iota((lines, 2 * lines), 0)
        c = iota((lines, 2 * lines), 1)
        keep = (r // 8) % 4 == (c // 8) % 4
        back_ref[s * lines : (s + 1) * lines, :] = jnp.where(
            keep, dot_nt(column[:lines], lines_rows), 0.0
        ).astype(BF16)


def turned_late_kernel(first, reply_ref, map_ref, moved_in_ref, moved_ref, late_ref, turned_ref):
    freq_local, angles, points = moved_ref.shape
    reply = reply_ref[...].astype(F32).reshape(map_ref.shape[0], freq_local * angles)
    turned_ref[...] = reply.T.astype(BF16)
    late_kernel(first, turned_ref, map_ref, moved_in_ref, moved_ref, late_ref)


def late_kernel(first, turned_ref, map_ref, moved_in_ref, *refs):
    moved_ref, late_ref = refs[-2:]
    freq_local, angles, points = moved_ref.shape
    outer = onehot(place_of(iota((GROUP, HALF), 0)) == iota((GROUP, HALF), 1) + HALF)
    for k in range(points // GROUP):
        here = slice(k * GROUP, (k + 1) * GROUP)
        inflow = dot(turned_ref[...], map_ref[:, (first + k) * GROUP : (first + k + 1) * GROUP])
        moved_ref[:, :, here] = moved_in_ref[:, :, here] + inflow.reshape(freq_local, angles, GROUP)
        for j in range(angles // 8):
            levels = moved_ref[:, 8 * j : 8 * j + 8, here].reshape(freq_local * 8, GROUP)
            late_ref[j, :, k * HALF : (k + 1) * HALF] = dot(levels.astype(BF16), outer).astype(BF16)


def nonlinear_tile(level_refs, shift_ref, spread_ref, image_ref, back_ref, rate_ref, shifted_ref, gained_ref):
    parts, own, width = level_refs[0].shape
    wide = shift_ref.shape[1]
    freqs = wide // 8
    lines = parts * 32
    start = lax.axis_index("spec") * (own // 8)
    for j in range(parts):
        levels = jnp.concatenate([ref[j] for ref in level_refs], axis=0)
        shifted_ref[j] = dot(shift_ref[...], levels).astype(BF16)
    def image_of(q):
        shifted = jnp.concatenate(
            [
                shifted_ref[j, s * wide + 32 * q : s * wide + 32 * q + 32, :]
                for s in range(2)
                for j in range(parts)
            ],
            axis=0,
        )
        return dot(image_ref[...], shifted)

    doubled = []
    coming = image_of(0)
    for q in range(freqs // 4):
        source, place = divmod(q * 32, own)
        images = coming
        if q + 1 < freqs // 4:
            coming = image_of(q + 1)
        level = jnp.concatenate(
            [level_refs[source][j, place : place + 32, :].astype(F32) for j in range(parts)], axis=0
        )
        rates = [rate_ref[(start + 4 * q + k) % freqs] for k in range(4)]
        scaled = jnp.concatenate(
            [
                level[32 * j + 8 * k : 32 * j + 8 * k + 8] * rates[k]
                for j in range(parts)
                for k in range(4)
            ],
            axis=0,
        )
        deltas = []
        for m in range(2):
            plus = images[2 * m * lines : (2 * m + 1) * lines]
            minus = images[(2 * m + 1) * lines : (2 * m + 2) * lines]
            deltas.append(scaled * (level * (plus + minus) - 2.0 * plus * minus))
        low = jnp.concatenate(deltas, axis=0).astype(BF16)
        back = dot(back_ref[...], low).astype(BF16)
        for s in range(2):
            for j in range(parts):
                gained_ref[j, s * wide + 32 * q : s * wide + 32 * q + 32, :] = back[
                    (s * parts + j) * 32 : (s * parts + j) * 32 + 32
                ]
        if source == 0:
            doubled.append(deltas[0] + deltas[1])
    result = []
    for j in range(parts):
        lost = jnp.concatenate([d[32 * j : 32 * j + 32] for d in doubled], axis=0)
        result.append(dot(spread_ref[...], gained_ref[j]) - 2.0 * lost)
    return result


def early_kernel(sources, *refs):
    levels = refs[:sources]
    shift_ref, spread_ref, image_ref, back_ref, rate_ref, out_ref, shifted_ref, gained_ref = refs[sources:]
    result = nonlinear_tile(
        levels, shift_ref, spread_ref, image_ref, back_ref, rate_ref, shifted_ref, gained_ref
    )
    for j, values in enumerate(result):
        out_ref[j] = values


def final_kernel(sources, first, *refs):
    levels = refs[:sources]
    shift_ref, spread_ref, image_ref, back_ref, rate_ref = refs[sources : sources + 5]
    early_ref, moved_ref, depth_hbm, wind_hbm, wet_hbm = refs[sources + 5 : sources + 10]
    out_hbm, shifted_ref, gained_ref, late_ref, gain_ref, depth_ref, wind_ref, wet_ref, out_ref, sems = (
        refs[-10:]
    )
    small = fetch([depth_hbm, wind_hbm, wet_hbm], [depth_ref, wind_ref, wet_ref], sems)
    late = nonlinear_tile(
        levels, shift_ref, spread_ref, image_ref, back_ref, rate_ref, shifted_ref, gained_ref
    )
    for j, values in enumerate(late):
        late_ref[j] = values
    freq_local, angles, _ = moved_ref.shape
    points = depth_ref.shape[1]
    groups = late_ref.shape[2] // HALF
    own = freq_local * 8
    for copy in small:
        copy.wait()
    radian_freq = radian_rows(freq_local, points)
    wave_kh = dispersion(radian_freq, depth_ref[...])
    gain_ref[...] = wave_kh / (radian_freq * depth_ref[...])
    scale = radian_freq[:, 0:LANES] * (TIME_STEP * WIND_GROWTH)
    cosine, sine = angle_table(angles, LANES)
    restore = onehot(iota((GROUP, GROUP), 0) == place_of(iota((GROUP, GROUP), 1)))

    def result_copy(k):
        part = pl.ds(pl.multiple_of((first + k) * GROUP, GROUP), GROUP)
        here = pl.ds(pl.multiple_of(k * GROUP, GROUP), GROUP)
        return pltpu.make_async_copy(
            out_ref.at[:, :, here], out_hbm.at[:, :, part], sems.at[len(small) + k]
        )

    def one_group(k, carry):
        early_lanes = pl.ds(pl.multiple_of((first + k) * HALF, HALF), HALF)
        late_lanes = pl.ds(pl.multiple_of(k * HALF, HALF), HALF)
        mixed = jnp.concatenate(
            [
                jnp.concatenate([early_ref[j, :, early_lanes], late_ref[j, :, late_lanes]], axis=1)
                for j in range(angles // 8)
            ],
            axis=0,
        )
        high = mixed.astype(BF16)
        low = (mixed - high.astype(F32)).astype(BF16)
        transfer = dot(high, restore) + dot(low, restore)
        for half in range(GROUP // LANES):
            part = pl.ds(pl.multiple_of((first + k) * GROUP + half * LANES, LANES), LANES)
            place = pl.ds(pl.multiple_of(k * GROUP + half * LANES, LANES), LANES)
            here = slice(half * LANES, (half + 1) * LANES)
            wet = jnp.broadcast_to(wet_ref[:, part].astype(F32), (angles, LANES))
            along = wind_ref[0:1, part] * cosine + wind_ref[1:2, part] * sine
            for f in range(freq_local):
                slow = jnp.broadcast_to(gain_ref[f : f + 1, part], (angles, LANES))
                rise = jnp.broadcast_to(scale[f : f + 1, :], (angles, LANES))
                growth = rise * jnp.maximum(along * slow - 1.0, 0.0)
                moved = moved_ref[f, :, place]
                gained = jnp.concatenate(
                    [
                        transfer[j * own + 8 * f : j * own + 8 * f + 8, here]
                        for j in range(angles // 8)
                    ],
                    axis=0,
                )
                out_ref[f, :, place] = wet * (moved + gained + growth * moved)
        result_copy(k).start()
        return carry

    lax.fori_loop(0, groups, one_group, 0)
    for k in range(groups):
        result_copy(k).wait()


HBM = pl.BlockSpec(memory_space=pltpu.HBM)
VMEM = pl.BlockSpec(memory_space=pltpu.VMEM)


def params():
    return pltpu.CompilerParams(vmem_limit_bytes=VMEM_BYTES)


def cost(flops, moved):
    return pl.CostEstimate(flops=int(flops), bytes_accessed=int(moved), transcendentals=0)


def shards(
    spectrum, depths, currents, slopes, wind_speed, wet_mask,
    face_owner, face_block, freq_weights, angle_weights, transfer_rate,
):
    freq_local, angles, points = spectrum.shape
    group_count = lax.axis_size("spec")
    peers = lax.axis_size("blk")
    faces = face_block.shape[0]
    freqs = freq_local * group_count
    groups = points // GROUP
    own = freq_local * 8
    parts = angles // 8
    rows_fd = freq_local * angles
    wide = freqs * 8
    lines = 4 * angles
    edges = groups * EDGE
    capacity = max(2, (faces // 2 + peers - 2) // (peers - 1))
    reply_rows = peers * capacity * TILE
    size = freq_local * angles * points

    owner_row = face_owner.reshape(1, faces)
    block_row = face_block.reshape(1, faces)
    depth_row = depths.reshape(1, points)
    wet_row = wet_mask.reshape(1, points)

    requests = pl.pallas_call(
        functools.partial(request_kernel, capacity),
        in_specs=[HBM, HBM],
        out_shape=jax.ShapeDtypeStruct((peers, 1, LANES), I32),
        scratch_shapes=[
            pltpu.VMEM((1, faces), I32),
            pltpu.VMEM((1, faces), I32),
            pltpu.SemaphoreType.DMA((2,)),
        ],
        compiler_params=params(),
        cost_estimate=cost(1e10, 4e7),
        name="requests",
    )(owner_row, block_row)
    asked = lax.all_to_all(requests, "blk", split_axis=0, concat_axis=0, tiled=True)

    moved_first, high, low, early = pl.pallas_call(
        transport_kernel,
        in_specs=[HBM] * 5,
        out_shape=[
            jax.ShapeDtypeStruct((freq_local, angles, points), F32),
            jax.ShapeDtypeStruct((rows_fd, edges), BF16),
            jax.ShapeDtypeStruct((rows_fd, edges), BF16),
            jax.ShapeDtypeStruct((parts, own, groups * HALF), BF16),
        ],
        scratch_shapes=[
            pltpu.VMEM((groups, freq_local, angles, GROUP), F32),
            pltpu.VMEM((1, points), F32),
            pltpu.VMEM((2, points), F32),
            pltpu.VMEM((2, points), F32),
            pltpu.VMEM((1, points), I32),
            pltpu.VMEM((freq_local, angles, 2 * GROUP), F32),
            pltpu.VMEM((freq_local, points), F32),
            pltpu.VMEM((freq_local, points), F32),
            pltpu.VMEM((freq_local, points), F32),
            pltpu.VMEM((2, points), F32),
            pltpu.SemaphoreType.DMA((4 + groups,)),
        ],
        compiler_params=params(),
        cost_estimate=cost(100 * size, 12 * size),
        name="transport",
    )(spectrum, depth_row, currents, slopes, wet_row)

    def exchanged(array):
        return [
            lax.ppermute(
                array, "spec", [(s, (s - step) % group_count) for s in range(group_count)]
            )
            for step in range(1, group_count)
        ]

    early_levels = [early] + exchanged(early)

    reply = pl.pallas_call(
        functools.partial(select_kernel, capacity),
        out_shape=jax.ShapeDtypeStruct((peers, capacity * TILE, rows_fd), BF16),
        compiler_params=params(),
        cost_estimate=cost(2 * reply_rows * edges * rows_fd, 4 * rows_fd * edges),
        name="select",
    )(asked, high)
    replies = lax.all_to_all(reply, "blk", split_axis=0, concat_axis=0, tiled=True)

    weights = pl.pallas_call(
        weights_kernel,
        out_shape=[
            jax.ShapeDtypeStruct((2 * wide, wide), BF16),
            jax.ShapeDtypeStruct((own, 2 * wide), BF16),
            jax.ShapeDtypeStruct((4 * lines, 2 * lines), BF16),
            jax.ShapeDtypeStruct((2 * lines, 2 * lines), BF16),
        ],
        compiler_params=params(),
        cost_estimate=cost(1e9, 1e6),
        name="weights",
    )(freq_weights, angle_weights)

    halves = 2
    half_groups = groups // halves
    tile = half_groups * HALF
    half_wave = jax.ShapeDtypeStruct((freq_local, angles, points // halves), F32)
    *moved_local, reply_map = pl.pallas_call(
        functools.partial(local_kernel, capacity),
        in_specs=[HBM, HBM, VMEM, VMEM, VMEM],
        out_shape=[half_wave] * halves + [jax.ShapeDtypeStruct((reply_rows, points), BF16)],
        scratch_shapes=[
            pltpu.VMEM((1, faces), I32),
            pltpu.VMEM((1, faces), I32),
            pltpu.SemaphoreType.DMA((2,)),
        ],
        compiler_params=params(),
        cost_estimate=cost(4 * rows_fd * edges * points, 10 * size),
        name="local_inflow",
    )(owner_row, block_row, high, low, moved_first)

    width = groups * HALF
    weight_specs = [VMEM] * 4 + [pl.BlockSpec(memory_space=pltpu.SMEM)]
    moved, turned, late_levels, gained_early = [], None, [], None
    for h in range(halves):
        after = [gained_early] if h else []
        out = pl.pallas_call(
            functools.partial(late_kernel if h else turned_late_kernel, h * half_groups),
            in_specs=[VMEM] * 3 + [pl.BlockSpec(memory_space=pl.ANY)] * len(after),
            out_shape=[half_wave, jax.ShapeDtypeStruct((parts, own, tile), BF16)]
            + [jax.ShapeDtypeStruct((rows_fd, reply_rows), BF16)] * (h == 0),
            input_output_aliases={2: 0},
            compiler_params=params(),
            cost_estimate=cost(rows_fd * reply_rows * points, 5 * size),
            name=f"late_inflow_{h}",
        )(turned if h else replies, reply_map, moved_local[h], *after)
        moved.append(out[0])
        turned = turned if h else out[2]
        late_levels.append([out[1]] + exchanged(out[1]))
        if h == 0:
            gained_early = pl.pallas_call(
                functools.partial(early_kernel, group_count),
                in_specs=[VMEM] * group_count + weight_specs,
                out_shape=jax.ShapeDtypeStruct((parts, own, width), F32),
                scratch_shapes=[pltpu.VMEM((parts, 2 * wide, width), BF16)] * 2,
                compiler_params=params(),
                cost_estimate=cost(3e9, 3 * size),
                name="early_transfer",
            )(*early_levels, *weights, transfer_rate)

    result = []
    for h in range(halves):
        operands = [
            *late_levels[h], *weights, transfer_rate, gained_early, moved[h],
            depth_row, wind_speed, wet_row, *result,
        ]
        result = [
            pl.pallas_call(
                functools.partial(final_kernel, group_count, h * half_groups),
                in_specs=[VMEM] * group_count
                + weight_specs
                + [VMEM, VMEM, HBM, HBM, HBM]
                + [HBM] * len(result),
                out_specs=HBM,
                out_shape=jax.ShapeDtypeStruct((freq_local, angles, points), F32),
                scratch_shapes=[pltpu.VMEM((parts, 2 * wide, tile), BF16)] * 2
                + [
                    pltpu.VMEM((parts, own, tile), F32),
                    pltpu.VMEM((freq_local, points), F32),
                    pltpu.VMEM((1, points), F32),
                    pltpu.VMEM((2, points), F32),
                    pltpu.VMEM((1, points), I32),
                    pltpu.VMEM((freq_local, angles, half_groups * GROUP), F32),
                    pltpu.SemaphoreType.DMA((3 + half_groups,)),
                ],
                input_output_aliases={len(operands) - 1: 0} if result else {},
                compiler_params=params(),
                cost_estimate=cost(2e9, 6 * size),
                name=f"late_transfer_{h}",
            )(*operands)
        ]
    return result[0]


def solution(mesh):
    in_specs = (
        P("spec", None, "blk"),
        P("blk"),
        P(None, "blk"),
        P(None, "blk"),
        P(None, "blk"),
        P("blk"),
        P("blk", None),
        P("blk"),
        P(),
        P(),
        P(),
    )
    out_specs = P("spec", None, "blk")
    return jax.shard_map(shards, mesh=mesh, in_specs=in_specs, out_specs=out_specs, check_vma=False)
```

```python
import functools
import math

import jax
import jax.numpy as jnp
from jax import lax
from jax.experimental import pallas as pl
from jax.experimental.pallas import tpu as pltpu
from jax.sharding import PartitionSpec as P

GRAVITY = 9.81
TIME_STEP = 200.0
CELL_SIZE = 5500.0
LOWEST_FREQ = 0.0418
FREQ_GROWTH = 1.1
WIND_GROWTH = 0.0003
TURN_LIMIT = 0.9

TILE = 8
CELLS = TILE * TILE
GROUP = 256
HALF = 128
EDGE = 128
LANES = 128
VMEM_BYTES = 24 * 1024 * 1024

F32 = jnp.float32
BF16 = jnp.bfloat16
I32 = jnp.int32


def iota(shape, dim):
    return lax.broadcasted_iota(I32, shape, dim)


def onehot(mask):
    return jnp.where(mask, 1.0, 0.0).astype(BF16)


def dot(a, b):
    return jnp.dot(a, b, preferred_element_type=F32)


def dot_nt(a, b):
    return lax.dot_general(a, b, (((1,), (1,)), ((), ())), preferred_element_type=F32)


def dispersion(radian_freq, water_depth):
    deep_kh = radian_freq * radian_freq / GRAVITY * water_depth
    wave_kh = deep_kh / jnp.sqrt(jnp.tanh(deep_kh))
    return wave_kh


def radian_rows(freq_local, width):
    index = iota((freq_local, width), 0) + lax.axis_index("spec") * freq_local
    return (2.0 * math.pi * LOWEST_FREQ) * jnp.exp(index.astype(F32) * math.log(FREQ_GROWTH))


def angle_table(angles, width):
    values = iota((angles, width), 0).astype(F32) * (2.0 * math.pi / angles)
    return jnp.cos(values), jnp.sin(values)


def place_of(point):
    block = point // CELLS
    row = (point // TILE) % TILE
    col = point % TILE
    inner = (row >= 1) & (row <= 6) & (col >= 1) & (col <= 6)
    rank = (row - 1) * 6 + jnp.clip(col - 1, 0, 6)
    early = inner & (rank < 32)
    before = jnp.clip(rank, 0, 32)
    return jnp.where(early, block * 32 + rank, HALF + block * 32 + point % CELLS - before)


def edge_columns(width):
    source = iota((2 * width, EDGE), 0)
    upright = source // width
    point = source % width
    block = point // CELLS
    row = (point // TILE) % TILE
    col = point % TILE
    across = jnp.where(upright == 0, col, row)
    along = jnp.where(upright == 0, row, col)
    edge = upright * 64 + jnp.where(across == 0, 0, 32) + block * TILE + along
    on_edge = (across == 0) | (across == TILE - 1)
    return onehot(on_edge & (edge == iota((2 * width, EDGE), 1)))


def fetch(sources, targets, sems, first=0):
    copies = [
        pltpu.make_async_copy(source, target, sems.at[first + k])
        for k, (source, target) in enumerate(zip(sources, targets))
    ]
    for copy in copies:
        copy.start()
    return copies


def request_kernel(capacity, owner_hbm, block_hbm, request_ref, owner_ref, block_ref, sems):
    copies = fetch([owner_hbm, block_hbm], [owner_ref, block_ref], sems)
    peers = request_ref.shape[0]
    faces = owner_ref.shape[1]
    mine = lax.axis_index("blk")
    for copy in copies:
        copy.wait()
    peer = iota((peers, faces), 0)
    asked = (owner_ref[...] == peer) & (peer != mine)
    earlier = onehot(iota((faces, faces), 0) < iota((faces, faces), 1))
    rank = dot(onehot(asked), earlier).astype(I32)
    side = iota((1, faces), 1) % 4
    block = block_ref[...]
    base = (block // 4) * EDGE + (side // 2) * 64 + (1 - side % 2) * 32 + (block % 4) * TILE + 1
    base = base.astype(F32)
    lane = iota((peers, LANES), 1)
    result = jnp.zeros((peers, LANES), F32)
    for k in range(capacity):
        found = jnp.sum(jnp.where(asked & (rank == k), base, 0.0), axis=1, keepdims=True)
        result = jnp.where(lane == k, found, result)
    result = result.astype(I32)
    for p in range(peers):
        request_ref[p] = result[p : p + 1]


def select_kernel(capacity, request_ref, high_ref, reply_ref):
    peers = request_ref.shape[0]
    rows = peers * capacity * TILE
    edges = high_ref.shape[1]
    asked = jnp.concatenate([request_ref[p] for p in range(peers)], axis=0)
    coarse = (asked // 16).astype(F32).astype(BF16)
    fine = (asked % 16).astype(F32).astype(BF16)
    spread = onehot(iota((rows, peers), 0) // (capacity * TILE) == iota((rows, peers), 1))
    asked = 16.0 * dot(spread, coarse) + dot(spread, fine)
    row = iota((rows, LANES), 0)
    slot = (row // TILE) % capacity
    chosen = (slot == iota((rows, LANES), 1)) & (asked > 0.0)
    target = jnp.sum(
        jnp.where(chosen, asked + (row % TILE).astype(F32), 0.0), axis=1, keepdims=True
    )
    pick = onehot(iota((rows, edges), 1).astype(F32) + 1.0 == target)
    reply = dot_nt(pick, high_ref[...]).astype(BF16)
    for p in range(peers):
        reply_ref[p] = reply[p * capacity * TILE : (p + 1) * capacity * TILE]


def set_speeds(depth_ref, wet_ref, current_ref, group_ref, drift_ref, first):
    freq_local, points = group_ref.shape
    part = slice(first, first + points)
    radian_freq = radian_rows(freq_local, points)
    depth = depth_ref[:, part]
    wave_kh = dispersion(radian_freq, depth)
    decay_two = jnp.exp(-2.0 * wave_kh)
    denom = 1.0 - decay_two * decay_two
    ratio = 4.0 * wave_kh * decay_two / denom
    phase = radian_freq * depth / wave_kh
    wet = wet_ref[:, part].astype(F32) * (TIME_STEP / CELL_SIZE)
    group_ref[...] = 0.5 * (1.0 + ratio) * phase * wet
    drift_ref[0:1, :] = current_ref[0:1, part] * wet
    drift_ref[1:2, :] = current_ref[1:2, part] * wet
    return 2.0 * radian_freq * decay_two / denom


def sides(angles):
    lane = iota((angles, LANES), 1)
    col = lane % TILE
    row = (lane // TILE) % TILE
    return col == 0, col == TILE - 1, row == 0, row == TILE - 1


def edges_kernel(spec_ref, depth_ref, current_ref, wet_ref, high_ref, flux_ref, group_ref, drift_ref):
    freq_local, angles, points = spec_ref.shape
    set_speeds(depth_ref, wet_ref, current_ref, group_ref, drift_ref, 0)
    cosine, sine = angle_table(angles, LANES)
    west, east, south, north = sides(angles)
    columns = edge_columns(GROUP)

    def one_group(g, carry):
        for half in range(GROUP // LANES):
            part = pl.ds(pl.multiple_of(g * GROUP + half * LANES, LANES), LANES)
            here = slice(half * LANES, (half + 1) * LANES)
            there = slice(GROUP + half * LANES, GROUP + (half + 1) * LANES)
            drift_x = jnp.broadcast_to(drift_ref[0:1, part], (angles, LANES))
            drift_y = jnp.broadcast_to(drift_ref[1:2, part], (angles, LANES))
            for f in range(freq_local):
                energy = spec_ref[f, :, part]
                speed = jnp.broadcast_to(group_ref[f : f + 1, part], (angles, LANES))
                flow_x = (speed * cosine + drift_x) * energy
                flow_y = (speed * sine + drift_y) * energy
                flux_ref[f, :, here] = jnp.maximum(jnp.where(east, flow_x, -flow_x), 0.0)
                flux_ref[f, :, there] = jnp.maximum(jnp.where(north, flow_y, -flow_y), 0.0)
        flux = flux_ref[...].reshape(freq_local * angles, 2 * GROUP)
        place = pl.ds(pl.multiple_of(g * EDGE, EDGE), EDGE)
        high_ref[:, place] = dot(flux.astype(BF16), columns).astype(BF16)
        return carry

    lax.fori_loop(0, points // GROUP, one_group, 0)


def transport_kernel(
    first, after_ref, spec_ref, depth_ref, current_ref, slope_ref, wet_ref,
    moved_ref, low_ref, early_ref,
    flux_ref, group_ref, turn_x_ref, turn_y_ref, drift_ref,
):
    freq_local, angles, points = moved_ref.shape
    cosine, sine = angle_table(angles, LANES)
    west, east, south, north = sides(angles)
    turn = set_speeds(depth_ref, wet_ref, current_ref, group_ref, drift_ref, first)
    turn = turn * (TIME_STEP / (2.0 * math.pi / angles))
    turn_x_ref[...] = turn * slope_ref[0:1, first : first + points]
    turn_y_ref[...] = turn * slope_ref[1:2, first : first + points]
    columns = edge_columns(GROUP)
    inner = onehot(place_of(iota((GROUP, HALF), 0)) == iota((GROUP, HALF), 1))

    def one_group(g, carry):
        for half in range(GROUP // LANES):
            part = pl.ds(pl.multiple_of(g * GROUP + half * LANES, LANES), LANES)
            wide_part = pl.ds(pl.multiple_of(first + g * GROUP + half * LANES, LANES), LANES)
            here = slice(half * LANES, (half + 1) * LANES)
            there = slice(GROUP + half * LANES, GROUP + (half + 1) * LANES)
            drift_x = jnp.broadcast_to(drift_ref[0:1, part], (angles, LANES))
            drift_y = jnp.broadcast_to(drift_ref[1:2, part], (angles, LANES))
            for f in range(freq_local):
                energy = spec_ref[f, :, wide_part]
                speed = jnp.broadcast_to(group_ref[f : f + 1, part], (angles, LANES))
                turn_x = jnp.broadcast_to(turn_x_ref[f : f + 1, part], (angles, LANES))
                turn_y = jnp.broadcast_to(turn_y_ref[f : f + 1, part], (angles, LANES))
                flow_x = (speed * cosine + drift_x) * energy
                flow_y = (speed * sine + drift_y) * energy
                turning = jnp.clip(sine * turn_x - cosine * turn_y, -TURN_LIMIT, TURN_LIMIT)
                flow_t = turning * energy
                right = jnp.maximum(flow_x, 0.0)
                left = right - flow_x
                up = jnp.maximum(flow_y, 0.0)
                down = up - flow_y
                ahead = jnp.maximum(flow_t, 0.0)
                back = ahead - flow_t
                total = energy - (right + left) - (up + down) - (ahead + back)
                total = total + pltpu.roll(jnp.where(east, 0.0, right), 1, 1)
                total = total + pltpu.roll(jnp.where(west, 0.0, left), LANES - 1, 1)
                total = total + pltpu.roll(jnp.where(north, 0.0, up), TILE, 1)
                total = total + pltpu.roll(jnp.where(south, 0.0, down), LANES - TILE, 1)
                total = total + pltpu.roll(ahead, 1, 0) + pltpu.roll(back, angles - 1, 0)
                moved_ref[f, :, part] = total
                flux_ref[f, :, here] = jnp.where(east, right, left)
                flux_ref[f, :, there] = jnp.where(north, up, down)
        flux = flux_ref[...].reshape(freq_local * angles, 2 * GROUP)
        low = (flux - flux.astype(BF16).astype(F32)).astype(BF16)
        place = pl.ds(pl.multiple_of(g * EDGE, EDGE), EDGE)
        low_ref[:, place] = dot(low, columns).astype(BF16)
        part = pl.ds(pl.multiple_of(g * GROUP, GROUP), GROUP)
        for j in range(angles // 8):
            levels = moved_ref[:, 8 * j : 8 * j + 8, part].reshape(freq_local * 8, GROUP).astype(BF16)
            early_ref[j, :, place] = dot(levels, inner).astype(BF16)
        return carry

    lax.fori_loop(0, points // GROUP, one_group, 0)


def local_kernel(capacity, halves, owner_ref, block_ref, high_ref, *refs):
    low_refs, sources = refs[:halves], refs[halves : 2 * halves]
    moved_refs, map_ref = refs[2 * halves : 3 * halves], refs[3 * halves]
    freq_local, angles, points = sources[0].shape
    each = points // GROUP
    ranks = face_ranks(owner_ref, block_ref)
    edges = high_ref.shape[1]
    piece = edges // halves
    for g in range(each * halves):
        part = slice(g * GROUP, (g + 1) * GROUP)
        pick, reply_map = inflow_maps(capacity, g, ranks, edges, map_ref.shape[0])
        map_ref[:, part] = reply_map
        inflow = dot(high_ref[...], pick)
        for h in range(halves):
            inflow = inflow + dot(low_refs[h][...], pick[h * piece : (h + 1) * piece])
        here = slice(g % each * GROUP, (g % each + 1) * GROUP)
        moved_refs[g // each][:, :, here] = sources[g // each][:, :, here] + inflow.reshape(
            freq_local, angles, GROUP
        )


def face_ranks(owner_ref, block_ref):
    faces = owner_ref.shape[1]
    owner = owner_ref[...]
    by_column = jnp.broadcast_to(owner, (faces, faces))
    below = iota((faces, faces), 0)
    right = iota((faces, faces), 1)
    by_row = jnp.sum(jnp.where(below == right, by_column, 0).astype(F32), axis=1, keepdims=True)
    equal = (by_row == by_column.astype(F32)) & (below < right)
    rank = jnp.sum(jnp.where(equal, 1.0, 0.0), axis=0, keepdims=True)
    return jnp.concatenate(
        [block_ref[...].astype(F32), owner.astype(F32), rank, jnp.zeros((5, faces), F32)], axis=0
    ).astype(BF16)


def inflow_maps(capacity, group, table, edges, rows):
    faces = table.shape[1]
    width = GROUP
    mine = lax.axis_index("blk")
    point = iota((faces, width), 1)
    block = point // CELLS + group * (width // CELLS)
    col = point % TILE
    row = (point // TILE) % TILE
    face = iota((faces, width), 0)
    at_x = dot(table, onehot((face == block * 4 + jnp.where(col == 0, 0, 1)))).astype(I32)
    at_y = dot(table, onehot((face == block * 4 + jnp.where(row == 0, 2, 3)))).astype(I32)
    point = iota((1, width), 1)
    col = point % TILE
    row = (point // TILE) % TILE

    def ids(found, across, along, upright):
        edge = (across == 0) | (across == TILE - 1)
        from_block, from_owner, slot = found[0:1], found[1:2], found[2:3]
        local = edge & (from_owner == mine)
        remote = edge & (from_owner != mine)
        base = upright * 64 + jnp.where(across == 0, 32, 0)
        source = (from_block // 4) * EDGE + base + (from_block % 4) * TILE + along
        reply = (from_owner * capacity + slot) * TILE + along
        return jnp.where(local, source, -1), jnp.where(remote, reply, -1)

    source_x, reply_x = ids(at_x, col, row, 0)
    source_y, reply_y = ids(at_y, row, col, 1)
    line = iota((rows, width), 0)
    reply_map = onehot((line == reply_x) | (line == reply_y))
    line = iota((edges, width), 0)
    return onehot((line == source_x) | (line == source_y)), reply_map


def weights_kernel(freq_ref, angle_ref, shift_ref, spread_ref, image_ref, back_ref):
    freqs = freq_ref.shape[1]
    angles = angle_ref.shape[2]
    wide = freqs * 8
    own = spread_ref.shape[0]
    start = lax.axis_index("spec") * (own // 8)
    rows = onehot((iota((wide, freqs), 0) // 8 + start) % freqs == iota((wide, freqs), 1))
    same = iota((wide, wide), 0) % 8 == iota((wide, wide), 1) % 8
    for s in range(2):
        weights = freq_ref[s]
        left = dot(rows, weights).astype(BF16)
        shift_ref[s * wide : (s + 1) * wide, :] = jnp.where(same, dot_nt(left, rows), 0.0).astype(BF16)
        turned = dot_nt(rows[:own], weights).astype(BF16)
        spread_ref[:, s * wide : (s + 1) * wide] = jnp.where(
            same[:own], dot_nt(turned, rows), 0.0
        ).astype(BF16)
    stacked = jnp.concatenate(
        [angle_ref[m, s].astype(F32) for m in range(2) for s in range(2)], axis=0
    ).astype(BF16)
    lines = angles * 4
    r = iota((4 * lines, 4 * angles), 0)
    c = iota((4 * lines, 4 * angles), 1)
    direction = (r // 32) % (angles // 8) * 8 + r % 8
    chosen = onehot((r // lines) * angles + direction == c)
    lines_rows = dot(chosen, stacked).astype(BF16)
    r = iota((2 * lines, angles), 0)
    column = onehot((r // 32) % (angles // 8) * 8 + r % 8 == iota((2 * lines, angles), 1))
    r = iota((4 * lines, 2 * lines), 0)
    c = iota((4 * lines, 2 * lines), 1)
    keep = ((r // lines) % 2 == c // lines) & ((r // 8) % 4 == (c // 8) % 4)
    image_ref[...] = jnp.where(keep, dot_nt(lines_rows, column), 0.0).astype(BF16)
    for s in range(2):
        r = iota((2 * lines, 4 * angles), 0)
        c = iota((2 * lines, 4 * angles), 1)
        direction = (r // 32) % (angles // 8) * 8 + r % 8
        chosen = onehot(((r // lines) * 2 + s) * angles + direction == c)
        lines_rows = dot(chosen, stacked).astype(BF16)
        r = iota((lines, 2 * lines), 0)
        c = iota((lines, 2 * lines), 1)
        keep = (r // 8) % 4 == (c // 8) % 4
        back_ref[s * lines : (s + 1) * lines, :] = jnp.where(
            keep, dot_nt(column[:lines], lines_rows), 0.0
        ).astype(BF16)


def turned_late_kernel(first, reply_ref, map_ref, moved_in_ref, moved_ref, late_ref, turned_ref):
    freq_local, angles, points = moved_ref.shape
    reply = reply_ref[...].astype(F32).reshape(map_ref.shape[0], freq_local * angles)
    turned_ref[...] = reply.T.astype(BF16)
    late_kernel(first, turned_ref, map_ref, moved_in_ref, moved_ref, late_ref)


def late_kernel(first, turned_ref, map_ref, moved_in_ref, *refs):
    moved_ref, late_ref = refs[-2:]
    freq_local, angles, points = moved_ref.shape
    outer = onehot(place_of(iota((GROUP, HALF), 0)) == iota((GROUP, HALF), 1) + HALF)
    for k in range(points // GROUP):
        here = slice(k * GROUP, (k + 1) * GROUP)
        inflow = dot(turned_ref[...], map_ref[:, (first + k) * GROUP : (first + k + 1) * GROUP])
        moved_ref[:, :, here] = moved_in_ref[:, :, here] + inflow.reshape(freq_local, angles, GROUP)
        for j in range(angles // 8):
            levels = moved_ref[:, 8 * j : 8 * j + 8, here].reshape(freq_local * 8, GROUP)
            late_ref[j, :, k * HALF : (k + 1) * HALF] = dot(levels.astype(BF16), outer).astype(BF16)


def nonlinear_tile(level_refs, shift_ref, spread_ref, image_ref, back_ref, rate_ref, shifted_ref, gained_ref):
    parts, own, width = level_refs[0].shape
    wide = shift_ref.shape[1]
    freqs = wide // 8
    lines = parts * 32
    start = lax.axis_index("spec") * (own // 8)
    for j in range(parts):
        levels = jnp.concatenate([ref[j] for ref in level_refs], axis=0)
        for s in range(2):
            rows = slice(s * wide, (s + 1) * wide)
            shifted_ref[j, rows, :] = dot(shift_ref[rows, :], levels).astype(BF16)
    def image_of(q):
        shifted = jnp.concatenate(
            [
                shifted_ref[j, s * wide + 32 * q : s * wide + 32 * q + 32, :]
                for s in range(2)
                for j in range(parts)
            ],
            axis=0,
        )
        return [dot(image_ref[2 * m * lines : 2 * (m + 1) * lines, :], shifted) for m in range(2)]

    doubled = []
    coming = image_of(0)
    for q in range(freqs // 4):
        source, place = divmod(q * 32, own)
        images = coming
        if q + 1 < freqs // 4:
            coming = image_of(q + 1)
        level = jnp.concatenate(
            [level_refs[source][j, place : place + 32, :].astype(F32) for j in range(parts)], axis=0
        )
        rates = [rate_ref[(start + 4 * q + k) % freqs] for k in range(4)]
        scaled = jnp.concatenate(
            [
                level[32 * j + 8 * k : 32 * j + 8 * k + 8] * rates[k]
                for j in range(parts)
                for k in range(4)
            ],
            axis=0,
        )
        deltas = []
        for m in range(2):
            plus = images[m][:lines]
            minus = images[m][lines:]
            deltas.append(scaled * (level * (plus + minus) - 2.0 * plus * minus))
        low = jnp.concatenate(deltas, axis=0).astype(BF16)
        for s in range(2):
            back = dot(back_ref[s * lines : (s + 1) * lines, :], low).astype(BF16)
            for j in range(parts):
                gained_ref[j, s * wide + 32 * q : s * wide + 32 * q + 32, :] = back[
                    32 * j : 32 * j + 32
                ]
        if source == 0:
            doubled.append(deltas[0] + deltas[1])
    result = []
    for j in range(parts):
        lost = jnp.concatenate([d[32 * j : 32 * j + 32] for d in doubled], axis=0)
        spread = [
            dot(spread_ref[:, s * wide : (s + 1) * wide], gained_ref[j, s * wide : (s + 1) * wide, :])
            for s in range(2)
        ]
        result.append(spread[0] + spread[1] - 2.0 * lost)
    return result


def early_kernel(sources, halves, *refs):
    count = sources * halves
    shift_ref, spread_ref, image_ref, back_ref, rate_ref, out_ref = refs[count : count + 6]
    joined, (shifted_ref, gained_ref) = refs[count + 6 : count + 6 + sources], refs[-2:]
    tile = refs[0].shape[2]
    for r in range(sources):
        for h in range(halves):
            joined[r][:, :, h * tile : (h + 1) * tile] = refs[h * sources + r][...]
    result = nonlinear_tile(
        joined, shift_ref, spread_ref, image_ref, back_ref, rate_ref, shifted_ref, gained_ref
    )
    for j, values in enumerate(result):
        out_ref[j] = values


def final_kernel(sources, first, *refs):
    levels = refs[:sources]
    shift_ref, spread_ref, image_ref, back_ref, rate_ref = refs[sources : sources + 5]
    early_ref, moved_ref, depth_hbm, wind_hbm, wet_hbm = refs[sources + 5 : sources + 10]
    out_hbm, shifted_ref, gained_ref, late_ref, gain_ref, depth_ref, wind_ref, wet_ref, out_ref, sems = (
        refs[-10:]
    )
    small = fetch([depth_hbm, wind_hbm, wet_hbm], [depth_ref, wind_ref, wet_ref], sems)
    late = nonlinear_tile(
        levels, shift_ref, spread_ref, image_ref, back_ref, rate_ref, shifted_ref, gained_ref
    )
    for j, values in enumerate(late):
        late_ref[j] = values
    freq_local, angles, _ = moved_ref.shape
    points = depth_ref.shape[1]
    groups = late_ref.shape[2] // HALF
    own = freq_local * 8
    for copy in small:
        copy.wait()
    radian_freq = radian_rows(freq_local, points)
    wave_kh = dispersion(radian_freq, depth_ref[...])
    gain_ref[...] = wave_kh / (radian_freq * depth_ref[...])
    scale = radian_freq[:, 0:LANES] * (TIME_STEP * WIND_GROWTH)
    cosine, sine = angle_table(angles, LANES)
    restore = onehot(iota((GROUP, GROUP), 0) == place_of(iota((GROUP, GROUP), 1)))

    def result_copy(k):
        part = pl.ds(pl.multiple_of((first + k) * GROUP, GROUP), GROUP)
        here = pl.ds(pl.multiple_of(k * GROUP, GROUP), GROUP)
        return pltpu.make_async_copy(
            out_ref.at[:, :, here], out_hbm.at[:, :, part], sems.at[len(small) + k]
        )

    def one_group(k, carry):
        early_lanes = pl.ds(pl.multiple_of((first + k) * HALF, HALF), HALF)
        late_lanes = pl.ds(pl.multiple_of(k * HALF, HALF), HALF)
        mixed = jnp.concatenate(
            [
                jnp.concatenate([early_ref[j, :, early_lanes], late_ref[j, :, late_lanes]], axis=1)
                for j in range(angles // 8)
            ],
            axis=0,
        )
        high = mixed.astype(BF16)
        low = (mixed - high.astype(F32)).astype(BF16)
        transfer = dot(high, restore) + dot(low, restore)
        for half in range(GROUP // LANES):
            part = pl.ds(pl.multiple_of((first + k) * GROUP + half * LANES, LANES), LANES)
            place = pl.ds(pl.multiple_of(k * GROUP + half * LANES, LANES), LANES)
            here = slice(half * LANES, (half + 1) * LANES)
            wet = jnp.broadcast_to(wet_ref[:, part].astype(F32), (angles, LANES))
            along = wind_ref[0:1, part] * cosine + wind_ref[1:2, part] * sine
            for f in range(freq_local):
                slow = jnp.broadcast_to(gain_ref[f : f + 1, part], (angles, LANES))
                rise = jnp.broadcast_to(scale[f : f + 1, :], (angles, LANES))
                growth = rise * jnp.maximum(along * slow - 1.0, 0.0)
                moved = moved_ref[f, :, place]
                gained = jnp.concatenate(
                    [
                        transfer[j * own + 8 * f : j * own + 8 * f + 8, here]
                        for j in range(angles // 8)
                    ],
                    axis=0,
                )
                out_ref[f, :, place] = wet * (moved + gained + growth * moved)
        result_copy(k).start()
        return carry

    lax.fori_loop(0, groups, one_group, 0)
    for k in range(groups):
        result_copy(k).wait()


HBM = pl.BlockSpec(memory_space=pltpu.HBM)
VMEM = pl.BlockSpec(memory_space=pltpu.VMEM)


def params():
    return pltpu.CompilerParams(vmem_limit_bytes=VMEM_BYTES)


def cost(flops, moved):
    return pl.CostEstimate(flops=int(flops), bytes_accessed=int(moved), transcendentals=0)


def shards(
    spectrum, depths, currents, slopes, wind_speed, wet_mask,
    face_owner, face_block, freq_weights, angle_weights, transfer_rate,
):
    freq_local, angles, points = spectrum.shape
    group_count = lax.axis_size("spec")
    peers = lax.axis_size("blk")
    faces = face_block.shape[0]
    freqs = freq_local * group_count
    groups = points // GROUP
    own = freq_local * 8
    parts = angles // 8
    rows_fd = freq_local * angles
    wide = freqs * 8
    lines = 4 * angles
    edges = groups * EDGE
    capacity = max(2, (faces // 2 + peers - 2) // (peers - 1))
    reply_rows = peers * capacity * TILE

    owner_row = face_owner.reshape(1, faces)
    block_row = face_block.reshape(1, faces)
    depth_row = depths.reshape(1, points)
    wet_row = wet_mask.reshape(1, points)

    requests = pl.pallas_call(
        functools.partial(request_kernel, capacity),
        in_specs=[HBM, HBM],
        out_shape=jax.ShapeDtypeStruct((peers, 1, LANES), I32),
        scratch_shapes=[
            pltpu.VMEM((1, faces), I32),
            pltpu.VMEM((1, faces), I32),
            pltpu.SemaphoreType.DMA((2,)),
        ],
        compiler_params=params(),
        cost_estimate=cost(1e10, 4e7),
        name="requests",
    )(owner_row, block_row)
    asked = lax.all_to_all(requests, "blk", split_axis=0, concat_axis=0, tiled=True)

    high = pl.pallas_call(
        edges_kernel,
        out_shape=jax.ShapeDtypeStruct((rows_fd, edges), BF16),
        scratch_shapes=[
            pltpu.VMEM((freq_local, angles, 2 * GROUP), F32),
            pltpu.VMEM((freq_local, points), F32),
            pltpu.VMEM((2, points), F32),
        ],
        compiler_params=params(),
        cost_estimate=cost(1e6, 1e5),
        name="edges",
    )(spectrum, depth_row, currents, wet_row)

    def exchanged(array):
        return [
            lax.ppermute(
                array, "spec", [(s, (s - step) % group_count) for s in range(group_count)]
            )
            for step in range(1, group_count)
        ]

    reply = pl.pallas_call(
        functools.partial(select_kernel, capacity),
        out_shape=jax.ShapeDtypeStruct((peers, capacity * TILE, rows_fd), BF16),
        compiler_params=params(),
        cost_estimate=cost(1e6, 1e5),
        name="select",
    )(asked, high)
    replies = lax.all_to_all(reply, "blk", split_axis=0, concat_axis=0, tiled=True)

    weights = pl.pallas_call(
        weights_kernel,
        out_shape=[
            jax.ShapeDtypeStruct((2 * wide, wide), BF16),
            jax.ShapeDtypeStruct((own, 2 * wide), BF16),
            jax.ShapeDtypeStruct((4 * lines, 2 * lines), BF16),
            jax.ShapeDtypeStruct((2 * lines, 2 * lines), BF16),
        ],
        compiler_params=params(),
        cost_estimate=cost(1e6, 1e5),
        name="weights",
    )(freq_weights, angle_weights)

    halves = 2
    half_groups = groups // halves
    half_points = points // halves
    tile = half_groups * HALF
    half_wave = jax.ShapeDtypeStruct((freq_local, angles, half_points), F32)
    half_levels = jax.ShapeDtypeStruct((parts, own, tile), BF16)
    moved_inner, low, early_levels = [], [], []
    for h in range(halves):
        out = pl.pallas_call(
            functools.partial(transport_kernel, h * half_points),
            in_specs=[pl.BlockSpec(memory_space=pl.ANY)] + [VMEM] * 5,
            out_shape=[half_wave, jax.ShapeDtypeStruct((rows_fd, edges // halves), BF16), half_levels],
            scratch_shapes=[pltpu.VMEM((freq_local, angles, 2 * GROUP), F32)]
            + [pltpu.VMEM((freq_local, half_points), F32)] * 3
            + [pltpu.VMEM((2, half_points), F32)],
            compiler_params=params(),
            cost_estimate=cost(1e6, 1e5),
            name=f"transport_{h}",
        )(reply, spectrum, depth_row, currents, slopes, wet_row)
        moved_inner.append(out[0])
        low.append(out[1])
        early_levels.append([out[2]] + exchanged(out[2]))

    *moved_local, reply_map = pl.pallas_call(
        functools.partial(local_kernel, capacity, halves),
        out_shape=[half_wave] * halves + [jax.ShapeDtypeStruct((reply_rows, points), BF16)],
        input_output_aliases={3 + halves + h: h for h in range(halves)},
        compiler_params=params(),
        cost_estimate=cost(1e6, 1e5),
        name="local_inflow",
    )(owner_row, block_row, high, *low, *moved_inner)

    width = groups * HALF
    weight_specs = [VMEM] * 4 + [pl.BlockSpec(memory_space=pltpu.SMEM)]
    moved, turned, late_levels, gained_early = [], None, [], None
    for h in range(halves):
        after = [gained_early] if h else []
        out = pl.pallas_call(
            functools.partial(late_kernel if h else turned_late_kernel, h * half_groups),
            in_specs=[VMEM] * 3 + [pl.BlockSpec(memory_space=pl.ANY)] * len(after),
            out_shape=[half_wave, jax.ShapeDtypeStruct((parts, own, tile), BF16)]
            + [jax.ShapeDtypeStruct((rows_fd, reply_rows), BF16)] * (h == 0),
            input_output_aliases={2: 0},
            compiler_params=params(),
            cost_estimate=cost(1e6, 1e5),
            name=f"late_inflow_{h}",
        )(turned if h else replies, reply_map, moved_local[h], *after)
        moved.append(out[0])
        turned = turned if h else out[2]
        late_levels.append([out[1]] + exchanged(out[1]))
        if h == 0:
            gained_early = pl.pallas_call(
                functools.partial(early_kernel, group_count, halves),
                in_specs=[VMEM] * (group_count * halves) + weight_specs,
                out_shape=jax.ShapeDtypeStruct((parts, own, width), F32),
                scratch_shapes=[pltpu.VMEM((parts, own, width), BF16)] * group_count
                + [pltpu.VMEM((parts, 2 * wide, width), BF16)] * 2,
                compiler_params=params(),
                cost_estimate=cost(1e6, 1e5),
                name="early_transfer",
            )(*early_levels[0], *early_levels[1], *weights, transfer_rate)

    result = []
    for h in range(halves):
        operands = [
            *late_levels[h], *weights, transfer_rate, gained_early, moved[h],
            depth_row, wind_speed, wet_row, *result,
        ]
        result = [
            pl.pallas_call(
                functools.partial(final_kernel, group_count, h * half_groups),
                in_specs=[VMEM] * group_count
                + weight_specs
                + [VMEM, VMEM, HBM, HBM, HBM]
                + [HBM] * len(result),
                out_specs=HBM,
                out_shape=jax.ShapeDtypeStruct((freq_local, angles, points), F32),
                scratch_shapes=[pltpu.VMEM((parts, 2 * wide, tile), BF16)] * 2
                + [
                    pltpu.VMEM((parts, own, tile), F32),
                    pltpu.VMEM((freq_local, points), F32),
                    pltpu.VMEM((1, points), F32),
                    pltpu.VMEM((2, points), F32),
                    pltpu.VMEM((1, points), I32),
                    pltpu.VMEM((freq_local, angles, half_groups * GROUP), F32),
                    pltpu.SemaphoreType.DMA((3 + half_groups,)),
                ],
                input_output_aliases={len(operands) - 1: 0} if result else {},
                compiler_params=params(),
                cost_estimate=cost(1e6, 1e5),
                name=f"late_transfer_{h}",
            )(*operands)
        ]
    return result[0]


def solution(mesh):
    in_specs = (
        P("spec", None, "blk"),
        P("blk"),
        P(None, "blk"),
        P(None, "blk"),
        P(None, "blk"),
        P("blk"),
        P("blk", None),
        P("blk"),
        P(),
        P(),
        P(),
    )
    out_specs = P("spec", None, "blk")
    return jax.shard_map(shards, mesh=mesh, in_specs=in_specs, out_specs=out_specs, check_vma=False)
```

```python
import functools
import math

import jax
import jax.numpy as jnp
from jax import lax
from jax.experimental import pallas as pl
from jax.experimental.pallas import tpu as pltpu
from jax.sharding import PartitionSpec as P

GRAVITY = 9.81
TIME_STEP = 200.0
CELL_SIZE = 5500.0
LOWEST_FREQ = 0.0418
FREQ_GROWTH = 1.1
WIND_GROWTH = 0.0003
TURN_LIMIT = 0.9

TILE = 8
CELLS = TILE * TILE
GROUP = 256
HALF = 128
EDGE = 128
LANES = 128
VMEM_BYTES = 24 * 1024 * 1024

F32 = jnp.float32
BF16 = jnp.bfloat16
I32 = jnp.int32


def iota(shape, dim):
    return lax.broadcasted_iota(I32, shape, dim)


def onehot(mask):
    return jnp.where(mask, 1.0, 0.0).astype(BF16)


def dot(a, b):
    return jnp.dot(a, b, preferred_element_type=F32)


def dot_nt(a, b):
    return lax.dot_general(a, b, (((1,), (1,)), ((), ())), preferred_element_type=F32)


def dispersion(radian_freq, water_depth):
    deep_kh = radian_freq * radian_freq / GRAVITY * water_depth
    wave_kh = deep_kh / jnp.sqrt(jnp.tanh(deep_kh))
    return wave_kh


def radian_rows(freq_local, width):
    index = iota((freq_local, width), 0) + lax.axis_index("spec") * freq_local
    return (2.0 * math.pi * LOWEST_FREQ) * jnp.exp(index.astype(F32) * math.log(FREQ_GROWTH))


def angle_table(angles, width):
    values = iota((angles, width), 0).astype(F32) * (2.0 * math.pi / angles)
    return jnp.cos(values), jnp.sin(values)


def place_of(point):
    block = point // CELLS
    row = (point // TILE) % TILE
    col = point % TILE
    inner = (row >= 1) & (row <= 6) & (col >= 1) & (col <= 6)
    rank = (row - 1) * 6 + jnp.clip(col - 1, 0, 6)
    early = inner & (rank < 32)
    before = jnp.clip(rank, 0, 32)
    return jnp.where(early, block * 32 + rank, HALF + block * 32 + point % CELLS - before)


def edge_columns(width):
    source = iota((2 * width, EDGE), 0)
    upright = source // width
    point = source % width
    block = point // CELLS
    row = (point // TILE) % TILE
    col = point % TILE
    across = jnp.where(upright == 0, col, row)
    along = jnp.where(upright == 0, row, col)
    edge = upright * 64 + jnp.where(across == 0, 0, 32) + block * TILE + along
    on_edge = (across == 0) | (across == TILE - 1)
    return onehot(on_edge & (edge == iota((2 * width, EDGE), 1)))


def fetch(sources, targets, sems, first=0):
    copies = [
        pltpu.make_async_copy(source, target, sems.at[first + k])
        for k, (source, target) in enumerate(zip(sources, targets))
    ]
    for copy in copies:
        copy.start()
    return copies


def request_kernel(capacity, coded_ref, request_ref):
    peers = request_ref.shape[0]
    faces = coded_ref.shape[1]
    mine = lax.axis_index("blk")
    owner, block = coded_ref[...] // 256, coded_ref[...] % 256
    peer = iota((peers, faces), 0)
    asked = (owner == peer) & (peer != mine)
    earlier = onehot(iota((faces, faces), 0) < iota((faces, faces), 1))
    rank = dot(onehot(asked), earlier).astype(I32)
    side = iota((1, faces), 1) % 4
    base = (block // 4) * EDGE + (side // 2) * 64 + (1 - side % 2) * 32 + (block % 4) * TILE + 1
    base = base.astype(F32)
    lane = iota((peers, LANES), 1)
    result = jnp.zeros((peers, LANES), F32)
    for k in range(capacity):
        found = jnp.sum(jnp.where(asked & (rank == k), base, 0.0), axis=1, keepdims=True)
        result = jnp.where(lane == k, found, result)
    result = result.astype(I32)
    for p in range(peers):
        request_ref[p] = result[p : p + 1]


def select_kernel(capacity, request_ref, high_ref, after_ref, reply_ref):
    peers = request_ref.shape[0]
    rows = peers * capacity * TILE
    edges = high_ref.shape[1]
    asked = jnp.concatenate([request_ref[p] for p in range(peers)], axis=0)
    coarse = (asked // 16).astype(F32).astype(BF16)
    fine = (asked % 16).astype(F32).astype(BF16)
    spread = onehot(iota((rows, peers), 0) // (capacity * TILE) == iota((rows, peers), 1))
    asked = 16.0 * dot(spread, coarse) + dot(spread, fine)
    row = iota((rows, LANES), 0)
    slot = (row // TILE) % capacity
    chosen = (slot == iota((rows, LANES), 1)) & (asked > 0.0)
    target = jnp.sum(
        jnp.where(chosen, asked + (row % TILE).astype(F32), 0.0), axis=1, keepdims=True
    )
    pick = onehot(iota((rows, edges), 1).astype(F32) + 1.0 == target)
    reply = dot_nt(pick, high_ref[...]).astype(BF16)
    for p in range(peers):
        reply_ref[p] = reply[p * capacity * TILE : (p + 1) * capacity * TILE]


def set_speeds(depth_ref, wet_ref, current_ref, group_ref, drift_ref, first):
    freq_local, points = group_ref.shape
    part = slice(first, first + points)
    radian_freq = radian_rows(freq_local, points)
    depth = depth_ref[:, part]
    wave_kh = dispersion(radian_freq, depth)
    decay_two = jnp.exp(-2.0 * wave_kh)
    denom = 1.0 - decay_two * decay_two
    ratio = 4.0 * wave_kh * decay_two / denom
    phase = radian_freq * depth / wave_kh
    wet = wet_ref[:, part].astype(F32) * (TIME_STEP / CELL_SIZE)
    group_ref[...] = 0.5 * (1.0 + ratio) * phase * wet
    drift_ref[0:1, :] = current_ref[0:1, part] * wet
    drift_ref[1:2, :] = current_ref[1:2, part] * wet
    return 2.0 * radian_freq * decay_two / denom


def sides(angles):
    lane = iota((angles, LANES), 1)
    col = lane % TILE
    row = (lane // TILE) % TILE
    return col == 0, col == TILE - 1, row == 0, row == TILE - 1


def edges_kernel(
    after_ref, spec_ref, depth_ref, current_ref, wet_ref, high_ref, flux_ref, group_ref, drift_ref
):
    freq_local, angles, points = spec_ref.shape
    set_speeds(depth_ref, wet_ref, current_ref, group_ref, drift_ref, 0)
    cosine, sine = angle_table(angles, LANES)
    west, east, south, north = sides(angles)
    columns = edge_columns(GROUP)

    def one_group(g, carry):
        for half in range(GROUP // LANES):
            part = pl.ds(pl.multiple_of(g * GROUP + half * LANES, LANES), LANES)
            here = slice(half * LANES, (half + 1) * LANES)
            there = slice(GROUP + half * LANES, GROUP + (half + 1) * LANES)
            drift_x = jnp.broadcast_to(drift_ref[0:1, part], (angles, LANES))
            drift_y = jnp.broadcast_to(drift_ref[1:2, part], (angles, LANES))
            for f in range(freq_local):
                energy = spec_ref[f, :, part]
                speed = jnp.broadcast_to(group_ref[f : f + 1, part], (angles, LANES))
                flow_x = (speed * cosine + drift_x) * energy
                flow_y = (speed * sine + drift_y) * energy
                flux_ref[f, :, here] = jnp.maximum(jnp.where(east, flow_x, -flow_x), 0.0)
                flux_ref[f, :, there] = jnp.maximum(jnp.where(north, flow_y, -flow_y), 0.0)
        flux = flux_ref[...].reshape(freq_local * angles, 2 * GROUP)
        place = pl.ds(pl.multiple_of(g * EDGE, EDGE), EDGE)
        high_ref[:, place] = dot(flux.astype(BF16), columns).astype(BF16)
        return carry

    lax.fori_loop(0, points // GROUP, one_group, 0)


def transport_kernel(first, spec_ref, depth_ref, current_ref, slope_ref, wet_ref, *refs):
    moved_ref, low_ref, early_ref, flux_ref, group_ref, turn_x_ref, turn_y_ref, drift_ref = refs[-8:]
    freq_local, angles, points = moved_ref.shape
    cosine, sine = angle_table(angles, LANES)
    west, east, south, north = sides(angles)
    turn = set_speeds(depth_ref, wet_ref, current_ref, group_ref, drift_ref, first)
    turn = turn * (TIME_STEP / (2.0 * math.pi / angles))
    turn_x_ref[...] = turn * slope_ref[0:1, first : first + points]
    turn_y_ref[...] = turn * slope_ref[1:2, first : first + points]
    columns = edge_columns(GROUP)
    inner = onehot(place_of(iota((GROUP, HALF), 0)) == iota((GROUP, HALF), 1))

    def one_group(g, carry):
        for half in range(GROUP // LANES):
            part = pl.ds(pl.multiple_of(g * GROUP + half * LANES, LANES), LANES)
            wide_part = pl.ds(pl.multiple_of(first + g * GROUP + half * LANES, LANES), LANES)
            here = slice(half * LANES, (half + 1) * LANES)
            there = slice(GROUP + half * LANES, GROUP + (half + 1) * LANES)
            drift_x = jnp.broadcast_to(drift_ref[0:1, part], (angles, LANES))
            drift_y = jnp.broadcast_to(drift_ref[1:2, part], (angles, LANES))
            for f in range(freq_local):
                energy = spec_ref[f, :, wide_part]
                speed = jnp.broadcast_to(group_ref[f : f + 1, part], (angles, LANES))
                turn_x = jnp.broadcast_to(turn_x_ref[f : f + 1, part], (angles, LANES))
                turn_y = jnp.broadcast_to(turn_y_ref[f : f + 1, part], (angles, LANES))
                flow_x = (speed * cosine + drift_x) * energy
                flow_y = (speed * sine + drift_y) * energy
                turning = jnp.clip(sine * turn_x - cosine * turn_y, -TURN_LIMIT, TURN_LIMIT)
                flow_t = turning * energy
                right = jnp.maximum(flow_x, 0.0)
                left = right - flow_x
                up = jnp.maximum(flow_y, 0.0)
                down = up - flow_y
                ahead = jnp.maximum(flow_t, 0.0)
                back = ahead - flow_t
                total = energy - (right + left) - (up + down) - (ahead + back)
                total = total + pltpu.roll(jnp.where(east, 0.0, right), 1, 1)
                total = total + pltpu.roll(jnp.where(west, 0.0, left), LANES - 1, 1)
                total = total + pltpu.roll(jnp.where(north, 0.0, up), TILE, 1)
                total = total + pltpu.roll(jnp.where(south, 0.0, down), LANES - TILE, 1)
                total = total + pltpu.roll(ahead, 1, 0) + pltpu.roll(back, angles - 1, 0)
                moved_ref[f, :, part] = total
                flux_ref[f, :, here] = jnp.where(east, right, left)
                flux_ref[f, :, there] = jnp.where(north, up, down)
        flux = flux_ref[...].reshape(freq_local * angles, 2 * GROUP)
        low = (flux - flux.astype(BF16).astype(F32)).astype(BF16)
        place = pl.ds(pl.multiple_of(g * EDGE, EDGE), EDGE)
        low_ref[:, place] = dot(low, columns).astype(BF16)
        part = pl.ds(pl.multiple_of(g * GROUP, GROUP), GROUP)
        for j in range(angles // 8):
            levels = moved_ref[:, 8 * j : 8 * j + 8, part].reshape(freq_local * 8, GROUP).astype(BF16)
            early_ref[j, :, place] = dot(levels, inner).astype(BF16)
        return carry

    lax.fori_loop(0, points // GROUP, one_group, 0)


def local_kernel(capacity, halves, coded_ref, high_ref, *refs):
    low_refs, sources = refs[:halves], refs[halves : 2 * halves]
    moved_refs, map_ref = refs[2 * halves : 3 * halves], refs[3 * halves]
    freq_local, angles, points = sources[0].shape
    each = points // GROUP
    ranks = face_ranks(coded_ref)
    edges = high_ref.shape[1]
    piece = edges // halves
    for g in range(each * halves):
        part = slice(g * GROUP, (g + 1) * GROUP)
        pick, reply_map = inflow_maps(capacity, g, ranks, edges, map_ref.shape[0])
        map_ref[:, part] = reply_map
        inflow = dot(high_ref[...], pick)
        for h in range(halves):
            inflow = inflow + dot(low_refs[h][...], pick[h * piece : (h + 1) * piece])
        here = slice(g % each * GROUP, (g % each + 1) * GROUP)
        moved_refs[g // each][:, :, here] = sources[g // each][:, :, here] + inflow.reshape(
            freq_local, angles, GROUP
        )


def face_ranks(coded_ref):
    faces = coded_ref.shape[1]
    owner, block = coded_ref[...] // 256, coded_ref[...] % 256
    by_column = jnp.broadcast_to(owner, (faces, faces))
    below = iota((faces, faces), 0)
    right = iota((faces, faces), 1)
    by_row = jnp.sum(jnp.where(below == right, by_column, 0).astype(F32), axis=1, keepdims=True)
    equal = (by_row == by_column.astype(F32)) & (below < right)
    rank = jnp.sum(jnp.where(equal, 1.0, 0.0), axis=0, keepdims=True)
    return jnp.concatenate(
        [block.astype(F32), owner.astype(F32), rank, jnp.zeros((5, faces), F32)], axis=0
    ).astype(BF16)


def inflow_maps(capacity, group, table, edges, rows):
    faces = table.shape[1]
    width = GROUP
    mine = lax.axis_index("blk")
    point = iota((faces, width), 1)
    block = point // CELLS + group * (width // CELLS)
    col = point % TILE
    row = (point // TILE) % TILE
    face = iota((faces, width), 0)
    at_x = dot(table, onehot((face == block * 4 + jnp.where(col == 0, 0, 1)))).astype(I32)
    at_y = dot(table, onehot((face == block * 4 + jnp.where(row == 0, 2, 3)))).astype(I32)
    point = iota((1, width), 1)
    col = point % TILE
    row = (point // TILE) % TILE

    def ids(found, across, along, upright):
        edge = (across == 0) | (across == TILE - 1)
        from_block, from_owner, slot = found[0:1], found[1:2], found[2:3]
        local = edge & (from_owner == mine)
        remote = edge & (from_owner != mine)
        base = upright * 64 + jnp.where(across == 0, 32, 0)
        source = (from_block // 4) * EDGE + base + (from_block % 4) * TILE + along
        reply = (from_owner * capacity + slot) * TILE + along
        return jnp.where(local, source, -1), jnp.where(remote, reply, -1)

    source_x, reply_x = ids(at_x, col, row, 0)
    source_y, reply_y = ids(at_y, row, col, 1)
    line = iota((rows, width), 0)
    reply_map = onehot((line == reply_x) | (line == reply_y))
    line = iota((edges, width), 0)
    return onehot((line == source_x) | (line == source_y)), reply_map


def weights_kernel(freq_ref, angle_ref, shift_ref, spread_ref, image_ref, back_ref):
    freqs = freq_ref.shape[1]
    angles = angle_ref.shape[2]
    wide = freqs * 8
    own = spread_ref.shape[0]
    start = lax.axis_index("spec") * (own // 8)
    rows = onehot((iota((wide, freqs), 0) // 8 + start) % freqs == iota((wide, freqs), 1))
    same = iota((wide, wide), 0) % 8 == iota((wide, wide), 1) % 8
    for s in range(2):
        weights = freq_ref[s]
        left = dot(rows, weights).astype(BF16)
        shift_ref[s * wide : (s + 1) * wide, :] = jnp.where(same, dot_nt(left, rows), 0.0).astype(BF16)
        turned = dot_nt(rows[:own], weights).astype(BF16)
        spread_ref[:, s * wide : (s + 1) * wide] = jnp.where(
            same[:own], dot_nt(turned, rows), 0.0
        ).astype(BF16)
    stacked = jnp.concatenate(
        [angle_ref[m, s].astype(F32) for m in range(2) for s in range(2)], axis=0
    ).astype(BF16)
    lines = angles * 4
    r = iota((4 * lines, 4 * angles), 0)
    c = iota((4 * lines, 4 * angles), 1)
    direction = (r // 32) % (angles // 8) * 8 + r % 8
    chosen = onehot((r // lines) * angles + direction == c)
    lines_rows = dot(chosen, stacked).astype(BF16)
    r = iota((2 * lines, angles), 0)
    column = onehot((r // 32) % (angles // 8) * 8 + r % 8 == iota((2 * lines, angles), 1))
    r = iota((4 * lines, 2 * lines), 0)
    c = iota((4 * lines, 2 * lines), 1)
    keep = ((r // lines) % 2 == c // lines) & ((r // 8) % 4 == (c // 8) % 4)
    image_ref[...] = jnp.where(keep, dot_nt(lines_rows, column), 0.0).astype(BF16)
    for s in range(2):
        r = iota((2 * lines, 4 * angles), 0)
        c = iota((2 * lines, 4 * angles), 1)
        direction = (r // 32) % (angles // 8) * 8 + r % 8
        chosen = onehot(((r // lines) * 2 + s) * angles + direction == c)
        lines_rows = dot(chosen, stacked).astype(BF16)
        r = iota((lines, 2 * lines), 0)
        c = iota((lines, 2 * lines), 1)
        keep = (r // 8) % 4 == (c // 8) % 4
        back_ref[s * lines : (s + 1) * lines, :] = jnp.where(
            keep, dot_nt(column[:lines], lines_rows), 0.0
        ).astype(BF16)


def turned_late_kernel(first, reply_ref, map_ref, moved_in_ref, *refs):
    moved_ref, late_ref, turned_ref = refs[-3:]
    freq_local, angles, points = moved_ref.shape
    reply = reply_ref[...].astype(F32).reshape(map_ref.shape[0], freq_local * angles)
    turned_ref[...] = reply.T.astype(BF16)
    late_kernel(first, turned_ref, map_ref, moved_in_ref, moved_ref, late_ref)


def late_kernel(first, turned_ref, map_ref, moved_in_ref, *refs):
    moved_ref, late_ref = refs[-2:]
    freq_local, angles, points = moved_ref.shape
    outer = onehot(place_of(iota((GROUP, HALF), 0)) == iota((GROUP, HALF), 1) + HALF)
    for k in range(points // GROUP):
        here = slice(k * GROUP, (k + 1) * GROUP)
        inflow = dot(turned_ref[...], map_ref[:, (first + k) * GROUP : (first + k + 1) * GROUP])
        moved_ref[:, :, here] = moved_in_ref[:, :, here] + inflow.reshape(freq_local, angles, GROUP)
        for j in range(angles // 8):
            levels = moved_ref[:, 8 * j : 8 * j + 8, here].reshape(freq_local * 8, GROUP)
            late_ref[j, :, k * HALF : (k + 1) * HALF] = dot(levels.astype(BF16), outer).astype(BF16)


def nonlinear_tile(level_refs, shift_ref, spread_ref, image_ref, back_ref, rate_ref, shifted_ref, gained_ref):
    parts, own, width = level_refs[0].shape
    wide = shift_ref.shape[1]
    freqs = wide // 8
    lines = parts * 32
    start = lax.axis_index("spec") * (own // 8)
    levels = jnp.concatenate(
        [jnp.concatenate([ref[j] for ref in level_refs], axis=0) for j in range(parts)], axis=1
    )
    for s in range(2):
        rows = slice(s * wide, (s + 1) * wide)
        shifted_ref[rows, :] = dot(shift_ref[rows, :], levels).astype(BF16)
    pairs = range(0, freqs // 4, 2)

    def beside(pieces):
        return jnp.concatenate(pieces, axis=1)

    def image_of(q):
        shifted = beside(
            [
                jnp.concatenate(
                    [
                        shifted_ref[
                            s * wide + 32 * k : s * wide + 32 * k + 32, j * width : (j + 1) * width
                        ]
                        for s in range(2)
                        for j in range(parts)
                    ],
                    axis=0,
                )
                for k in (q, q + 1)
            ]
        )
        return [dot(image_ref[2 * m * lines : 2 * (m + 1) * lines, :], shifted) for m in range(2)]

    doubled = []
    coming = image_of(0)
    for q in pairs:
        images = coming
        if q + 2 < freqs // 4:
            coming = image_of(q + 2)
        lows = []
        for side, k in enumerate((q, q + 1)):
            source, place = divmod(k * 32, own)
            here = slice(side * width, (side + 1) * width)
            level = jnp.concatenate(
                [level_refs[source][j, place : place + 32, :].astype(F32) for j in range(parts)], axis=0
            )
            rates = [rate_ref[(start + 4 * k + i) % freqs] for i in range(4)]
            scaled = jnp.concatenate(
                [
                    level[32 * j + 8 * i : 32 * j + 8 * i + 8] * rates[i]
                    for j in range(parts)
                    for i in range(4)
                ],
                axis=0,
            )
            deltas = []
            for m in range(2):
                plus = images[m][:lines, here]
                minus = images[m][lines:, here]
                deltas.append(scaled * (level * (plus + minus) - 2.0 * plus * minus))
            lows.append(jnp.concatenate(deltas, axis=0).astype(BF16))
            if source == 0:
                doubled.append(deltas[0] + deltas[1])
        low = beside(lows)
        for s in range(2):
            back = dot(back_ref[s * lines : (s + 1) * lines, :], low).astype(BF16)
            for side, k in enumerate((q, q + 1)):
                for j in range(parts):
                    gained_ref[
                        s * wide + 32 * k : s * wide + 32 * k + 32, j * width : (j + 1) * width
                    ] = back[32 * j : 32 * j + 32, side * width : (side + 1) * width]
    spread = [
        dot(spread_ref[:, s * wide : (s + 1) * wide], gained_ref[s * wide : (s + 1) * wide, :])
        for s in range(2)
    ]
    result = []
    for j in range(parts):
        here = slice(j * width, (j + 1) * width)
        lost = jnp.concatenate([d[32 * j : 32 * j + 32] for d in doubled], axis=0)
        result.append(spread[0][:, here] + spread[1][:, here] - 2.0 * lost)
    return result


def put_back(values, where):
    stacked = jnp.concatenate(values, axis=0)
    high = stacked.astype(BF16)
    low = (stacked - high.astype(F32)).astype(BF16)
    return dot(jnp.concatenate([high, low], axis=1), where)


def places(first):
    position = iota((2 * HALF, GROUP), 0) % HALF + first
    return onehot(position == place_of(iota((2 * HALF, GROUP), 1)))


def early_kernel(sources, *refs):
    shift_ref, spread_ref, image_ref, back_ref, rate_ref = refs[sources : sources + 5]
    out_ref, shifted_ref, gained_ref = refs[-3:]
    result = nonlinear_tile(
        refs[:sources], shift_ref, spread_ref, image_ref, back_ref, rate_ref, shifted_ref, gained_ref
    )
    where = places(0)
    for k in range(out_ref.shape[1] // GROUP):
        values = [values[:, k * HALF : (k + 1) * HALF] for values in result]
        out_ref[:, k * GROUP : (k + 1) * GROUP] = put_back(values, where)


def final_kernel(sources, first, *refs):
    levels = refs[:sources]
    shift_ref, spread_ref, image_ref, back_ref, rate_ref = refs[sources : sources + 5]
    early_ref, moved_ref, depth_hbm, wind_hbm, wet_hbm = refs[sources + 5 : sources + 10]
    out_hbm, shifted_ref, gained_ref, late_ref, gain_ref, depth_ref, wind_ref, wet_ref, out_ref, sems = (
        refs[-10:]
    )
    small = fetch([depth_hbm, wind_hbm, wet_hbm], [depth_ref, wind_ref, wet_ref], sems)
    late = nonlinear_tile(
        levels, shift_ref, spread_ref, image_ref, back_ref, rate_ref, shifted_ref, gained_ref
    )
    for j, values in enumerate(late):
        late_ref[j] = values
    freq_local, angles, _ = moved_ref.shape
    points = depth_ref.shape[1]
    groups = late_ref.shape[2] // HALF
    own = freq_local * 8
    for copy in small:
        copy.wait()
    radian_freq = radian_rows(freq_local, points)
    wave_kh = dispersion(radian_freq, depth_ref[...])
    gain_ref[...] = wave_kh / (radian_freq * depth_ref[...])
    scale = radian_freq[:, 0:LANES] * (TIME_STEP * WIND_GROWTH)
    cosine, sine = angle_table(angles, LANES)
    where = places(HALF)

    def result_copy(k):
        part = pl.ds(pl.multiple_of((first + k) * GROUP, GROUP), GROUP)
        here = pl.ds(pl.multiple_of(k * GROUP, GROUP), GROUP)
        return pltpu.make_async_copy(
            out_ref.at[:, :, here], out_hbm.at[:, :, part], sems.at[len(small) + k]
        )

    def one_group(k, carry):
        lanes = pl.ds(pl.multiple_of(k * HALF, HALF), HALF)
        transfer = put_back([late_ref[j, :, lanes] for j in range(angles // 8)], where)
        here = pl.ds(pl.multiple_of(k * GROUP, GROUP), GROUP)
        transfer = transfer + early_ref[:, here]
        for half in range(GROUP // LANES):
            part = pl.ds(pl.multiple_of((first + k) * GROUP + half * LANES, LANES), LANES)
            place = pl.ds(pl.multiple_of(k * GROUP + half * LANES, LANES), LANES)
            here = slice(half * LANES, (half + 1) * LANES)
            wet = jnp.broadcast_to(wet_ref[:, part].astype(F32), (angles, LANES))
            along = wind_ref[0:1, part] * cosine + wind_ref[1:2, part] * sine
            for f in range(freq_local):
                slow = jnp.broadcast_to(gain_ref[f : f + 1, part], (angles, LANES))
                rise = jnp.broadcast_to(scale[f : f + 1, :], (angles, LANES))
                growth = rise * jnp.maximum(along * slow - 1.0, 0.0)
                moved = moved_ref[f, :, place]
                gained = jnp.concatenate(
                    [
                        transfer[j * own + 8 * f : j * own + 8 * f + 8, here]
                        for j in range(angles // 8)
                    ],
                    axis=0,
                )
                out_ref[f, :, place] = wet * (moved + gained + growth * moved)
        result_copy(k).start()
        return carry

    lax.fori_loop(0, groups, one_group, 0)
    for k in range(groups):
        result_copy(k).wait()


HBM = pl.BlockSpec(memory_space=pltpu.HBM)
VMEM = pl.BlockSpec(memory_space=pltpu.VMEM)
ANY = pl.BlockSpec(memory_space=pl.ANY)


def params():
    return pltpu.CompilerParams(vmem_limit_bytes=VMEM_BYTES)


def cost(flops, moved):
    return pl.CostEstimate(flops=int(flops), bytes_accessed=int(moved), transcendentals=0)


def shards(
    spectrum, depths, currents, slopes, wind_speed, wet_mask,
    face_owner, face_block, freq_weights, angle_weights, transfer_rate,
):
    freq_local, angles, points = spectrum.shape
    group_count = lax.axis_size("spec")
    peers = lax.axis_size("blk")
    faces = face_block.shape[0]
    freqs = freq_local * group_count
    groups = points // GROUP
    own = freq_local * 8
    parts = angles // 8
    rows_fd = freq_local * angles
    wide = freqs * 8
    lines = 4 * angles
    edges = groups * EDGE
    capacity = max(2, (faces // 2 + peers - 2) // (peers - 1))
    reply_rows = peers * capacity * TILE

    coded = face_owner.reshape(1, faces) * 256 + face_block.reshape(1, faces)
    depth_row = depths.reshape(1, points)
    wet_row = wet_mask.reshape(1, points)

    requests = pl.pallas_call(
        functools.partial(request_kernel, capacity),
        out_shape=jax.ShapeDtypeStruct((peers, 1, LANES), I32),
        compiler_params=params(),
        cost_estimate=cost(1e10, 4e7),
        name="requests",
    )(coded)
    asked = lax.all_to_all(requests, "blk", split_axis=0, concat_axis=0, tiled=True)

    high = pl.pallas_call(
        edges_kernel,
        in_specs=[ANY] + [VMEM] * 4,
        out_shape=jax.ShapeDtypeStruct((rows_fd, edges), BF16),
        scratch_shapes=[
            pltpu.VMEM((freq_local, angles, 2 * GROUP), F32),
            pltpu.VMEM((freq_local, points), F32),
            pltpu.VMEM((2, points), F32),
        ],
        compiler_params=params(),
        cost_estimate=cost(1e6, 1e5),
        name="edges",
    )(requests, spectrum, depth_row, currents, wet_row)

    def exchanged(array):
        return [
            lax.ppermute(
                array, "spec", [(s, (s - step) % group_count) for s in range(group_count)]
            )
            for step in range(1, group_count)
        ]

    weights = pl.pallas_call(
        weights_kernel,
        out_shape=[
            jax.ShapeDtypeStruct((2 * wide, wide), BF16),
            jax.ShapeDtypeStruct((own, 2 * wide), BF16),
            jax.ShapeDtypeStruct((4 * lines, 2 * lines), BF16),
            jax.ShapeDtypeStruct((2 * lines, 2 * lines), BF16),
        ],
        compiler_params=params(),
        cost_estimate=cost(1e6, 1e5),
        name="weights",
    )(freq_weights, angle_weights)

    halves = 2
    half_groups = groups // halves
    half_points = points // halves
    tile = half_groups * HALF
    half_wave = jax.ShapeDtypeStruct((freq_local, angles, half_points), F32)
    half_levels = jax.ShapeDtypeStruct((parts, own, tile), BF16)
    moved_inner, low, early_levels = [], [], []
    for h in range(halves):
        out = pl.pallas_call(
            functools.partial(transport_kernel, h * half_points),
            in_specs=[VMEM] * 5 + [ANY],
            out_shape=[half_wave, jax.ShapeDtypeStruct((rows_fd, edges // halves), BF16), half_levels],
            scratch_shapes=[pltpu.VMEM((freq_local, angles, 2 * GROUP), F32)]
            + [pltpu.VMEM((freq_local, half_points), F32)] * 3
            + [pltpu.VMEM((2, half_points), F32)],
            compiler_params=params(),
            cost_estimate=cost(1e6, 1e5),
            name=f"transport_{h}",
        )(spectrum, depth_row, currents, slopes, wet_row, reply if h else high)
        moved_inner.append(out[0])
        low.append(out[1])
        early_levels.append([out[2]] + exchanged(out[2]))
        if h == 0:
            reply = pl.pallas_call(
                functools.partial(select_kernel, capacity),
                in_specs=[VMEM, VMEM, ANY],
                out_shape=jax.ShapeDtypeStruct((peers, capacity * TILE, rows_fd), BF16),
                compiler_params=params(),
                cost_estimate=cost(1e6, 1e5),
                name="select",
            )(asked, high, out[1])
            replies = lax.all_to_all(reply, "blk", split_axis=0, concat_axis=0, tiled=True)

    *moved_local, reply_map = pl.pallas_call(
        functools.partial(local_kernel, capacity, halves),
        out_shape=[half_wave] * halves + [jax.ShapeDtypeStruct((reply_rows, points), BF16)],
        input_output_aliases={2 + halves + h: h for h in range(halves)},
        compiler_params=params(),
        cost_estimate=cost(1e6, 1e5),
        name="local_inflow",
    )(coded, high, *low, *moved_inner)

    weight_specs = [VMEM] * 4 + [pl.BlockSpec(memory_space=pltpu.SMEM)]
    tile_scratch = [pltpu.VMEM((2 * wide, parts * tile), BF16)] * 2
    moved, turned, late_levels, gained_early = [], None, [], []
    for h in range(halves):
        gained_early.append(
            pl.pallas_call(
                functools.partial(early_kernel, group_count),
                in_specs=[VMEM] * group_count + weight_specs + [ANY],
                out_shape=jax.ShapeDtypeStruct((parts * own, half_points), F32),
                scratch_shapes=tile_scratch,
                compiler_params=params(),
                cost_estimate=cost(1e6, 1e5),
                name=f"early_transfer_{h}",
            )(*early_levels[h], *weights, transfer_rate, turned if h else reply_map)
        )
        out = pl.pallas_call(
            functools.partial(late_kernel if h else turned_late_kernel, h * half_groups),
            in_specs=[VMEM] * 3 + [ANY],
            out_shape=[half_wave, jax.ShapeDtypeStruct((parts, own, tile), BF16)]
            + [jax.ShapeDtypeStruct((rows_fd, reply_rows), BF16)] * (h == 0),
            input_output_aliases={2: 0},
            compiler_params=params(),
            cost_estimate=cost(*((1e6, 1e5) if h else (1.5e8, 4e6))),
            name=f"late_inflow_{h}",
        )(turned if h else replies, reply_map, moved_local[h], gained_early[h])
        moved.append(out[0])
        turned = turned if h else out[2]
        late_levels.append([out[1]] + exchanged(out[1]))

    result = []
    for h in range(halves):
        operands = [
            *late_levels[h], *weights, transfer_rate, gained_early[h], moved[h],
            depth_row, wind_speed, wet_row, *result,
        ]
        result = [
            pl.pallas_call(
                functools.partial(final_kernel, group_count, h * half_groups),
                in_specs=[VMEM] * group_count
                + weight_specs
                + [VMEM, VMEM, HBM, HBM, HBM]
                + [HBM] * len(result),
                out_specs=HBM,
                out_shape=jax.ShapeDtypeStruct((freq_local, angles, points), F32),
                scratch_shapes=tile_scratch
                + [
                    pltpu.VMEM((parts, own, tile), F32),
                    pltpu.VMEM((freq_local, points), F32),
                    pltpu.VMEM((1, points), F32),
                    pltpu.VMEM((2, points), F32),
                    pltpu.VMEM((1, points), I32),
                    pltpu.VMEM((freq_local, angles, half_groups * GROUP), F32),
                    pltpu.SemaphoreType.DMA((3 + half_groups,)),
                ],
                input_output_aliases={len(operands) - 1: 0} if result else {},
                compiler_params=params(),
                cost_estimate=cost(1e6, 1e5),
                name=f"late_transfer_{h}",
            )(*operands)
        ]
    return result[0]


def solution(mesh):
    in_specs = (
        P("spec", None, "blk"),
        P("blk"),
        P(None, "blk"),
        P(None, "blk"),
        P(None, "blk"),
        P("blk"),
        P("blk", None),
        P("blk"),
        P(),
        P(),
        P(),
    )
    out_specs = P("spec", None, "blk")
    return jax.shard_map(shards, mesh=mesh, in_specs=in_specs, out_specs=out_specs, check_vma=False)
```

```python
import functools
import math

import jax
import jax.numpy as jnp
from jax import lax
from jax.experimental import pallas as pl
from jax.experimental.pallas import tpu as pltpu
from jax.sharding import PartitionSpec as P

GRAVITY = 9.81
TIME_STEP = 200.0
CELL_SIZE = 5500.0
LOWEST_FREQ = 0.0418
FREQ_GROWTH = 1.1
WIND_GROWTH = 0.0003
TURN_LIMIT = 0.9

TILE = 8
CELLS = TILE * TILE
GROUP = 256
HALF = 128
EDGE = 128
LANES = 128
VMEM_BYTES = 24 * 1024 * 1024

F32 = jnp.float32
BF16 = jnp.bfloat16
I32 = jnp.int32


def iota(shape, dim):
    return lax.broadcasted_iota(I32, shape, dim)


def onehot(mask):
    return jnp.where(mask, 1.0, 0.0).astype(BF16)


def dot(a, b):
    return jnp.dot(a, b, preferred_element_type=F32)


def dot_nt(a, b):
    return lax.dot_general(a, b, (((1,), (1,)), ((), ())), preferred_element_type=F32)


def dispersion(radian_freq, water_depth):
    deep_kh = radian_freq * radian_freq / GRAVITY * water_depth
    wave_kh = deep_kh / jnp.sqrt(jnp.tanh(deep_kh))
    return wave_kh


def radian_rows(freq_local, width):
    index = iota((freq_local, width), 0) + lax.axis_index("spec") * freq_local
    return (2.0 * math.pi * LOWEST_FREQ) * jnp.exp(index.astype(F32) * math.log(FREQ_GROWTH))


def angle_table(angles, width):
    values = iota((angles, width), 0).astype(F32) * (2.0 * math.pi / angles)
    return jnp.cos(values), jnp.sin(values)


def place_of(point):
    block = point // CELLS
    row = (point // TILE) % TILE
    col = point % TILE
    inner = (row >= 1) & (row <= 6) & (col >= 1) & (col <= 6)
    rank = (row - 1) * 6 + jnp.clip(col - 1, 0, 6)
    early = inner & (rank < 32)
    before = jnp.clip(rank, 0, 32)
    return jnp.where(early, block * 32 + rank, HALF + block * 32 + point % CELLS - before)


def edge_columns(width):
    source = iota((2 * width, EDGE), 0)
    upright = source // width
    point = source % width
    block = point // CELLS
    row = (point // TILE) % TILE
    col = point % TILE
    across = jnp.where(upright == 0, col, row)
    along = jnp.where(upright == 0, row, col)
    edge = upright * 64 + jnp.where(across == 0, 0, 32) + block * TILE + along
    on_edge = (across == 0) | (across == TILE - 1)
    return onehot(on_edge & (edge == iota((2 * width, EDGE), 1)))


def fetch(sources, targets, sems, first=0):
    copies = [
        pltpu.make_async_copy(source, target, sems.at[first + k])
        for k, (source, target) in enumerate(zip(sources, targets))
    ]
    for copy in copies:
        copy.start()
    return copies


def request_kernel(capacity, coded_ref, request_ref):
    peers = request_ref.shape[0]
    faces = coded_ref.shape[1]
    mine = lax.axis_index("blk")
    owner, block = coded_ref[...] // 256, coded_ref[...] % 256
    peer = iota((peers, faces), 0)
    asked = (owner == peer) & (peer != mine)
    earlier = onehot(iota((faces, faces), 0) < iota((faces, faces), 1))
    rank = dot(onehot(asked), earlier).astype(I32)
    side = iota((1, faces), 1) % 4
    base = (block // 4) * EDGE + (side // 2) * 64 + (1 - side % 2) * 32 + (block % 4) * TILE + 1
    base = base.astype(F32)
    lane = iota((peers, LANES), 1)
    result = jnp.zeros((peers, LANES), F32)
    for k in range(capacity):
        found = jnp.sum(jnp.where(asked & (rank == k), base, 0.0), axis=1, keepdims=True)
        result = jnp.where(lane == k, found, result)
    result = result.astype(I32)
    for p in range(peers):
        request_ref[p] = result[p : p + 1]


def select_kernel(capacity, request_ref, high_ref, reply_ref):
    peers = request_ref.shape[0]
    rows = peers * capacity * TILE
    edges = high_ref.shape[1]
    asked = jnp.concatenate([request_ref[p] for p in range(peers)], axis=0)
    coarse = (asked // 16).astype(F32).astype(BF16)
    fine = (asked % 16).astype(F32).astype(BF16)
    spread = onehot(iota((rows, peers), 0) // (capacity * TILE) == iota((rows, peers), 1))
    asked = 16.0 * dot(spread, coarse) + dot(spread, fine)
    row = iota((rows, LANES), 0)
    slot = (row // TILE) % capacity
    chosen = (slot == iota((rows, LANES), 1)) & (asked > 0.0)
    target = jnp.sum(
        jnp.where(chosen, asked + (row % TILE).astype(F32), 0.0), axis=1, keepdims=True
    )
    pick = onehot(iota((rows, edges), 1).astype(F32) + 1.0 == target)
    reply = dot_nt(pick, high_ref[...]).astype(BF16)
    for p in range(peers):
        reply_ref[p] = reply[p * capacity * TILE : (p + 1) * capacity * TILE]


def set_speeds(depth_ref, wet_ref, current_ref, group_ref, drift_ref):
    radian_freq = radian_rows(*group_ref.shape)
    depth = depth_ref[...]
    wave_kh = dispersion(radian_freq, depth)
    decay_two = jnp.exp(-2.0 * wave_kh)
    denom = 1.0 - decay_two * decay_two
    ratio = 4.0 * wave_kh * decay_two / denom
    phase = radian_freq * depth / wave_kh
    wet = wet_ref[...].astype(F32) * (TIME_STEP / CELL_SIZE)
    group_ref[...] = 0.5 * (1.0 + ratio) * phase * wet
    drift_ref[0:1, :] = current_ref[0:1, :] * wet
    drift_ref[1:2, :] = current_ref[1:2, :] * wet
    return 2.0 * radian_freq * decay_two / denom


def sides(angles):
    lane = iota((angles, LANES), 1)
    col = lane % TILE
    row = (lane // TILE) % TILE
    return col == 0, col == TILE - 1, row == 0, row == TILE - 1


def transport_kernel(after_ref, spec_ref, depth_ref, current_ref, slope_ref, wet_ref, *refs):
    moved_ref, high_ref, low_ref, early_ref, flux_ref, group_ref, turn_x_ref, turn_y_ref, drift_ref = refs
    freq_local, angles, points = moved_ref.shape
    cosine, sine = angle_table(angles, LANES)
    west, east, south, north = sides(angles)
    turn = set_speeds(depth_ref, wet_ref, current_ref, group_ref, drift_ref)
    turn = turn * (TIME_STEP / (2.0 * math.pi / angles))
    turn_x_ref[...] = turn * slope_ref[0:1, :]
    turn_y_ref[...] = turn * slope_ref[1:2, :]
    columns = edge_columns(GROUP)
    inner = onehot(place_of(iota((GROUP, HALF), 0)) == iota((GROUP, HALF), 1))

    def one_group(g, carry):
        for half in range(GROUP // LANES):
            part = pl.ds(pl.multiple_of(g * GROUP + half * LANES, LANES), LANES)
            here = slice(half * LANES, (half + 1) * LANES)
            there = slice(GROUP + half * LANES, GROUP + (half + 1) * LANES)
            drift_x = jnp.broadcast_to(drift_ref[0:1, part], (angles, LANES))
            drift_y = jnp.broadcast_to(drift_ref[1:2, part], (angles, LANES))
            for f in range(freq_local):
                energy = spec_ref[f, :, part]
                speed = jnp.broadcast_to(group_ref[f : f + 1, part], (angles, LANES))
                turn_x = jnp.broadcast_to(turn_x_ref[f : f + 1, part], (angles, LANES))
                turn_y = jnp.broadcast_to(turn_y_ref[f : f + 1, part], (angles, LANES))
                flow_x = (speed * cosine + drift_x) * energy
                flow_y = (speed * sine + drift_y) * energy
                turning = jnp.clip(sine * turn_x - cosine * turn_y, -TURN_LIMIT, TURN_LIMIT)
                flow_t = turning * energy
                right = jnp.maximum(flow_x, 0.0)
                left = right - flow_x
                up = jnp.maximum(flow_y, 0.0)
                down = up - flow_y
                ahead = jnp.maximum(flow_t, 0.0)
                back = ahead - flow_t
                total = energy - (right + left) - (up + down) - (ahead + back)
                total = total + pltpu.roll(jnp.where(east, 0.0, right), 1, 1)
                total = total + pltpu.roll(jnp.where(west, 0.0, left), LANES - 1, 1)
                total = total + pltpu.roll(jnp.where(north, 0.0, up), TILE, 1)
                total = total + pltpu.roll(jnp.where(south, 0.0, down), LANES - TILE, 1)
                total = total + pltpu.roll(ahead, 1, 0) + pltpu.roll(back, angles - 1, 0)
                moved_ref[f, :, part] = total
                flux_ref[f, :, here] = jnp.where(east, right, left)
                flux_ref[f, :, there] = jnp.where(north, up, down)
        flux = flux_ref[...].reshape(freq_local * angles, 2 * GROUP)
        high = flux.astype(BF16)
        low = (flux - high.astype(F32)).astype(BF16)
        place = pl.ds(pl.multiple_of(g * EDGE, EDGE), EDGE)
        high_ref[:, place] = dot(high, columns).astype(BF16)
        low_ref[:, place] = dot(low, columns).astype(BF16)
        part = pl.ds(pl.multiple_of(g * GROUP, GROUP), GROUP)
        for j in range(angles // 8):
            levels = moved_ref[:, 8 * j : 8 * j + 8, part].reshape(freq_local * 8, GROUP).astype(BF16)
            early_ref[j, :, place] = dot(levels, inner).astype(BF16)
        return carry

    lax.fori_loop(0, points // GROUP, one_group, 0)


def local_kernel(capacity, coded_ref, high_ref, low_ref, moved_in_ref, *refs):
    *moved_refs, map_ref = refs
    freq_local, angles, points = moved_in_ref.shape
    each = moved_refs[0].shape[2] // GROUP
    ranks = face_ranks(coded_ref)
    for g in range(points // GROUP):
        part = slice(g * GROUP, (g + 1) * GROUP)
        pick, reply_map = inflow_maps(capacity, g, ranks, high_ref.shape[1], map_ref.shape[0])
        map_ref[:, part] = reply_map
        inflow = dot(high_ref[...], pick) + dot(low_ref[...], pick)
        here = slice(g % each * GROUP, (g % each + 1) * GROUP)
        moved_refs[g // each][:, :, here] = moved_in_ref[:, :, part] + inflow.reshape(
            freq_local, angles, GROUP
        )


def face_ranks(coded_ref):
    faces = coded_ref.shape[1]
    owner, block = coded_ref[...] // 256, coded_ref[...] % 256
    by_column = jnp.broadcast_to(owner, (faces, faces))
    below = iota((faces, faces), 0)
    right = iota((faces, faces), 1)
    by_row = jnp.sum(jnp.where(below == right, by_column, 0).astype(F32), axis=1, keepdims=True)
    equal = (by_row == by_column.astype(F32)) & (below < right)
    rank = jnp.sum(jnp.where(equal, 1.0, 0.0), axis=0, keepdims=True)
    return jnp.concatenate(
        [block.astype(F32), owner.astype(F32), rank, jnp.zeros((5, faces), F32)], axis=0
    ).astype(BF16)


def inflow_maps(capacity, group, table, edges, rows):
    faces = table.shape[1]
    width = GROUP
    mine = lax.axis_index("blk")
    point = iota((faces, width), 1)
    block = point // CELLS + group * (width // CELLS)
    col = point % TILE
    row = (point // TILE) % TILE
    face = iota((faces, width), 0)
    at_x = dot(table, onehot((face == block * 4 + jnp.where(col == 0, 0, 1)))).astype(I32)
    at_y = dot(table, onehot((face == block * 4 + jnp.where(row == 0, 2, 3)))).astype(I32)
    point = iota((1, width), 1)
    col = point % TILE
    row = (point // TILE) % TILE

    def ids(found, across, along, upright):
        edge = (across == 0) | (across == TILE - 1)
        from_block, from_owner, slot = found[0:1], found[1:2], found[2:3]
        local = edge & (from_owner == mine)
        remote = edge & (from_owner != mine)
        base = upright * 64 + jnp.where(across == 0, 32, 0)
        source = (from_block // 4) * EDGE + base + (from_block % 4) * TILE + along
        reply = (from_owner * capacity + slot) * TILE + along
        return jnp.where(local, source, -1), jnp.where(remote, reply, -1)

    source_x, reply_x = ids(at_x, col, row, 0)
    source_y, reply_y = ids(at_y, row, col, 1)
    line = iota((rows, width), 0)
    reply_map = onehot((line == reply_x) | (line == reply_y))
    line = iota((edges, width), 0)
    return onehot((line == source_x) | (line == source_y)), reply_map


def weights_kernel(freq_ref, angle_ref, shift_ref, spread_ref, image_ref, back_ref):
    freqs = freq_ref.shape[1]
    angles = angle_ref.shape[2]
    wide = freqs * 8
    own = spread_ref.shape[0]
    start = lax.axis_index("spec") * (own // 8)
    rows = onehot((iota((wide, freqs), 0) // 8 + start) % freqs == iota((wide, freqs), 1))
    same = iota((wide, wide), 0) % 8 == iota((wide, wide), 1) % 8
    for s in range(2):
        weights = freq_ref[s]
        left = dot(rows, weights).astype(BF16)
        shift_ref[s * wide : (s + 1) * wide, :] = jnp.where(same, dot_nt(left, rows), 0.0).astype(BF16)
        turned = dot_nt(rows[:own], weights).astype(BF16)
        spread_ref[:, s * wide : (s + 1) * wide] = jnp.where(
            same[:own], dot_nt(turned, rows), 0.0
        ).astype(BF16)
    stacked = jnp.concatenate(
        [angle_ref[m, s].astype(F32) for m in range(2) for s in range(2)], axis=0
    ).astype(BF16)
    lines = angles * 4
    r = iota((4 * lines, 4 * angles), 0)
    c = iota((4 * lines, 4 * angles), 1)
    direction = (r // 32) % (angles // 8) * 8 + r % 8
    chosen = onehot((r // lines) * angles + direction == c)
    lines_rows = dot(chosen, stacked).astype(BF16)
    r = iota((2 * lines, angles), 0)
    column = onehot((r // 32) % (angles // 8) * 8 + r % 8 == iota((2 * lines, angles), 1))
    r = iota((4 * lines, 2 * lines), 0)
    c = iota((4 * lines, 2 * lines), 1)
    keep = ((r // lines) % 2 == c // lines) & ((r // 8) % 4 == (c // 8) % 4)
    image_ref[...] = jnp.where(keep, dot_nt(lines_rows, column), 0.0).astype(BF16)
    for s in range(2):
        r = iota((2 * lines, 4 * angles), 0)
        c = iota((2 * lines, 4 * angles), 1)
        direction = (r // 32) % (angles // 8) * 8 + r % 8
        chosen = onehot(((r // lines) * 2 + s) * angles + direction == c)
        lines_rows = dot(chosen, stacked).astype(BF16)
        r = iota((lines, 2 * lines), 0)
        c = iota((lines, 2 * lines), 1)
        keep = (r // 8) % 4 == (c // 8) % 4
        back_ref[s * lines : (s + 1) * lines, :] = jnp.where(
            keep, dot_nt(column[:lines], lines_rows), 0.0
        ).astype(BF16)


def turned_late_kernel(first, reply_ref, map_ref, moved_in_ref, *refs):
    moved_ref, late_ref, turned_ref = refs[-3:]
    freq_local, angles, points = moved_ref.shape
    reply = reply_ref[...].astype(F32).reshape(map_ref.shape[0], freq_local * angles)
    turned_ref[...] = reply.T.astype(BF16)
    late_kernel(first, turned_ref, map_ref, moved_in_ref, moved_ref, late_ref)


def late_kernel(first, turned_ref, map_ref, moved_in_ref, *refs):
    moved_ref, late_ref = refs[-2:]
    freq_local, angles, points = moved_ref.shape
    outer = onehot(place_of(iota((GROUP, HALF), 0)) == iota((GROUP, HALF), 1) + HALF)
    for k in range(points // GROUP):
        here = slice(k * GROUP, (k + 1) * GROUP)
        inflow = dot(turned_ref[...], map_ref[:, (first + k) * GROUP : (first + k + 1) * GROUP])
        moved_ref[:, :, here] = moved_in_ref[:, :, here] + inflow.reshape(freq_local, angles, GROUP)
        for j in range(angles // 8):
            levels = moved_ref[:, 8 * j : 8 * j + 8, here].reshape(freq_local * 8, GROUP)
            late_ref[j, :, k * HALF : (k + 1) * HALF] = dot(levels.astype(BF16), outer).astype(BF16)


def nonlinear_tile(level_refs, shift_ref, spread_ref, image_ref, back_ref, rate_ref, shifted_ref, gained_ref):
    parts, own, width = level_refs[0].shape
    wide = shift_ref.shape[1]
    freqs = wide // 8
    lines = parts * 32
    start = lax.axis_index("spec") * (own // 8)
    levels = jnp.concatenate(
        [jnp.concatenate([ref[j] for ref in level_refs], axis=0) for j in range(parts)], axis=1
    )
    for s in range(2):
        rows = slice(s * wide, (s + 1) * wide)
        shifted_ref[rows, :] = dot(shift_ref[rows, :], levels).astype(BF16)
    group = 2 if width <= 256 else 1

    def beside(pieces):
        return jnp.concatenate(pieces, axis=1)

    def image_of(q):
        shifted = beside(
            [
                jnp.concatenate(
                    [
                        shifted_ref[
                            s * wide + 32 * k : s * wide + 32 * k + 32, j * width : (j + 1) * width
                        ]
                        for s in range(2)
                        for j in range(parts)
                    ],
                    axis=0,
                )
                for k in range(q, q + group)
            ]
        )
        return [dot(image_ref[2 * m * lines : 2 * (m + 1) * lines, :], shifted) for m in range(2)]

    doubled = []
    coming = image_of(0)
    for q in range(0, freqs // 4, group):
        images = coming
        if q + group < freqs // 4:
            coming = image_of(q + group)
        lows = []
        for side, k in enumerate(range(q, q + group)):
            source, place = divmod(k * 32, own)
            here = slice(side * width, (side + 1) * width)
            level = jnp.concatenate(
                [level_refs[source][j, place : place + 32, :].astype(F32) for j in range(parts)], axis=0
            )
            rates = [rate_ref[(start + 4 * k + i) % freqs] for i in range(4)]
            scaled = jnp.concatenate(
                [
                    level[32 * j + 8 * i : 32 * j + 8 * i + 8] * rates[i]
                    for j in range(parts)
                    for i in range(4)
                ],
                axis=0,
            )
            deltas = []
            for m in range(2):
                plus = images[m][:lines, here]
                minus = images[m][lines:, here]
                deltas.append(scaled * (level * (plus + minus) - 2.0 * plus * minus))
            lows.append(jnp.concatenate(deltas, axis=0).astype(BF16))
            if source == 0:
                doubled.append(deltas[0] + deltas[1])
        low = beside(lows)
        for s in range(2):
            back = dot(back_ref[s * lines : (s + 1) * lines, :], low).astype(BF16)
            for side, k in enumerate(range(q, q + group)):
                for j in range(parts):
                    gained_ref[
                        s * wide + 32 * k : s * wide + 32 * k + 32, j * width : (j + 1) * width
                    ] = back[32 * j : 32 * j + 32, side * width : (side + 1) * width]
    spread = [
        dot(spread_ref[:, s * wide : (s + 1) * wide], gained_ref[s * wide : (s + 1) * wide, :])
        for s in range(2)
    ]
    result = []
    for j in range(parts):
        here = slice(j * width, (j + 1) * width)
        lost = jnp.concatenate([d[32 * j : 32 * j + 32] for d in doubled], axis=0)
        result.append(spread[0][:, here] + spread[1][:, here] - 2.0 * lost)
    return result


def put_back(values, where):
    stacked = jnp.concatenate(values, axis=0)
    high = stacked.astype(BF16)
    low = (stacked - high.astype(F32)).astype(BF16)
    return dot(jnp.concatenate([high, low], axis=1), where)


def places(first):
    position = iota((2 * HALF, GROUP), 0) % HALF + first
    return onehot(position == place_of(iota((2 * HALF, GROUP), 1)))


def early_kernel(sources, *refs):
    shift_ref, spread_ref, image_ref, back_ref, rate_ref = refs[sources : sources + 5]
    out_ref, shifted_ref, gained_ref = refs[-3:]
    result = nonlinear_tile(
        refs[:sources], shift_ref, spread_ref, image_ref, back_ref, rate_ref, shifted_ref, gained_ref
    )
    where = places(0)
    for k in range(out_ref.shape[1] // GROUP):
        values = [values[:, k * HALF : (k + 1) * HALF] for values in result]
        out_ref[:, k * GROUP : (k + 1) * GROUP] = put_back(values, where)


def final_kernel(sources, first, *refs):
    levels = refs[:sources]
    shift_ref, spread_ref, image_ref, back_ref, rate_ref = refs[sources : sources + 5]
    early_ref, moved_ref, depth_hbm, wind_hbm, wet_hbm = refs[sources + 5 : sources + 10]
    out_hbm, shifted_ref, gained_ref, late_ref, gain_ref, depth_ref, wind_ref, wet_ref, out_ref, sems = (
        refs[-10:]
    )
    small = fetch([depth_hbm, wind_hbm, wet_hbm], [depth_ref, wind_ref, wet_ref], sems)
    late = nonlinear_tile(
        levels, shift_ref, spread_ref, image_ref, back_ref, rate_ref, shifted_ref, gained_ref
    )
    for j, values in enumerate(late):
        late_ref[j] = values
    freq_local, angles, _ = moved_ref.shape
    points = depth_ref.shape[1]
    groups = late_ref.shape[2] // HALF
    own = freq_local * 8
    for copy in small:
        copy.wait()
    radian_freq = radian_rows(freq_local, points)
    wave_kh = dispersion(radian_freq, depth_ref[...])
    gain_ref[...] = wave_kh / (radian_freq * depth_ref[...])
    scale = radian_freq[:, 0:LANES] * (TIME_STEP * WIND_GROWTH)
    cosine, sine = angle_table(angles, LANES)
    where = places(HALF)

    def result_copy(k):
        part = pl.ds(pl.multiple_of((first + k) * GROUP, GROUP), GROUP)
        here = pl.ds(pl.multiple_of(k * GROUP, GROUP), GROUP)
        return pltpu.make_async_copy(
            out_ref.at[:, :, here], out_hbm.at[:, :, part], sems.at[len(small) + k]
        )

    def one_group(k, carry):
        lanes = pl.ds(pl.multiple_of(k * HALF, HALF), HALF)
        transfer = put_back([late_ref[j, :, lanes] for j in range(angles // 8)], where)
        here = pl.ds(pl.multiple_of((first + k) * GROUP, GROUP), GROUP)
        transfer = transfer + early_ref[:, here]
        for half in range(GROUP // LANES):
            part = pl.ds(pl.multiple_of((first + k) * GROUP + half * LANES, LANES), LANES)
            place = pl.ds(pl.multiple_of(k * GROUP + half * LANES, LANES), LANES)
            here = slice(half * LANES, (half + 1) * LANES)
            wet = jnp.broadcast_to(wet_ref[:, part].astype(F32), (angles, LANES))
            along = wind_ref[0:1, part] * cosine + wind_ref[1:2, part] * sine
            for f in range(freq_local):
                slow = jnp.broadcast_to(gain_ref[f : f + 1, part], (angles, LANES))
                rise = jnp.broadcast_to(scale[f : f + 1, :], (angles, LANES))
                growth = rise * jnp.maximum(along * slow - 1.0, 0.0)
                moved = moved_ref[f, :, place]
                gained = jnp.concatenate(
                    [
                        transfer[j * own + 8 * f : j * own + 8 * f + 8, here]
                        for j in range(angles // 8)
                    ],
                    axis=0,
                )
                out_ref[f, :, place] = wet * (moved + gained + growth * moved)
        result_copy(k).start()
        return carry

    lax.fori_loop(0, groups, one_group, 0)
    for k in range(groups):
        result_copy(k).wait()


HBM = pl.BlockSpec(memory_space=pltpu.HBM)
VMEM = pl.BlockSpec(memory_space=pltpu.VMEM)
ANY = pl.BlockSpec(memory_space=pl.ANY)


def params():
    return pltpu.CompilerParams(vmem_limit_bytes=VMEM_BYTES)


def cost(flops, moved):
    return pl.CostEstimate(flops=int(flops), bytes_accessed=int(moved), transcendentals=0)


def shards(
    spectrum, depths, currents, slopes, wind_speed, wet_mask,
    face_owner, face_block, freq_weights, angle_weights, transfer_rate,
):
    freq_local, angles, points = spectrum.shape
    group_count = lax.axis_size("spec")
    peers = lax.axis_size("blk")
    faces = face_block.shape[0]
    freqs = freq_local * group_count
    groups = points // GROUP
    own = freq_local * 8
    parts = angles // 8
    rows_fd = freq_local * angles
    wide = freqs * 8
    lines = 4 * angles
    edges = groups * EDGE
    capacity = max(2, (faces // 2 + peers - 2) // (peers - 1))
    reply_rows = peers * capacity * TILE

    coded = face_owner.reshape(1, faces) * 256 + face_block.reshape(1, faces)
    depth_row = depths.reshape(1, points)
    wet_row = wet_mask.reshape(1, points)

    requests = pl.pallas_call(
        functools.partial(request_kernel, capacity),
        out_shape=jax.ShapeDtypeStruct((peers, 1, LANES), I32),
        compiler_params=params(),
        cost_estimate=cost(1e10, 4e7),
        name="requests",
    )(coded)
    asked = lax.all_to_all(requests, "blk", split_axis=0, concat_axis=0, tiled=True)

    moved_inner, high, low, early = pl.pallas_call(
        transport_kernel,
        in_specs=[ANY] + [VMEM] * 5,
        out_shape=[
            jax.ShapeDtypeStruct((freq_local, angles, points), F32),
            jax.ShapeDtypeStruct((rows_fd, edges), BF16),
            jax.ShapeDtypeStruct((rows_fd, edges), BF16),
            jax.ShapeDtypeStruct((parts, own, groups * HALF), BF16),
        ],
        scratch_shapes=[pltpu.VMEM((freq_local, angles, 2 * GROUP), F32)]
        + [pltpu.VMEM((freq_local, points), F32)] * 3
        + [pltpu.VMEM((2, points), F32)],
        compiler_params=params(),
        cost_estimate=cost(1e6, 1e5),
        name="transport",
    )(requests, spectrum, depth_row, currents, slopes, wet_row)

    reply = pl.pallas_call(
        functools.partial(select_kernel, capacity),
        out_shape=jax.ShapeDtypeStruct((peers, capacity * TILE, rows_fd), BF16),
        compiler_params=params(),
        cost_estimate=cost(1e6, 1e5),
        name="select",
    )(asked, high)
    replies = lax.all_to_all(reply, "blk", split_axis=0, concat_axis=0, tiled=True)

    weights = pl.pallas_call(
        weights_kernel,
        out_shape=[
            jax.ShapeDtypeStruct((2 * wide, wide), BF16),
            jax.ShapeDtypeStruct((own, 2 * wide), BF16),
            jax.ShapeDtypeStruct((4 * lines, 2 * lines), BF16),
            jax.ShapeDtypeStruct((2 * lines, 2 * lines), BF16),
        ],
        compiler_params=params(),
        cost_estimate=cost(1e6, 1e5),
        name="weights",
    )(freq_weights, angle_weights)

    def exchanged(array):
        return [
            lax.ppermute(
                array, "spec", [(s, (s - step) % group_count) for s in range(group_count)]
            )
            for step in range(1, group_count)
        ]

    early_levels = [early] + exchanged(early)

    halves = 2
    half_groups = groups // halves
    half_points = points // halves
    tile = half_groups * HALF
    half_wave = jax.ShapeDtypeStruct((freq_local, angles, half_points), F32)
    *moved_local, reply_map = pl.pallas_call(
        functools.partial(local_kernel, capacity),
        out_shape=[half_wave] * halves + [jax.ShapeDtypeStruct((reply_rows, points), BF16)],
        compiler_params=params(),
        cost_estimate=cost(1e6, 1e5),
        name="local_inflow",
    )(coded, high, low, moved_inner)

    weight_specs = [VMEM] * 4 + [pl.BlockSpec(memory_space=pltpu.SMEM)]
    moved, turned, late_levels, gained_early = [], None, [], None
    for h in range(halves):
        out = pl.pallas_call(
            functools.partial(late_kernel if h else turned_late_kernel, h * half_groups),
            in_specs=[VMEM] * 3 + [ANY] * h,
            out_shape=[half_wave, jax.ShapeDtypeStruct((parts, own, tile), BF16)]
            + [jax.ShapeDtypeStruct((rows_fd, reply_rows), BF16)] * (h == 0),
            input_output_aliases={2: 0},
            compiler_params=params(),
            cost_estimate=cost(1e6, 1e5),
            name=f"late_inflow_{h}",
        )(*([turned, reply_map, moved_local[h], gained_early] if h else [replies, reply_map, moved_local[h]]))
        moved.append(out[0])
        turned = turned if h else out[2]
        late_levels.append([out[1]] + exchanged(out[1]))
        if h == 0:
            gained_early = pl.pallas_call(
                functools.partial(early_kernel, group_count),
                in_specs=[VMEM] * group_count + weight_specs + [ANY],
                out_shape=jax.ShapeDtypeStruct((parts * own, points), F32),
                scratch_shapes=[pltpu.VMEM((2 * wide, parts * groups * HALF), BF16)] * 2,
                compiler_params=params(),
                cost_estimate=cost(1e6, 1e5),
                name="early_transfer",
            )(*early_levels, *weights, transfer_rate, turned)

    result = []
    for h in range(halves):
        operands = [
            *late_levels[h], *weights, transfer_rate, gained_early, moved[h],
            depth_row, wind_speed, wet_row, *result,
        ]
        result = [
            pl.pallas_call(
                functools.partial(final_kernel, group_count, h * half_groups),
                in_specs=[VMEM] * group_count
                + weight_specs
                + [VMEM, VMEM, HBM, HBM, HBM]
                + [HBM] * len(result),
                out_specs=HBM,
                out_shape=jax.ShapeDtypeStruct((freq_local, angles, points), F32),
                scratch_shapes=[pltpu.VMEM((2 * wide, parts * tile), BF16)] * 2
                + [
                    pltpu.VMEM((parts, own, tile), F32),
                    pltpu.VMEM((freq_local, points), F32),
                    pltpu.VMEM((1, points), F32),
                    pltpu.VMEM((2, points), F32),
                    pltpu.VMEM((1, points), I32),
                    pltpu.VMEM((freq_local, angles, half_groups * GROUP), F32),
                    pltpu.SemaphoreType.DMA((3 + half_groups,)),
                ],
                input_output_aliases={len(operands) - 1: 0} if result else {},
                compiler_params=params(),
                cost_estimate=cost(1e6, 1e5),
                name=f"late_transfer_{h}",
            )(*operands)
        ]
    return result[0]


def solution(mesh):
    in_specs = (
        P("spec", None, "blk"),
        P("blk"),
        P(None, "blk"),
        P(None, "blk"),
        P(None, "blk"),
        P("blk"),
        P("blk", None),
        P("blk"),
        P(),
        P(),
        P(),
    )
    out_specs = P("spec", None, "blk")
    return jax.shard_map(shards, mesh=mesh, in_specs=in_specs, out_specs=out_specs, check_vma=False)
```

```python
import functools
import math

import jax
import jax.numpy as jnp
from jax import lax
from jax.experimental import pallas as pl
from jax.experimental.pallas import tpu as pltpu
from jax.sharding import PartitionSpec as P

GRAVITY = 9.81
TIME_STEP = 200.0
CELL_SIZE = 5500.0
LOWEST_FREQ = 0.0418
FREQ_GROWTH = 1.1
WIND_GROWTH = 0.0003
TURN_LIMIT = 0.9

TILE = 8
CELLS = TILE * TILE
GROUP = 256
HALF = 128
EDGE = 128
LANES = 128
VMEM_BYTES = 24 * 1024 * 1024

F32 = jnp.float32
BF16 = jnp.bfloat16
I32 = jnp.int32


def iota(shape, dim):
    return lax.broadcasted_iota(I32, shape, dim)


def onehot(mask):
    return jnp.where(mask, 1.0, 0.0).astype(BF16)


def dot(a, b):
    return jnp.dot(a, b, preferred_element_type=F32)


def dot_nt(a, b):
    return lax.dot_general(a, b, (((1,), (1,)), ((), ())), preferred_element_type=F32)


def dispersion(radian_freq, water_depth):
    deep_kh = radian_freq * radian_freq / GRAVITY * water_depth
    wave_kh = deep_kh / jnp.sqrt(jnp.tanh(deep_kh))
    return wave_kh


def radian_rows(freq_local, width):
    index = iota((freq_local, width), 0) + lax.axis_index("spec") * freq_local
    return (2.0 * math.pi * LOWEST_FREQ) * jnp.exp(index.astype(F32) * math.log(FREQ_GROWTH))


def angle_table(angles, width):
    values = iota((angles, width), 0).astype(F32) * (2.0 * math.pi / angles)
    return jnp.cos(values), jnp.sin(values)


def place_of(point):
    block = point // CELLS
    row = (point // TILE) % TILE
    col = point % TILE
    inner = (row >= 1) & (row <= 6) & (col >= 1) & (col <= 6)
    rank = (row - 1) * 6 + jnp.clip(col - 1, 0, 6)
    early = inner & (rank < 32)
    before = jnp.clip(rank, 0, 32)
    return jnp.where(early, block * 32 + rank, HALF + block * 32 + point % CELLS - before)


def edge_columns(width):
    source = iota((2 * width, EDGE), 0)
    upright = source // width
    point = source % width
    block = point // CELLS
    row = (point // TILE) % TILE
    col = point % TILE
    across = jnp.where(upright == 0, col, row)
    along = jnp.where(upright == 0, row, col)
    edge = upright * 64 + jnp.where(across == 0, 0, 32) + block * TILE + along
    on_edge = (across == 0) | (across == TILE - 1)
    return onehot(on_edge & (edge == iota((2 * width, EDGE), 1)))


def fetch(sources, targets, sems, first=0):
    copies = [
        pltpu.make_async_copy(source, target, sems.at[first + k])
        for k, (source, target) in enumerate(zip(sources, targets))
    ]
    for copy in copies:
        copy.start()
    return copies


def request_kernel(capacity, coded_ref, request_ref):
    peers = request_ref.shape[0]
    faces = coded_ref.shape[1]
    mine = lax.axis_index("blk")
    owner, block = coded_ref[...] // 256, coded_ref[...] % 256
    peer = iota((peers, faces), 0)
    asked = (owner == peer) & (peer != mine)
    earlier = onehot(iota((faces, faces), 0) < iota((faces, faces), 1))
    rank = dot(onehot(asked), earlier).astype(I32)
    side = iota((1, faces), 1) % 4
    base = (block // 4) * EDGE + (side // 2) * 64 + (1 - side % 2) * 32 + (block % 4) * TILE + 1
    base = base.astype(F32)
    lane = iota((peers, LANES), 1)
    result = jnp.zeros((peers, LANES), F32)
    for k in range(capacity):
        found = jnp.sum(jnp.where(asked & (rank == k), base, 0.0), axis=1, keepdims=True)
        result = jnp.where(lane == k, found, result)
    result = result.astype(I32)
    for p in range(peers):
        request_ref[p] = result[p : p + 1]


def select_kernel(capacity, request_ref, high_ref, reply_ref):
    peers = request_ref.shape[0]
    rows = peers * capacity * TILE
    edges = high_ref.shape[1]
    asked = jnp.concatenate([request_ref[p] for p in range(peers)], axis=0)
    coarse = (asked // 16).astype(F32).astype(BF16)
    fine = (asked % 16).astype(F32).astype(BF16)
    spread = onehot(iota((rows, peers), 0) // (capacity * TILE) == iota((rows, peers), 1))
    asked = 16.0 * dot(spread, coarse) + dot(spread, fine)
    row = iota((rows, LANES), 0)
    slot = (row // TILE) % capacity
    chosen = (slot == iota((rows, LANES), 1)) & (asked > 0.0)
    target = jnp.sum(
        jnp.where(chosen, asked + (row % TILE).astype(F32), 0.0), axis=1, keepdims=True
    )
    pick = onehot(iota((rows, edges), 1).astype(F32) + 1.0 == target)
    reply = dot_nt(pick, high_ref[...]).astype(BF16)
    for p in range(peers):
        reply_ref[p] = reply[p * capacity * TILE : (p + 1) * capacity * TILE]


def set_speeds(depth_ref, wet_ref, current_ref, group_ref, drift_ref):
    radian_freq = radian_rows(*group_ref.shape)
    depth = depth_ref[...]
    wave_kh = dispersion(radian_freq, depth)
    decay_two = jnp.exp(-2.0 * wave_kh)
    denom = 1.0 - decay_two * decay_two
    ratio = 4.0 * wave_kh * decay_two / denom
    phase = radian_freq * depth / wave_kh
    wet = wet_ref[...].astype(F32) * (TIME_STEP / CELL_SIZE)
    group_ref[...] = 0.5 * (1.0 + ratio) * phase * wet
    drift_ref[0:1, :] = current_ref[0:1, :] * wet
    drift_ref[1:2, :] = current_ref[1:2, :] * wet
    return 2.0 * radian_freq * decay_two / denom


def sides(angles):
    lane = iota((angles, LANES), 1)
    col = lane % TILE
    row = (lane // TILE) % TILE
    return col == 0, col == TILE - 1, row == 0, row == TILE - 1


def transport_kernel(after_ref, spec_ref, depth_ref, current_ref, slope_ref, wet_ref, *refs):
    *moved_refs, high_ref, low_ref, early_ref, flux_ref, group_ref, turn_x_ref, turn_y_ref, drift_ref = refs
    freq_local, angles, points = spec_ref.shape
    each = points // GROUP // len(moved_refs)
    cosine, sine = angle_table(angles, LANES)
    west, east, south, north = sides(angles)
    turn = set_speeds(depth_ref, wet_ref, current_ref, group_ref, drift_ref)
    turn = turn * (TIME_STEP / (2.0 * math.pi / angles))
    turn_x_ref[...] = turn * slope_ref[0:1, :]
    turn_y_ref[...] = turn * slope_ref[1:2, :]
    columns = edge_columns(GROUP)
    inner = onehot(place_of(iota((GROUP, HALF), 0)) == iota((GROUP, HALF), 1))

    def one_group(moved_ref, first, k, carry):
        g = first + k
        for half in range(GROUP // LANES):
            part = pl.ds(pl.multiple_of(g * GROUP + half * LANES, LANES), LANES)
            inside = pl.ds(pl.multiple_of(k * GROUP + half * LANES, LANES), LANES)
            here = slice(half * LANES, (half + 1) * LANES)
            there = slice(GROUP + half * LANES, GROUP + (half + 1) * LANES)
            drift_x = jnp.broadcast_to(drift_ref[0:1, part], (angles, LANES))
            drift_y = jnp.broadcast_to(drift_ref[1:2, part], (angles, LANES))
            for f in range(freq_local):
                energy = spec_ref[f, :, part]
                speed = jnp.broadcast_to(group_ref[f : f + 1, part], (angles, LANES))
                turn_x = jnp.broadcast_to(turn_x_ref[f : f + 1, part], (angles, LANES))
                turn_y = jnp.broadcast_to(turn_y_ref[f : f + 1, part], (angles, LANES))
                flow_x = (speed * cosine + drift_x) * energy
                flow_y = (speed * sine + drift_y) * energy
                turning = jnp.clip(sine * turn_x - cosine * turn_y, -TURN_LIMIT, TURN_LIMIT)
                flow_t = turning * energy
                right = jnp.maximum(flow_x, 0.0)
                left = right - flow_x
                up = jnp.maximum(flow_y, 0.0)
                down = up - flow_y
                ahead = jnp.maximum(flow_t, 0.0)
                back = ahead - flow_t
                total = energy - (right + left) - (up + down) - (ahead + back)
                total = total + pltpu.roll(jnp.where(east, 0.0, right), 1, 1)
                total = total + pltpu.roll(jnp.where(west, 0.0, left), LANES - 1, 1)
                total = total + pltpu.roll(jnp.where(north, 0.0, up), TILE, 1)
                total = total + pltpu.roll(jnp.where(south, 0.0, down), LANES - TILE, 1)
                total = total + pltpu.roll(ahead, 1, 0) + pltpu.roll(back, angles - 1, 0)
                moved_ref[f, :, inside] = total
                flux_ref[f, :, here] = jnp.where(east, right, left)
                flux_ref[f, :, there] = jnp.where(north, up, down)
        flux = flux_ref[...].reshape(freq_local * angles, 2 * GROUP)
        high = flux.astype(BF16)
        low = (flux - high.astype(F32)).astype(BF16)
        place = pl.ds(pl.multiple_of(g * EDGE, EDGE), EDGE)
        high_ref[:, place] = dot(high, columns).astype(BF16)
        low_ref[:, place] = dot(low, columns).astype(BF16)
        part = pl.ds(pl.multiple_of(k * GROUP, GROUP), GROUP)
        for j in range(angles // 8):
            levels = moved_ref[:, 8 * j : 8 * j + 8, part].reshape(freq_local * 8, GROUP).astype(BF16)
            early_ref[j, :, place] = dot(levels, inner).astype(BF16)
        return carry

    for h, moved_ref in enumerate(moved_refs):
        lax.fori_loop(0, each, functools.partial(one_group, moved_ref, h * each), 0)


def local_kernel(capacity, halves, coded_ref, high_ref, low_ref, *refs):
    sources, moved_refs, map_ref = refs[:halves], refs[halves : 2 * halves], refs[-1]
    freq_local, angles, points = sources[0].shape
    each = points // GROUP
    ranks = face_ranks(coded_ref)
    for g in range(each * halves):
        part = slice(g * GROUP, (g + 1) * GROUP)
        pick, reply_map = inflow_maps(capacity, g, ranks, high_ref.shape[1], map_ref.shape[0])
        map_ref[:, part] = reply_map
        inflow = dot(high_ref[...], pick) + dot(low_ref[...], pick)
        here = slice(g % each * GROUP, (g % each + 1) * GROUP)
        moved_refs[g // each][:, :, here] = sources[g // each][:, :, here] + inflow.reshape(
            freq_local, angles, GROUP
        )


def face_ranks(coded_ref):
    faces = coded_ref.shape[1]
    owner, block = coded_ref[...] // 256, coded_ref[...] % 256
    by_column = jnp.broadcast_to(owner, (faces, faces))
    below = iota((faces, faces), 0)
    right = iota((faces, faces), 1)
    by_row = jnp.sum(jnp.where(below == right, by_column, 0).astype(F32), axis=1, keepdims=True)
    equal = (by_row == by_column.astype(F32)) & (below < right)
    rank = jnp.sum(jnp.where(equal, 1.0, 0.0), axis=0, keepdims=True)
    return jnp.concatenate(
        [block.astype(F32), owner.astype(F32), rank, jnp.zeros((5, faces), F32)], axis=0
    ).astype(BF16)


def inflow_maps(capacity, group, table, edges, rows):
    faces = table.shape[1]
    width = GROUP
    mine = lax.axis_index("blk")
    point = iota((faces, width), 1)
    block = point // CELLS + group * (width // CELLS)
    col = point % TILE
    row = (point // TILE) % TILE
    face = iota((faces, width), 0)
    at_x = dot(table, onehot((face == block * 4 + jnp.where(col == 0, 0, 1)))).astype(I32)
    at_y = dot(table, onehot((face == block * 4 + jnp.where(row == 0, 2, 3)))).astype(I32)
    point = iota((1, width), 1)
    col = point % TILE
    row = (point // TILE) % TILE

    def ids(found, across, along, upright):
        edge = (across == 0) | (across == TILE - 1)
        from_block, from_owner, slot = found[0:1], found[1:2], found[2:3]
        local = edge & (from_owner == mine)
        remote = edge & (from_owner != mine)
        base = upright * 64 + jnp.where(across == 0, 32, 0)
        source = (from_block // 4) * EDGE + base + (from_block % 4) * TILE + along
        reply = (from_owner * capacity + slot) * TILE + along
        return jnp.where(local, source, -1), jnp.where(remote, reply, -1)

    source_x, reply_x = ids(at_x, col, row, 0)
    source_y, reply_y = ids(at_y, row, col, 1)
    line = iota((rows, width), 0)
    reply_map = onehot((line == reply_x) | (line == reply_y))
    line = iota((edges, width), 0)
    return onehot((line == source_x) | (line == source_y)), reply_map


def weights_kernel(freq_ref, angle_ref, shift_ref, spread_ref, image_ref, back_ref):
    freqs = freq_ref.shape[1]
    angles = angle_ref.shape[2]
    wide = freqs * 8
    own = spread_ref.shape[0]
    start = lax.axis_index("spec") * (own // 8)
    rows = onehot((iota((wide, freqs), 0) // 8 + start) % freqs == iota((wide, freqs), 1))
    same = iota((wide, wide), 0) % 8 == iota((wide, wide), 1) % 8
    for s in range(2):
        weights = freq_ref[s]
        left = dot(rows, weights).astype(BF16)
        shift_ref[s * wide : (s + 1) * wide, :] = jnp.where(same, dot_nt(left, rows), 0.0).astype(BF16)
        turned = dot_nt(rows[:own], weights).astype(BF16)
        spread_ref[:, s * wide : (s + 1) * wide] = jnp.where(
            same[:own], dot_nt(turned, rows), 0.0
        ).astype(BF16)
    stacked = jnp.concatenate(
        [angle_ref[m, s].astype(F32) for m in range(2) for s in range(2)], axis=0
    ).astype(BF16)
    lines = angles * 4
    r = iota((4 * lines, 4 * angles), 0)
    c = iota((4 * lines, 4 * angles), 1)
    direction = (r // 32) % (angles // 8) * 8 + r % 8
    chosen = onehot((r // lines) * angles + direction == c)
    lines_rows = dot(chosen, stacked).astype(BF16)
    r = iota((2 * lines, angles), 0)
    column = onehot((r // 32) % (angles // 8) * 8 + r % 8 == iota((2 * lines, angles), 1))
    r = iota((4 * lines, 2 * lines), 0)
    c = iota((4 * lines, 2 * lines), 1)
    keep = ((r // lines) % 2 == c // lines) & ((r // 8) % 4 == (c // 8) % 4)
    image_ref[...] = jnp.where(keep, dot_nt(lines_rows, column), 0.0).astype(BF16)
    for s in range(2):
        r = iota((2 * lines, 4 * angles), 0)
        c = iota((2 * lines, 4 * angles), 1)
        direction = (r // 32) % (angles // 8) * 8 + r % 8
        chosen = onehot(((r // lines) * 2 + s) * angles + direction == c)
        lines_rows = dot(chosen, stacked).astype(BF16)
        r = iota((lines, 2 * lines), 0)
        c = iota((lines, 2 * lines), 1)
        keep = (r // 8) % 4 == (c // 8) % 4
        back_ref[s * lines : (s + 1) * lines, :] = jnp.where(
            keep, dot_nt(column[:lines], lines_rows), 0.0
        ).astype(BF16)


def turned_late_kernel(first, reply_ref, map_ref, moved_in_ref, *refs):
    moved_ref, late_ref, turned_ref = refs[-3:]
    freq_local, angles, points = moved_ref.shape
    reply = reply_ref[...].astype(F32).reshape(map_ref.shape[0], freq_local * angles)
    turned_ref[...] = reply.T.astype(BF16)
    late_kernel(first, turned_ref, map_ref, moved_in_ref, moved_ref, late_ref)


def late_kernel(first, turned_ref, map_ref, moved_in_ref, *refs):
    moved_ref, late_ref = refs[-2:]
    freq_local, angles, points = moved_ref.shape
    outer = onehot(place_of(iota((GROUP, HALF), 0)) == iota((GROUP, HALF), 1) + HALF)
    for k in range(points // GROUP):
        here = slice(k * GROUP, (k + 1) * GROUP)
        inflow = dot(turned_ref[...], map_ref[:, (first + k) * GROUP : (first + k + 1) * GROUP])
        moved_ref[:, :, here] = moved_in_ref[:, :, here] + inflow.reshape(freq_local, angles, GROUP)
        for j in range(angles // 8):
            levels = moved_ref[:, 8 * j : 8 * j + 8, here].reshape(freq_local * 8, GROUP)
            late_ref[j, :, k * HALF : (k + 1) * HALF] = dot(levels.astype(BF16), outer).astype(BF16)


def nonlinear_tile(level_refs, shift_ref, spread_ref, image_ref, back_ref, rate_ref, shifted_ref, gained_ref):
    parts, own, width = level_refs[0].shape
    wide = shift_ref.shape[1]
    freqs = wide // 8
    lines = parts * 32
    start = lax.axis_index("spec") * (own // 8)
    levels = jnp.concatenate(
        [jnp.concatenate([ref[j] for ref in level_refs], axis=0) for j in range(parts)], axis=1
    )
    for s in range(2):
        rows = slice(s * wide, (s + 1) * wide)
        shifted_ref[rows, :] = dot(shift_ref[rows, :], levels).astype(BF16)
    group = 2 if width <= 256 else 1

    def beside(pieces):
        return jnp.concatenate(pieces, axis=1)

    def image_of(q):
        shifted = beside(
            [
                jnp.concatenate(
                    [
                        shifted_ref[
                            s * wide + 32 * k : s * wide + 32 * k + 32, j * width : (j + 1) * width
                        ]
                        for s in range(2)
                        for j in range(parts)
                    ],
                    axis=0,
                )
                for k in range(q, q + group)
            ]
        )
        return [dot(image_ref[2 * m * lines : 2 * (m + 1) * lines, :], shifted) for m in range(2)]

    doubled = []
    coming = image_of(0)
    for q in range(0, freqs // 4, group):
        images = coming
        if q + group < freqs // 4:
            coming = image_of(q + group)
        lows = []
        for side, k in enumerate(range(q, q + group)):
            source, place = divmod(k * 32, own)
            here = slice(side * width, (side + 1) * width)
            level = jnp.concatenate(
                [level_refs[source][j, place : place + 32, :].astype(F32) for j in range(parts)], axis=0
            )
            rates = [rate_ref[(start + 4 * k + i) % freqs] for i in range(4)]
            scaled = jnp.concatenate(
                [
                    level[32 * j + 8 * i : 32 * j + 8 * i + 8] * rates[i]
                    for j in range(parts)
                    for i in range(4)
                ],
                axis=0,
            )
            deltas = []
            for m in range(2):
                plus = images[m][:lines, here]
                minus = images[m][lines:, here]
                deltas.append(scaled * (level * (plus + minus) - 2.0 * plus * minus))
            lows.append(jnp.concatenate(deltas, axis=0).astype(BF16))
            if source == 0:
                doubled.append(deltas[0] + deltas[1])
        low = beside(lows)
        for s in range(2):
            back = dot(back_ref[s * lines : (s + 1) * lines, :], low).astype(BF16)
            for side, k in enumerate(range(q, q + group)):
                for j in range(parts):
                    gained_ref[
                        s * wide + 32 * k : s * wide + 32 * k + 32, j * width : (j + 1) * width
                    ] = back[32 * j : 32 * j + 32, side * width : (side + 1) * width]
    spread = [
        dot(spread_ref[:, s * wide : (s + 1) * wide], gained_ref[s * wide : (s + 1) * wide, :])
        for s in range(2)
    ]
    result = []
    for j in range(parts):
        here = slice(j * width, (j + 1) * width)
        lost = jnp.concatenate([d[32 * j : 32 * j + 32] for d in doubled], axis=0)
        result.append(spread[0][:, here] + spread[1][:, here] - 2.0 * lost)
    return result


def put_back(values, where):
    stacked = jnp.concatenate(values, axis=0)
    high = stacked.astype(BF16)
    low = (stacked - high.astype(F32)).astype(BF16)
    return dot(jnp.concatenate([high, low], axis=1), where)


def places(first):
    position = iota((2 * HALF, GROUP), 0) % HALF + first
    return onehot(position == place_of(iota((2 * HALF, GROUP), 1)))


def early_kernel(sources, *refs):
    shift_ref, spread_ref, image_ref, back_ref, rate_ref = refs[sources : sources + 5]
    out_ref, shifted_ref, gained_ref = refs[-3:]
    result = nonlinear_tile(
        refs[:sources], shift_ref, spread_ref, image_ref, back_ref, rate_ref, shifted_ref, gained_ref
    )
    where = places(0)
    for k in range(out_ref.shape[1] // GROUP):
        values = [values[:, k * HALF : (k + 1) * HALF] for values in result]
        out_ref[:, k * GROUP : (k + 1) * GROUP] = put_back(values, where)


def final_kernel(sources, first, *refs):
    levels = refs[:sources]
    shift_ref, spread_ref, image_ref, back_ref, rate_ref = refs[sources : sources + 5]
    early_ref, moved_ref, depth_hbm, wind_hbm, wet_hbm = refs[sources + 5 : sources + 10]
    out_hbm, shifted_ref, gained_ref, late_ref, gain_ref, depth_ref, wind_ref, wet_ref, out_ref, sems = (
        refs[-10:]
    )
    small = fetch([depth_hbm, wind_hbm, wet_hbm], [depth_ref, wind_ref, wet_ref], sems)
    late = nonlinear_tile(
        levels, shift_ref, spread_ref, image_ref, back_ref, rate_ref, shifted_ref, gained_ref
    )
    for j, values in enumerate(late):
        late_ref[j] = values
    freq_local, angles, _ = moved_ref.shape
    points = depth_ref.shape[1]
    groups = late_ref.shape[2] // HALF
    own = freq_local * 8
    for copy in small:
        copy.wait()
    radian_freq = radian_rows(freq_local, points)
    wave_kh = dispersion(radian_freq, depth_ref[...])
    gain_ref[...] = wave_kh / (radian_freq * depth_ref[...])
    scale = radian_freq[:, 0:LANES] * (TIME_STEP * WIND_GROWTH)
    cosine, sine = angle_table(angles, LANES)
    where = places(HALF)

    def result_copy(k):
        part = pl.ds(pl.multiple_of((first + k) * GROUP, GROUP), GROUP)
        here = pl.ds(pl.multiple_of(k * GROUP, GROUP), GROUP)
        return pltpu.make_async_copy(
            out_ref.at[:, :, here], out_hbm.at[:, :, part], sems.at[len(small) + k]
        )

    def one_group(k, carry):
        lanes = pl.ds(pl.multiple_of(k * HALF, HALF), HALF)
        transfer = put_back([late_ref[j, :, lanes] for j in range(angles // 8)], where)
        here = pl.ds(pl.multiple_of((first + k) * GROUP, GROUP), GROUP)
        transfer = transfer + early_ref[:, here]
        for half in range(GROUP // LANES):
            part = pl.ds(pl.multiple_of((first + k) * GROUP + half * LANES, LANES), LANES)
            place = pl.ds(pl.multiple_of(k * GROUP + half * LANES, LANES), LANES)
            here = slice(half * LANES, (half + 1) * LANES)
            wet = jnp.broadcast_to(wet_ref[:, part].astype(F32), (angles, LANES))
            along = wind_ref[0:1, part] * cosine + wind_ref[1:2, part] * sine
            for f in range(freq_local):
                slow = jnp.broadcast_to(gain_ref[f : f + 1, part], (angles, LANES))
                rise = jnp.broadcast_to(scale[f : f + 1, :], (angles, LANES))
                growth = rise * jnp.maximum(along * slow - 1.0, 0.0)
                moved = moved_ref[f, :, place]
                gained = jnp.concatenate(
                    [
                        transfer[j * own + 8 * f : j * own + 8 * f + 8, here]
                        for j in range(angles // 8)
                    ],
                    axis=0,
                )
                out_ref[f, :, place] = wet * (moved + gained + growth * moved)
        result_copy(k).start()
        return carry

    lax.fori_loop(0, groups, one_group, 0)
    for k in range(groups):
        result_copy(k).wait()


HBM = pl.BlockSpec(memory_space=pltpu.HBM)
VMEM = pl.BlockSpec(memory_space=pltpu.VMEM)
ANY = pl.BlockSpec(memory_space=pl.ANY)


def params():
    return pltpu.CompilerParams(vmem_limit_bytes=VMEM_BYTES)


def cost(flops, moved):
    return pl.CostEstimate(flops=int(flops), bytes_accessed=int(moved), transcendentals=0)


def shards(
    spectrum, depths, currents, slopes, wind_speed, wet_mask,
    face_owner, face_block, freq_weights, angle_weights, transfer_rate,
):
    freq_local, angles, points = spectrum.shape
    group_count = lax.axis_size("spec")
    peers = lax.axis_size("blk")
    faces = face_block.shape[0]
    freqs = freq_local * group_count
    groups = points // GROUP
    own = freq_local * 8
    parts = angles // 8
    rows_fd = freq_local * angles
    wide = freqs * 8
    lines = 4 * angles
    edges = groups * EDGE
    capacity = max(2, (faces // 2 + peers - 2) // (peers - 1))
    reply_rows = peers * capacity * TILE

    coded = face_owner.reshape(1, faces) * 256 + face_block.reshape(1, faces)
    depth_row = depths.reshape(1, points)
    wet_row = wet_mask.reshape(1, points)

    requests = pl.pallas_call(
        functools.partial(request_kernel, capacity),
        out_shape=jax.ShapeDtypeStruct((peers, 1, LANES), I32),
        compiler_params=params(),
        cost_estimate=cost(1e10, 4e7),
        name="requests",
    )(coded)
    asked = lax.all_to_all(requests, "blk", split_axis=0, concat_axis=0, tiled=True)

    halves = 2
    half_groups = groups // halves
    half_points = points // halves
    tile = half_groups * HALF
    half_wave = jax.ShapeDtypeStruct((freq_local, angles, half_points), F32)
    *moved_inner, high, low, early = pl.pallas_call(
        transport_kernel,
        in_specs=[ANY] + [VMEM] * 5,
        out_shape=[half_wave] * halves
        + [
            jax.ShapeDtypeStruct((rows_fd, edges), BF16),
            jax.ShapeDtypeStruct((rows_fd, edges), BF16),
            jax.ShapeDtypeStruct((parts, own, groups * HALF), BF16),
        ],
        scratch_shapes=[pltpu.VMEM((freq_local, angles, 2 * GROUP), F32)]
        + [pltpu.VMEM((freq_local, points), F32)] * 3
        + [pltpu.VMEM((2, points), F32)],
        compiler_params=params(),
        cost_estimate=cost(1e6, 1e5),
        name="transport",
    )(requests, spectrum, depth_row, currents, slopes, wet_row)

    reply = pl.pallas_call(
        functools.partial(select_kernel, capacity),
        out_shape=jax.ShapeDtypeStruct((peers, capacity * TILE, rows_fd), BF16),
        compiler_params=params(),
        cost_estimate=cost(1e6, 1e5),
        name="select",
    )(asked, high)
    replies = lax.all_to_all(reply, "blk", split_axis=0, concat_axis=0, tiled=True)

    weights = pl.pallas_call(
        weights_kernel,
        out_shape=[
            jax.ShapeDtypeStruct((2 * wide, wide), BF16),
            jax.ShapeDtypeStruct((own, 2 * wide), BF16),
            jax.ShapeDtypeStruct((4 * lines, 2 * lines), BF16),
            jax.ShapeDtypeStruct((2 * lines, 2 * lines), BF16),
        ],
        compiler_params=params(),
        cost_estimate=cost(1e6, 1e5),
        name="weights",
    )(freq_weights, angle_weights)

    def exchanged(array):
        return [
            lax.ppermute(
                array, "spec", [(s, (s - step) % group_count) for s in range(group_count)]
            )
            for step in range(1, group_count)
        ]

    early_levels = [early] + exchanged(early)
    *moved_local, reply_map = pl.pallas_call(
        functools.partial(local_kernel, capacity, halves),
        out_shape=[half_wave] * halves + [jax.ShapeDtypeStruct((reply_rows, points), BF16)],
        input_output_aliases={3 + h: h for h in range(halves)},
        compiler_params=params(),
        cost_estimate=cost(1e6, 1e5),
        name="local_inflow",
    )(coded, high, low, *moved_inner)

    weight_specs = [VMEM] * 4 + [pl.BlockSpec(memory_space=pltpu.SMEM)]
    moved, turned, late_levels, gained_early = [], None, [], None
    for h in range(halves):
        out = pl.pallas_call(
            functools.partial(late_kernel if h else turned_late_kernel, h * half_groups),
            in_specs=[VMEM] * 3 + [ANY] * h,
            out_shape=[half_wave, jax.ShapeDtypeStruct((parts, own, tile), BF16)]
            + [jax.ShapeDtypeStruct((rows_fd, reply_rows), BF16)] * (h == 0),
            input_output_aliases={2: 0},
            compiler_params=params(),
            cost_estimate=cost(1e6, 1e5),
            name=f"late_inflow_{h}",
        )(*([turned, reply_map, moved_local[h], gained_early] if h else [replies, reply_map, moved_local[h]]))
        moved.append(out[0])
        turned = turned if h else out[2]
        late_levels.append([out[1]] + exchanged(out[1]))
        if h == 0:
            gained_early = pl.pallas_call(
                functools.partial(early_kernel, group_count),
                in_specs=[VMEM] * group_count + weight_specs + [ANY],
                out_shape=jax.ShapeDtypeStruct((parts * own, points), F32),
                scratch_shapes=[pltpu.VMEM((2 * wide, parts * groups * HALF), BF16)] * 2,
                compiler_params=params(),
                cost_estimate=cost(1e6, 1e5),
                name="early_transfer",
            )(*early_levels, *weights, transfer_rate, turned)

    result = []
    for h in range(halves):
        operands = [
            *late_levels[h], *weights, transfer_rate, gained_early, moved[h],
            depth_row, wind_speed, wet_row, *result,
        ]
        result = [
            pl.pallas_call(
                functools.partial(final_kernel, group_count, h * half_groups),
                in_specs=[VMEM] * group_count
                + weight_specs
                + [VMEM, VMEM, HBM, HBM, HBM]
                + [HBM] * len(result),
                out_specs=HBM,
                out_shape=jax.ShapeDtypeStruct((freq_local, angles, points), F32),
                scratch_shapes=[pltpu.VMEM((2 * wide, parts * tile), BF16)] * 2
                + [
                    pltpu.VMEM((parts, own, tile), F32),
                    pltpu.VMEM((freq_local, points), F32),
                    pltpu.VMEM((1, points), F32),
                    pltpu.VMEM((2, points), F32),
                    pltpu.VMEM((1, points), I32),
                    pltpu.VMEM((freq_local, angles, half_groups * GROUP), F32),
                    pltpu.SemaphoreType.DMA((3 + half_groups,)),
                ],
                input_output_aliases={len(operands) - 1: 0} if result else {},
                compiler_params=params(),
                cost_estimate=cost(1e6, 1e5),
                name=f"late_transfer_{h}",
            )(*operands)
        ]
    return result[0]


def solution(mesh):
    in_specs = (
        P("spec", None, "blk"),
        P("blk"),
        P(None, "blk"),
        P(None, "blk"),
        P(None, "blk"),
        P("blk"),
        P("blk", None),
        P("blk"),
        P(),
        P(),
        P(),
    )
    out_specs = P("spec", None, "blk")
    return jax.shard_map(shards, mesh=mesh, in_specs=in_specs, out_specs=out_specs, check_vma=False)
```

```python
import functools
import math

import jax
import jax.numpy as jnp
from jax import lax
from jax.experimental import pallas as pl
from jax.experimental.pallas import tpu as pltpu
from jax.sharding import PartitionSpec as P

GRAVITY = 9.81
TIME_STEP = 200.0
CELL_SIZE = 5500.0
LOWEST_FREQ = 0.0418
FREQ_GROWTH = 1.1
WIND_GROWTH = 0.0003
TURN_LIMIT = 0.9

TILE = 8
CELLS = TILE * TILE
GROUP = 256
HALF = 128
EDGE = 128
LANES = 128
VMEM_BYTES = 24 * 1024 * 1024

F32 = jnp.float32
BF16 = jnp.bfloat16
I32 = jnp.int32


def iota(shape, dim):
    return lax.broadcasted_iota(I32, shape, dim)


def onehot(mask):
    return jnp.where(mask, 1.0, 0.0).astype(BF16)


def dot(a, b):
    return jnp.dot(a, b, preferred_element_type=F32)


def dot_nt(a, b):
    return lax.dot_general(a, b, (((1,), (1,)), ((), ())), preferred_element_type=F32)


def dispersion(radian_freq, water_depth):
    deep_kh = radian_freq * radian_freq / GRAVITY * water_depth
    wave_kh = deep_kh / jnp.sqrt(jnp.tanh(deep_kh))
    return wave_kh


def radian_rows(freq_local, width):
    index = iota((freq_local, width), 0) + lax.axis_index("spec") * freq_local
    return (2.0 * math.pi * LOWEST_FREQ) * jnp.exp(index.astype(F32) * math.log(FREQ_GROWTH))


def angle_table(angles, width):
    values = iota((angles, width), 0).astype(F32) * (2.0 * math.pi / angles)
    return jnp.cos(values), jnp.sin(values)


def place_of(point):
    block = point // CELLS
    row = (point // TILE) % TILE
    col = point % TILE
    inner = (row >= 1) & (row <= 6) & (col >= 1) & (col <= 6)
    rank = (row - 1) * 6 + jnp.clip(col - 1, 0, 6)
    early = inner & (rank < 32)
    before = jnp.clip(rank, 0, 32)
    return jnp.where(early, block * 32 + rank, HALF + block * 32 + point % CELLS - before)


def edge_columns(width):
    source = iota((2 * width, EDGE), 0)
    upright = source // width
    point = source % width
    block = point // CELLS
    row = (point // TILE) % TILE
    col = point % TILE
    across = jnp.where(upright == 0, col, row)
    along = jnp.where(upright == 0, row, col)
    edge = upright * 64 + jnp.where(across == 0, 0, 32) + block * TILE + along
    on_edge = (across == 0) | (across == TILE - 1)
    return onehot(on_edge & (edge == iota((2 * width, EDGE), 1)))


def fetch(sources, targets, sems, first=0):
    copies = [
        pltpu.make_async_copy(source, target, sems.at[first + k])
        for k, (source, target) in enumerate(zip(sources, targets))
    ]
    for copy in copies:
        copy.start()
    return copies


def request_kernel(capacity, coded_ref, request_ref):
    peers = request_ref.shape[0]
    faces = coded_ref.shape[1]
    mine = lax.axis_index("blk")
    owner, block = coded_ref[...] // 256, coded_ref[...] % 256
    peer = iota((peers, faces), 0)
    asked = (owner == peer) & (peer != mine)
    earlier = onehot(iota((faces, faces), 0) < iota((faces, faces), 1))
    rank = dot(onehot(asked), earlier).astype(I32)
    side = iota((1, faces), 1) % 4
    base = (block // 4) * EDGE + (side // 2) * 64 + (1 - side % 2) * 32 + (block % 4) * TILE + 1
    base = base.astype(F32)
    lane = iota((peers, LANES), 1)
    result = jnp.zeros((peers, LANES), F32)
    for k in range(capacity):
        found = jnp.sum(jnp.where(asked & (rank == k), base, 0.0), axis=1, keepdims=True)
        result = jnp.where(lane == k, found, result)
    result = result.astype(I32)
    for p in range(peers):
        request_ref[p] = result[p : p + 1]


def select_kernel(capacity, request_ref, high_ref, reply_ref):
    peers = request_ref.shape[0]
    rows = peers * capacity * TILE
    edges = high_ref.shape[1]
    asked = jnp.concatenate([request_ref[p] for p in range(peers)], axis=0)
    coarse = (asked // 16).astype(F32).astype(BF16)
    fine = (asked % 16).astype(F32).astype(BF16)
    spread = onehot(iota((rows, peers), 0) // (capacity * TILE) == iota((rows, peers), 1))
    asked = 16.0 * dot(spread, coarse) + dot(spread, fine)
    row = iota((rows, LANES), 0)
    slot = (row // TILE) % capacity
    chosen = (slot == iota((rows, LANES), 1)) & (asked > 0.0)
    target = jnp.sum(
        jnp.where(chosen, asked + (row % TILE).astype(F32), 0.0), axis=1, keepdims=True
    )
    pick = onehot(iota((rows, edges), 1).astype(F32) + 1.0 == target)
    reply = dot_nt(pick, high_ref[...]).astype(BF16)
    for p in range(peers):
        reply_ref[p] = reply[p * capacity * TILE : (p + 1) * capacity * TILE]


def set_speeds(depth_ref, wet_ref, current_ref, group_ref, drift_ref):
    radian_freq = radian_rows(*group_ref.shape)
    depth = depth_ref[...]
    wave_kh = dispersion(radian_freq, depth)
    decay_two = jnp.exp(-2.0 * wave_kh)
    denom = 1.0 - decay_two * decay_two
    ratio = 4.0 * wave_kh * decay_two / denom
    phase = radian_freq * depth / wave_kh
    wet = wet_ref[...].astype(F32) * (TIME_STEP / CELL_SIZE)
    group_ref[...] = 0.5 * (1.0 + ratio) * phase * wet
    drift_ref[0:1, :] = current_ref[0:1, :] * wet
    drift_ref[1:2, :] = current_ref[1:2, :] * wet
    return 2.0 * radian_freq * decay_two / denom


def sides(angles):
    lane = iota((angles, LANES), 1)
    col = lane % TILE
    row = (lane // TILE) % TILE
    return col == 0, col == TILE - 1, row == 0, row == TILE - 1


def transport_kernel(after_ref, spec_ref, depth_ref, current_ref, slope_ref, wet_ref, *refs):
    moved_ref, high_ref, low_ref, early_ref, flux_ref, group_ref, turn_x_ref, turn_y_ref, drift_ref = refs
    freq_local, angles, points = moved_ref.shape
    cosine, sine = angle_table(angles, LANES)
    west, east, south, north = sides(angles)
    turn = set_speeds(depth_ref, wet_ref, current_ref, group_ref, drift_ref)
    turn = turn * (TIME_STEP / (2.0 * math.pi / angles))
    turn_x_ref[...] = turn * slope_ref[0:1, :]
    turn_y_ref[...] = turn * slope_ref[1:2, :]
    columns = edge_columns(GROUP)
    inner = onehot(place_of(iota((GROUP, HALF), 0)) == iota((GROUP, HALF), 1))

    def one_group(g, carry):
        for half in range(GROUP // LANES):
            part = pl.ds(pl.multiple_of(g * GROUP + half * LANES, LANES), LANES)
            here = slice(half * LANES, (half + 1) * LANES)
            there = slice(GROUP + half * LANES, GROUP + (half + 1) * LANES)
            drift_x = jnp.broadcast_to(drift_ref[0:1, part], (angles, LANES))
            drift_y = jnp.broadcast_to(drift_ref[1:2, part], (angles, LANES))
            for f in range(freq_local):
                energy = spec_ref[f, :, part]
                speed = jnp.broadcast_to(group_ref[f : f + 1, part], (angles, LANES))
                turn_x = jnp.broadcast_to(turn_x_ref[f : f + 1, part], (angles, LANES))
                turn_y = jnp.broadcast_to(turn_y_ref[f : f + 1, part], (angles, LANES))
                flow_x = (speed * cosine + drift_x) * energy
                flow_y = (speed * sine + drift_y) * energy
                turning = jnp.clip(sine * turn_x - cosine * turn_y, -TURN_LIMIT, TURN_LIMIT)
                flow_t = turning * energy
                right = jnp.maximum(flow_x, 0.0)
                left = right - flow_x
                up = jnp.maximum(flow_y, 0.0)
                down = up - flow_y
                ahead = jnp.maximum(flow_t, 0.0)
                back = ahead - flow_t
                total = energy - (right + left) - (up + down) - (ahead + back)
                total = total + pltpu.roll(jnp.where(east, 0.0, right), 1, 1)
                total = total + pltpu.roll(jnp.where(west, 0.0, left), LANES - 1, 1)
                total = total + pltpu.roll(jnp.where(north, 0.0, up), TILE, 1)
                total = total + pltpu.roll(jnp.where(south, 0.0, down), LANES - TILE, 1)
                total = total + pltpu.roll(ahead, 1, 0) + pltpu.roll(back, angles - 1, 0)
                moved_ref[f, :, part] = total
                flux_ref[f, :, here] = jnp.where(east, right, left)
                flux_ref[f, :, there] = jnp.where(north, up, down)
        flux = flux_ref[...].reshape(freq_local * angles, 2 * GROUP)
        high = flux.astype(BF16)
        low = (flux - high.astype(F32)).astype(BF16)
        place = pl.ds(pl.multiple_of(g * EDGE, EDGE), EDGE)
        high_ref[:, place] = dot(high, columns).astype(BF16)
        low_ref[:, place] = dot(low, columns).astype(BF16)
        part = pl.ds(pl.multiple_of(g * GROUP, GROUP), GROUP)
        for j in range(angles // 8):
            levels = moved_ref[:, 8 * j : 8 * j + 8, part].reshape(freq_local * 8, GROUP).astype(BF16)
            early_ref[j, :, place] = dot(levels, inner).astype(BF16)
        return carry

    lax.fori_loop(0, points // GROUP, one_group, 0)


def local_kernel(capacity, coded_ref, high_ref, low_ref, moved_in_ref, *refs):
    *moved_refs, map_ref = refs
    freq_local, angles, points = moved_in_ref.shape
    each = moved_refs[0].shape[2] // GROUP
    ranks = face_ranks(coded_ref)
    for g in range(points // GROUP):
        part = slice(g * GROUP, (g + 1) * GROUP)
        pick, reply_map = inflow_maps(capacity, g, ranks, high_ref.shape[1], map_ref.shape[0])
        map_ref[:, part] = reply_map
        inflow = dot(high_ref[...], pick) + dot(low_ref[...], pick)
        here = slice(g % each * GROUP, (g % each + 1) * GROUP)
        moved_refs[g // each][:, :, here] = moved_in_ref[:, :, part] + inflow.reshape(
            freq_local, angles, GROUP
        )


def face_ranks(coded_ref):
    faces = coded_ref.shape[1]
    owner, block = coded_ref[...] // 256, coded_ref[...] % 256
    by_column = jnp.broadcast_to(owner, (faces, faces))
    below = iota((faces, faces), 0)
    right = iota((faces, faces), 1)
    by_row = jnp.sum(jnp.where(below == right, by_column, 0).astype(F32), axis=1, keepdims=True)
    equal = (by_row == by_column.astype(F32)) & (below < right)
    rank = jnp.sum(jnp.where(equal, 1.0, 0.0), axis=0, keepdims=True)
    return jnp.concatenate(
        [block.astype(F32), owner.astype(F32), rank, jnp.zeros((5, faces), F32)], axis=0
    ).astype(BF16)


def inflow_maps(capacity, group, table, edges, rows):
    faces = table.shape[1]
    width = GROUP
    mine = lax.axis_index("blk")
    point = iota((faces, width), 1)
    block = point // CELLS + group * (width // CELLS)
    col = point % TILE
    row = (point // TILE) % TILE
    face = iota((faces, width), 0)
    at_x = dot(table, onehot((face == block * 4 + jnp.where(col == 0, 0, 1)))).astype(I32)
    at_y = dot(table, onehot((face == block * 4 + jnp.where(row == 0, 2, 3)))).astype(I32)
    point = iota((1, width), 1)
    col = point % TILE
    row = (point // TILE) % TILE

    def ids(found, across, along, upright):
        edge = (across == 0) | (across == TILE - 1)
        from_block, from_owner, slot = found[0:1], found[1:2], found[2:3]
        local = edge & (from_owner == mine)
        remote = edge & (from_owner != mine)
        base = upright * 64 + jnp.where(across == 0, 32, 0)
        source = (from_block // 4) * EDGE + base + (from_block % 4) * TILE + along
        reply = (from_owner * capacity + slot) * TILE + along
        return jnp.where(local, source, -1), jnp.where(remote, reply, -1)

    source_x, reply_x = ids(at_x, col, row, 0)
    source_y, reply_y = ids(at_y, row, col, 1)
    line = iota((rows, width), 0)
    reply_map = onehot((line == reply_x) | (line == reply_y))
    line = iota((edges, width), 0)
    return onehot((line == source_x) | (line == source_y)), reply_map


def weights_kernel(freq_ref, angle_ref, shift_ref, spread_ref, image_ref, back_ref):
    freqs = freq_ref.shape[1]
    angles = angle_ref.shape[2]
    wide = freqs * 8
    own = spread_ref.shape[0]
    start = lax.axis_index("spec") * (own // 8)
    rows = onehot((iota((wide, freqs), 0) // 8 + start) % freqs == iota((wide, freqs), 1))
    same = iota((wide, wide), 0) % 8 == iota((wide, wide), 1) % 8
    for s in range(2):
        weights = freq_ref[s]
        left = dot(rows, weights).astype(BF16)
        shift_ref[s * wide : (s + 1) * wide, :] = jnp.where(same, dot_nt(left, rows), 0.0).astype(BF16)
        turned = dot_nt(rows[:own], weights).astype(BF16)
        spread_ref[:, s * wide : (s + 1) * wide] = jnp.where(
            same[:own], dot_nt(turned, rows), 0.0
        ).astype(BF16)
    stacked = jnp.concatenate(
        [angle_ref[m, s].astype(F32) for m in range(2) for s in range(2)], axis=0
    ).astype(BF16)
    lines = angles * 4
    r = iota((4 * lines, 4 * angles), 0)
    c = iota((4 * lines, 4 * angles), 1)
    direction = (r // 32) % (angles // 8) * 8 + r % 8
    chosen = onehot((r // lines) * angles + direction == c)
    lines_rows = dot(chosen, stacked).astype(BF16)
    r = iota((2 * lines, angles), 0)
    column = onehot((r // 32) % (angles // 8) * 8 + r % 8 == iota((2 * lines, angles), 1))
    r = iota((4 * lines, 2 * lines), 0)
    c = iota((4 * lines, 2 * lines), 1)
    keep = ((r // lines) % 2 == c // lines) & ((r // 8) % 4 == (c // 8) % 4)
    image_ref[...] = jnp.where(keep, dot_nt(lines_rows, column), 0.0).astype(BF16)
    for s in range(2):
        r = iota((2 * lines, 4 * angles), 0)
        c = iota((2 * lines, 4 * angles), 1)
        direction = (r // 32) % (angles // 8) * 8 + r % 8
        chosen = onehot(((r // lines) * 2 + s) * angles + direction == c)
        lines_rows = dot(chosen, stacked).astype(BF16)
        r = iota((lines, 2 * lines), 0)
        c = iota((lines, 2 * lines), 1)
        keep = (r // 8) % 4 == (c // 8) % 4
        back_ref[s * lines : (s + 1) * lines, :] = jnp.where(
            keep, dot_nt(column[:lines], lines_rows), 0.0
        ).astype(BF16)


def turned_late_kernel(first, reply_ref, map_ref, moved_in_ref, *refs):
    moved_ref, late_ref, turned_ref = refs[-3:]
    freq_local, angles, points = moved_ref.shape
    reply = reply_ref[...].astype(F32).reshape(map_ref.shape[0], freq_local * angles)
    turned_ref[...] = reply.T.astype(BF16)
    late_kernel(first, turned_ref, map_ref, moved_in_ref, moved_ref, late_ref)


def late_kernel(first, turned_ref, map_ref, moved_in_ref, *refs):
    moved_ref, late_ref = refs[-2:]
    freq_local, angles, points = moved_ref.shape
    outer = onehot(place_of(iota((GROUP, HALF), 0)) == iota((GROUP, HALF), 1) + HALF)
    for k in range(points // GROUP):
        here = slice(k * GROUP, (k + 1) * GROUP)
        inflow = dot(turned_ref[...], map_ref[:, (first + k) * GROUP : (first + k + 1) * GROUP])
        moved_ref[:, :, here] = moved_in_ref[:, :, here] + inflow.reshape(freq_local, angles, GROUP)
        for j in range(angles // 8):
            levels = moved_ref[:, 8 * j : 8 * j + 8, here].reshape(freq_local * 8, GROUP)
            late_ref[j, :, k * HALF : (k + 1) * HALF] = dot(levels.astype(BF16), outer).astype(BF16)


def nonlinear_tile(level_refs, shift_ref, spread_ref, image_ref, back_ref, rate_ref, shifted_ref, gained_ref):
    parts, own, width = level_refs[0].shape
    wide = shift_ref.shape[1]
    freqs = wide // 8
    lines = parts * 32
    start = lax.axis_index("spec") * (own // 8)
    levels = jnp.concatenate(
        [jnp.concatenate([ref[j] for ref in level_refs], axis=0) for j in range(parts)], axis=1
    )
    for s in range(2):
        rows = slice(s * wide, (s + 1) * wide)
        shifted_ref[rows, :] = dot(shift_ref[rows, :], levels).astype(BF16)
    group = 2 if width <= 256 else 1

    def beside(pieces):
        return jnp.concatenate(pieces, axis=1)

    def image_of(q):
        shifted = beside(
            [
                jnp.concatenate(
                    [
                        shifted_ref[
                            s * wide + 32 * k : s * wide + 32 * k + 32, j * width : (j + 1) * width
                        ]
                        for s in range(2)
                        for j in range(parts)
                    ],
                    axis=0,
                )
                for k in range(q, q + group)
            ]
        )
        return [dot(image_ref[2 * m * lines : 2 * (m + 1) * lines, :], shifted) for m in range(2)]

    doubled = []
    coming = image_of(0)
    for q in range(0, freqs // 4, group):
        images = coming
        if q + group < freqs // 4:
            coming = image_of(q + group)
        lows = []
        for side, k in enumerate(range(q, q + group)):
            source, place = divmod(k * 32, own)
            here = slice(side * width, (side + 1) * width)
            level = jnp.concatenate(
                [level_refs[source][j, place : place + 32, :].astype(F32) for j in range(parts)], axis=0
            )
            rates = [rate_ref[(start + 4 * k + i) % freqs] for i in range(4)]
            scaled = jnp.concatenate(
                [
                    level[32 * j + 8 * i : 32 * j + 8 * i + 8] * rates[i]
                    for j in range(parts)
                    for i in range(4)
                ],
                axis=0,
            )
            deltas = []
            for m in range(2):
                plus = images[m][:lines, here]
                minus = images[m][lines:, here]
                deltas.append(scaled * (level * (plus + minus) - 2.0 * plus * minus))
            lows.append(jnp.concatenate(deltas, axis=0).astype(BF16))
            if source == 0:
                doubled.append(deltas[0] + deltas[1])
        low = beside(lows)
        for s in range(2):
            back = dot(back_ref[s * lines : (s + 1) * lines, :], low).astype(BF16)
            for side, k in enumerate(range(q, q + group)):
                for j in range(parts):
                    gained_ref[
                        s * wide + 32 * k : s * wide + 32 * k + 32, j * width : (j + 1) * width
                    ] = back[32 * j : 32 * j + 32, side * width : (side + 1) * width]
    spread = [
        dot(spread_ref[:, s * wide : (s + 1) * wide], gained_ref[s * wide : (s + 1) * wide, :])
        for s in range(2)
    ]
    result = []
    for j in range(parts):
        here = slice(j * width, (j + 1) * width)
        lost = jnp.concatenate([d[32 * j : 32 * j + 32] for d in doubled], axis=0)
        result.append(spread[0][:, here] + spread[1][:, here] - 2.0 * lost)
    return result


def put_back(values, where):
    stacked = jnp.concatenate(values, axis=0)
    high = stacked.astype(BF16)
    low = (stacked - high.astype(F32)).astype(BF16)
    return dot(jnp.concatenate([high, low], axis=1), where)


def places(first):
    position = iota((2 * HALF, GROUP), 0) % HALF + first
    return onehot(position == place_of(iota((2 * HALF, GROUP), 1)))


def early_kernel(sources, *refs):
    shift_ref, spread_ref, image_ref, back_ref, rate_ref = refs[sources : sources + 5]
    out_ref, shifted_ref, gained_ref = refs[-3:]
    result = nonlinear_tile(
        refs[:sources], shift_ref, spread_ref, image_ref, back_ref, rate_ref, shifted_ref, gained_ref
    )
    where = places(0)
    for k in range(out_ref.shape[1] // GROUP):
        values = [values[:, k * HALF : (k + 1) * HALF] for values in result]
        out_ref[:, k * GROUP : (k + 1) * GROUP] = put_back(values, where)


def final_kernel(sources, first, *refs):
    levels = refs[:sources]
    shift_ref, spread_ref, image_ref, back_ref, rate_ref = refs[sources : sources + 5]
    early_ref, moved_ref, depth_hbm, wind_hbm, wet_hbm = refs[sources + 5 : sources + 10]
    out_hbm, shifted_ref, gained_ref, late_ref, gain_ref, depth_ref, wind_ref, wet_ref, out_ref, sems = (
        refs[-10:]
    )
    small = fetch([depth_hbm, wind_hbm, wet_hbm], [depth_ref, wind_ref, wet_ref], sems)
    late = nonlinear_tile(
        levels, shift_ref, spread_ref, image_ref, back_ref, rate_ref, shifted_ref, gained_ref
    )
    for j, values in enumerate(late):
        late_ref[j] = values
    freq_local, angles, _ = moved_ref.shape
    points = depth_ref.shape[1]
    groups = late_ref.shape[2] // HALF
    own = freq_local * 8
    for copy in small:
        copy.wait()
    radian_freq = radian_rows(freq_local, points)
    wave_kh = dispersion(radian_freq, depth_ref[...])
    gain_ref[...] = wave_kh / (radian_freq * depth_ref[...])
    scale = radian_freq[:, 0:LANES] * (TIME_STEP * WIND_GROWTH)
    cosine, sine = angle_table(angles, LANES)
    where = places(HALF)

    def result_copy(k):
        part = pl.ds(pl.multiple_of((first + k) * GROUP, GROUP), GROUP)
        here = pl.ds(pl.multiple_of(k * GROUP, GROUP), GROUP)
        return pltpu.make_async_copy(
            out_ref.at[:, :, here], out_hbm.at[:, :, part], sems.at[len(small) + k]
        )

    def one_group(k, carry):
        lanes = pl.ds(pl.multiple_of(k * HALF, HALF), HALF)
        transfer = put_back([late_ref[j, :, lanes] for j in range(angles // 8)], where)
        here = pl.ds(pl.multiple_of((first + k) * GROUP, GROUP), GROUP)
        transfer = transfer + early_ref[:, here]
        for half in range(GROUP // LANES):
            part = pl.ds(pl.multiple_of((first + k) * GROUP + half * LANES, LANES), LANES)
            place = pl.ds(pl.multiple_of(k * GROUP + half * LANES, LANES), LANES)
            here = slice(half * LANES, (half + 1) * LANES)
            wet = jnp.broadcast_to(wet_ref[:, part].astype(F32), (angles, LANES))
            along = wind_ref[0:1, part] * cosine + wind_ref[1:2, part] * sine
            for f in range(freq_local):
                slow = jnp.broadcast_to(gain_ref[f : f + 1, part], (angles, LANES))
                rise = jnp.broadcast_to(scale[f : f + 1, :], (angles, LANES))
                growth = rise * jnp.maximum(along * slow - 1.0, 0.0)
                moved = moved_ref[f, :, place]
                gained = jnp.concatenate(
                    [
                        transfer[j * own + 8 * f : j * own + 8 * f + 8, here]
                        for j in range(angles // 8)
                    ],
                    axis=0,
                )
                out_ref[f, :, place] = wet * (moved + gained + growth * moved)
        result_copy(k).start()
        return carry

    lax.fori_loop(0, groups, one_group, 0)
    for k in range(groups):
        result_copy(k).wait()


HBM = pl.BlockSpec(memory_space=pltpu.HBM)
VMEM = pl.BlockSpec(memory_space=pltpu.VMEM)
ANY = pl.BlockSpec(memory_space=pl.ANY)


def params():
    return pltpu.CompilerParams(vmem_limit_bytes=VMEM_BYTES)


def cost(flops, moved):
    return pl.CostEstimate(flops=int(flops), bytes_accessed=int(moved), transcendentals=0)


def shards(
    spectrum, depths, currents, slopes, wind_speed, wet_mask,
    face_owner, face_block, freq_weights, angle_weights, transfer_rate,
):
    freq_local, angles, points = spectrum.shape
    group_count = lax.axis_size("spec")
    peers = lax.axis_size("blk")
    faces = face_block.shape[0]
    freqs = freq_local * group_count
    groups = points // GROUP
    own = freq_local * 8
    parts = angles // 8
    rows_fd = freq_local * angles
    wide = freqs * 8
    lines = 4 * angles
    edges = groups * EDGE
    capacity = max(2, (faces // 2 + peers - 2) // (peers - 1))
    reply_rows = peers * capacity * TILE
    size = freq_local * angles * points

    coded = face_owner.reshape(1, faces) * 256 + face_block.reshape(1, faces)
    depth_row = depths.reshape(1, points)
    wet_row = wet_mask.reshape(1, points)

    requests = pl.pallas_call(
        functools.partial(request_kernel, capacity),
        out_shape=jax.ShapeDtypeStruct((peers, 1, LANES), I32),
        compiler_params=params(),
        cost_estimate=cost(1e10, 4e7),
        name="requests",
    )(coded)
    asked = lax.all_to_all(requests, "blk", split_axis=0, concat_axis=0, tiled=True)

    moved_inner, high, low, early = pl.pallas_call(
        transport_kernel,
        in_specs=[ANY] + [VMEM] * 5,
        out_shape=[
            jax.ShapeDtypeStruct((freq_local, angles, points), F32),
            jax.ShapeDtypeStruct((rows_fd, edges), BF16),
            jax.ShapeDtypeStruct((rows_fd, edges), BF16),
            jax.ShapeDtypeStruct((parts, own, groups * HALF), BF16),
        ],
        scratch_shapes=[pltpu.VMEM((freq_local, angles, 2 * GROUP), F32)]
        + [pltpu.VMEM((freq_local, points), F32)] * 3
        + [pltpu.VMEM((2, points), F32)],
        compiler_params=params(),
        cost_estimate=cost(100 * size, 12 * size),
        name="transport",
    )(requests, spectrum, depth_row, currents, slopes, wet_row)

    reply = pl.pallas_call(
        functools.partial(select_kernel, capacity),
        out_shape=jax.ShapeDtypeStruct((peers, capacity * TILE, rows_fd), BF16),
        compiler_params=params(),
        cost_estimate=cost(2 * reply_rows * edges * rows_fd, 4 * rows_fd * edges),
        name="select",
    )(asked, high)
    replies = lax.all_to_all(reply, "blk", split_axis=0, concat_axis=0, tiled=True)

    weights = pl.pallas_call(
        weights_kernel,
        out_shape=[
            jax.ShapeDtypeStruct((2 * wide, wide), BF16),
            jax.ShapeDtypeStruct((own, 2 * wide), BF16),
            jax.ShapeDtypeStruct((4 * lines, 2 * lines), BF16),
            jax.ShapeDtypeStruct((2 * lines, 2 * lines), BF16),
        ],
        compiler_params=params(),
        cost_estimate=cost(1e9, 1e6),
        name="weights",
    )(freq_weights, angle_weights)

    def exchanged(array):
        return [
            lax.ppermute(
                array, "spec", [(s, (s - step) % group_count) for s in range(group_count)]
            )
            for step in range(1, group_count)
        ]

    early_levels = [early] + exchanged(early)

    halves = 2
    half_groups = groups // halves
    half_points = points // halves
    tile = half_groups * HALF
    half_wave = jax.ShapeDtypeStruct((freq_local, angles, half_points), F32)
    *moved_local, reply_map = pl.pallas_call(
        functools.partial(local_kernel, capacity),
        out_shape=[half_wave] * halves + [jax.ShapeDtypeStruct((reply_rows, points), BF16)],
        compiler_params=params(),
        cost_estimate=cost(4 * rows_fd * edges * points, 10 * size),
        name="local_inflow",
    )(coded, high, low, moved_inner)

    weight_specs = [VMEM] * 4 + [pl.BlockSpec(memory_space=pltpu.SMEM)]
    moved, turned, late_levels, gained_early = [], None, [], None
    for h in range(halves):
        out = pl.pallas_call(
            functools.partial(late_kernel if h else turned_late_kernel, h * half_groups),
            in_specs=[VMEM] * 3 + [ANY] * h,
            out_shape=[half_wave, jax.ShapeDtypeStruct((parts, own, tile), BF16)]
            + [jax.ShapeDtypeStruct((rows_fd, reply_rows), BF16)] * (h == 0),
            input_output_aliases={2: 0},
            compiler_params=params(),
            cost_estimate=cost(rows_fd * reply_rows * points, 5 * size),
            name=f"late_inflow_{h}",
        )(*([turned, reply_map, moved_local[h], gained_early] if h else [replies, reply_map, moved_local[h]]))
        moved.append(out[0])
        turned = turned if h else out[2]
        late_levels.append([out[1]] + exchanged(out[1]))
        if h == 0:
            gained_early = pl.pallas_call(
                functools.partial(early_kernel, group_count),
                in_specs=[VMEM] * group_count + weight_specs + [ANY],
                out_shape=jax.ShapeDtypeStruct((parts * own, points), F32),
                scratch_shapes=[pltpu.VMEM((2 * wide, parts * groups * HALF), BF16)] * 2,
                compiler_params=params(),
                cost_estimate=cost(3e9, 3 * size),
                name="early_transfer",
            )(*early_levels, *weights, transfer_rate, turned)

    result = []
    for h in range(halves):
        operands = [
            *late_levels[h], *weights, transfer_rate, gained_early, moved[h],
            depth_row, wind_speed, wet_row, *result,
        ]
        result = [
            pl.pallas_call(
                functools.partial(final_kernel, group_count, h * half_groups),
                in_specs=[VMEM] * group_count
                + weight_specs
                + [VMEM, VMEM, HBM, HBM, HBM]
                + [HBM] * len(result),
                out_specs=HBM,
                out_shape=jax.ShapeDtypeStruct((freq_local, angles, points), F32),
                scratch_shapes=[pltpu.VMEM((2 * wide, parts * tile), BF16)] * 2
                + [
                    pltpu.VMEM((parts, own, tile), F32),
                    pltpu.VMEM((freq_local, points), F32),
                    pltpu.VMEM((1, points), F32),
                    pltpu.VMEM((2, points), F32),
                    pltpu.VMEM((1, points), I32),
                    pltpu.VMEM((freq_local, angles, half_groups * GROUP), F32),
                    pltpu.SemaphoreType.DMA((3 + half_groups,)),
                ],
                input_output_aliases={len(operands) - 1: 0} if result else {},
                compiler_params=params(),
                cost_estimate=cost(2e9, 6 * size),
                name=f"late_transfer_{h}",
            )(*operands)
        ]
    return result[0]


def solution(mesh):
    in_specs = (
        P("spec", None, "blk"),
        P("blk"),
        P(None, "blk"),
        P(None, "blk"),
        P(None, "blk"),
        P("blk"),
        P("blk", None),
        P("blk"),
        P(),
        P(),
        P(),
    )
    out_specs = P("spec", None, "blk")
    return jax.shard_map(shards, mesh=mesh, in_specs=in_specs, out_specs=out_specs, check_vma=False)
```
